32 devices in a mesh: box: 8 (over y, x, core), samp: 4 (over z).
Axes of the slice: x: 2, y: 2, z: 4, core: 2. Of those that a mesh axis runs over, the one named last changes fastest.
Arguments:
- xvec: bfloat16 [512, 2, 4, 128], P(('box', 'samp')), may hold values from -6 to 6
- near_blocks: bfloat16 [512, 8, 2, 128, 128], P(('box', 'samp')), may hold values from -0.1875 to 0.1875
- neighbours: int32 [512, 8], P(('box', 'samp')), may hold values from 0 to 511, as said below
- lift: bfloat16 [512, 2, 128, 128], P(('box', 'samp')), may hold values from -0.5 to 0.5
- place: bfloat16 [512, 2, 128, 128], P(('box', 'samp')), may hold values from -0.25 to 0.25
- interp: bfloat16 [2048, 128], replicated, may hold values from -0.5 to 0.5
- phases: float32 [8, 2, 2048], replicated, may hold values from -1 to 1, as said below
- octant: int32 [512], P(('box', 'samp')), may hold values from 0 to 7, as said below
- leaf_parent_index: int32 [512], P(('box', 'samp')), may hold values from 0 to 63, as said below
- translators: float32 [64, 2, 2048], P(None, None, 'samp'), may hold values from -0.5 to 0.5
- inter_list: int32 [64, 14], P('box'), may hold values from 0 to 63, as said below
- trans_id: int32 [64, 14], P('box'), may hold values from 0 to 63
Outputs:
- product: float32 [512, 2, 4, 128], P(('box', 'samp'))
The draws below stay inside these ranges and needn't reach their ends.
Inputs may be any that keep to these rules, and one draw needn't show every extreme that they name: `neighbours`: row n starts with n itself; its other entries are distinct and lie within 8 boxes of n in cyclic order over all 512 leaf boxes (the texture is periodic). `leaf_parent_index`: leaf box n belongs to box group g = n // 64 and its parent is one of that group's upper-level boxes g * 8 to g * 8 + 7; every upper-level box has exactly 8 children. `octant`: the 8 children of an upper-level box have 8 distinct octants. `inter_list`: entries of row p are distinct, each equal to p + d modulo 64 with 2 <= |d| <= 8 (the periodic tree's interaction zone). `phases`: each entry has magnitude one: real part squared plus imaginary part squared is 1.
All inputs are finite; a program needn't handle non-finite values.
Results may differ from the reference program's by a relative error of at most 0.0065.
Values may be sent and summed in bfloat16 or wider, within the bound.
No kernel may reach another device: no remote copies, remote signals or barrier semaphores. Data moves between devices by JAX's collectives and lax.ppermute only.
A program may use at most 64 MiB of HBM per device.

```python
import math
import jax
import jax.numpy as jnp
from jax import lax

B_DEV = 16
U = 128
R = 4
K = 8
Q0 = 128
Q1 = 2048
NT = 64
NB = 512
HB = 8
GB = 64
NPG = 8
NP = 64
KI = 14
N_BOX = 8


def draw_neighbours(key, part):
    offsets = jnp.concatenate([jnp.arange(-HB, 0, dtype=jnp.int32), jnp.arange(1, HB + 1, dtype=jnp.int32)])
    scores = jax.random.randint(key, (NB, 2 * HB), 0, 1 << 20) * (2 * HB) + jnp.arange(2 * HB, dtype=jnp.int32)[None, :]
    order = jnp.argsort(scores, axis=1)[:, :K - 1]
    picked = offsets[order]
    picked = jnp.concatenate([jnp.zeros((NB, 1), jnp.int32), picked], axis=1)
    return jnp.mod(jnp.arange(NB, dtype=jnp.int32)[:, None] + picked, NB).astype(jnp.int32)


def tree_slots(key):
    inner = jax.random.fold_in(key, 7)
    groups = NB // GB
    scores = jax.random.randint(inner, (groups, GB), 0, 1 << 20) * GB + jnp.arange(GB, dtype=jnp.int32)[None, :]
    return jnp.argsort(scores, axis=1).astype(jnp.int32)


def draw_leaf_parent_index(key, part):
    slots = tree_slots(key)
    groups = NB // GB
    base = jnp.arange(groups, dtype=jnp.int32)[:, None] * NPG
    return (base + slots // 8).reshape(NB).astype(jnp.int32)


def draw_octant(key, part):
    slots = tree_slots(key)
    return (slots % 8).reshape(NB).astype(jnp.int32)


def draw_phases(key, part):
    angle = jax.random.uniform(key, (8, Q1), jnp.float32, -math.pi, math.pi)
    return jnp.stack([jnp.cos(angle), jnp.sin(angle)], 1).astype(jnp.float32)


def draw_inter_list(key, part):
    reach = jnp.arange(2, NPG + 1, dtype=jnp.int32)
    offsets = jnp.concatenate([-reach, reach])
    width = 2 * NPG - 2
    scores = jax.random.randint(key, (NP, width), 0, 1 << 20) * width + jnp.arange(width, dtype=jnp.int32)[None, :]
    picked = offsets[jnp.argsort(scores, axis=1)[:, :KI]]
    return jnp.mod(jnp.arange(NP, dtype=jnp.int32)[:, None] + picked, NP).astype(jnp.int32)


def place_ends(drawn, stream_key, least, high):
    longest = drawn.shape.index(max(drawn.shape))
    spots = []
    for shift in (0, 1):
        where = [jax.random.randint(jax.random.fold_in(stream_key, axis), (), 0, length) for axis, length in enumerate(drawn.shape)]
        where[longest] = (where[longest] + shift) % drawn.shape[longest]
        spots.append(tuple(where))
    return drawn.at[spots[0]].set(least).at[spots[1]].set(high)


def steps_of(rng, dims, split, smallest, high):
    gain = 1.0
    for position, blocks in split:
        heights = jax.random.uniform(jax.random.fold_in(jax.random.fold_in(rng, 6), position), (blocks,), jnp.float32, smallest / len(split), high / len(split))
        gain = gain * jnp.repeat(jnp.exp(heights), dims[position] // blocks).reshape((-1,) + (1,) * (len(dims) - 1 - position))
    return gain


def noise(own_key, extent, scale, most, pieces=(), held_as=jnp.bfloat16):
    entries = jax.random.normal(own_key, extent, jnp.float32) * scale
    if len(pieces) > 0:
        entries = steps_of(own_key, extent, pieces, -0.22, 0.18) * entries
    return jnp.clip(entries, min=-most, max=most).astype(held_as)


def setup_inputs(seed: int = 0) -> dict:
    splits = jax.random.split(jax.random.key(seed), 13)
    return {
        "xvec": noise(splits[0], (NB, 2, R, U), 1.0, 6.0, ((0, 32),)),
        "near_blocks": noise(splits[1], (NB, K, 2, U, U), (K * U) ** -0.5, 0.1875, ((0, 32),)),
        "neighbours": draw_neighbours(jax.random.fold_in(splits[12], 71), 0),
        "lift": noise(splits[3], (NB, 2, Q0, U), U ** -0.5, 0.5, ((0, 32),)),
        "place": noise(splits[4], (NB, 2, U, Q0), (4 * Q0) ** -0.5, 0.25, ((0, 32),)),
        "interp": noise(splits[5], (Q1, Q0), Q0 ** -0.5, 0.5),
        "phases": draw_phases(jax.random.fold_in(splits[12], 71), 0),
        "octant": draw_octant(jax.random.fold_in(splits[12], 71), 0),
        "leaf_parent_index": draw_leaf_parent_index(jax.random.fold_in(splits[12], 71), 0),
        "translators": noise(splits[9], (NT, 2, Q1), (8 * KI) ** -0.5, 0.5, ((2, 4),), jnp.float32),
        "inter_list": draw_inter_list(jax.random.fold_in(splits[12], 71), 0),
        "trans_id": place_ends(jax.random.randint(splits[11], (NP, KI), 0, NT), jax.random.fold_in(splits[11], 1), 0, NT - 1).astype(jnp.int32),
    }


def cmul(ar, ai, br, bi):
    return ar * br - ai * bi, ar * bi + ai * br


def reference(xvec, near_blocks, neighbours, lift, place, interp, phases, octant, leaf_parent_index, translators, inter_list, trans_id):
    f32 = jnp.float32
    bf16 = jnp.bfloat16
    spans = NB // B_DEV

    def near_span(args):
        blocks, index, lifts, xs = args
        xn = xvec[index].astype(f32)
        z = blocks.astype(f32)

        def apply(a, b):
            return jnp.einsum('bkpq,bkrq->brp', a, b)

        yr = apply(z[:, :, 0], xn[:, :, 0]) - apply(z[:, :, 1], xn[:, :, 1])
        yi = apply(z[:, :, 0], xn[:, :, 1]) + apply(z[:, :, 1], xn[:, :, 0])
        lf = lifts.astype(f32)
        xf = xs.astype(f32)

        def radiate(a, b):
            return jnp.einsum('bqu,bru->brq', a, b)

        pr = radiate(lf[:, 0], xf[:, 0]) - radiate(lf[:, 1], xf[:, 1])
        pim = radiate(lf[:, 0], xf[:, 1]) + radiate(lf[:, 1], xf[:, 0])
        return jnp.stack([yr, yi], 1), jnp.stack([pr, pim], 1).astype(bf16)

    near, pattern = lax.map(near_span, (near_blocks.reshape(spans, B_DEV, K, 2, U, U), neighbours.reshape(spans, B_DEV, K), lift.reshape(spans, B_DEV, 2, Q0, U), xvec.reshape(spans, B_DEV, 2, R, U)))
    near = near.reshape(NB, 2, R, U)
    pattern = lax.optimization_barrier(pattern.reshape(NB, 2, R, Q0))
    interpolation_filter = interp.astype(f32)

    def up_group(args):
        group, pats, octs, pars = args
        upv = jnp.einsum('sq,bcrq->bcrs', interpolation_filter, pats.astype(f32))
        ph = phases[octs]
        cr, ci = cmul(ph[:, 0][:, None, :], ph[:, 1][:, None, :], upv[:, 0], upv[:, 1])
        indicator_matrix = (pars[None, :] == group * NPG + jnp.arange(NPG, dtype=jnp.int32)[:, None]).astype(f32)
        return jnp.stack([jnp.einsum('pb,brs->prs', indicator_matrix, cr), jnp.einsum('pb,brs->prs', indicator_matrix, ci)], 1)

    parents = lax.map(up_group, (jnp.arange(N_BOX, dtype=jnp.int32), pattern.reshape(N_BOX, GB, 2, R, Q0), octant.reshape(N_BOX, GB), leaf_parent_index.reshape(N_BOX, GB)))
    parents = lax.optimization_barrier(parents.reshape(NP, 2, R, Q1).astype(bf16))

    def translate(args):
        ilist, tids = args
        src = parents[ilist].astype(f32)
        tr = translators[tids]
        ar, ai = cmul(tr[:, :, 0][:, :, None, :], tr[:, :, 1][:, :, None, :], src[:, :, 0], src[:, :, 1])
        return jnp.stack([ar.sum(1), ai.sum(1)], 1)

    incoming = lax.map(translate, (inter_list.reshape(N_BOX, NPG, KI), trans_id.reshape(N_BOX, NPG, KI)))
    incoming = lax.optimization_barrier(incoming.reshape(NP, 2, R, Q1).astype(bf16))

    def down_group(args):
        octs, pars = args
        sel = incoming[pars].astype(f32)
        ph = phases[octs]
        sr, si = cmul(ph[:, 0][:, None, :], ph[:, 1][:, None, :], sel[:, 0], sel[:, 1])
        shifted = lax.optimization_barrier(jnp.stack([sr, si], 1).astype(bf16)).astype(f32)
        return jnp.einsum('bcrs,sq->bcrq', shifted, interpolation_filter).astype(bf16)

    field = lax.map(down_group, (octant.reshape(N_BOX, GB), leaf_parent_index.reshape(N_BOX, GB)))
    field = lax.optimization_barrier(field.reshape(NB, 2, R, Q0)).astype(f32)
    pl = place.astype(f32)

    def receive(a, b):
        return jnp.einsum('buq,brq->bru', a, b)

    fr = receive(pl[:, 0], field[:, 0]) - receive(pl[:, 1], field[:, 1])
    fi = receive(pl[:, 0], field[:, 1]) + receive(pl[:, 1], field[:, 0])
    return near + jnp.stack([fr, fi], 1)
```

```python
import jax
import jax.numpy as jnp
from jax import lax
from jax.experimental import pallas as pl
from jax.experimental.pallas import tpu as pltpu
from jax.sharding import PartitionSpec as P

F32 = jnp.float32
BF16 = jnp.bfloat16
LANES = 128


def nt_dot(a, b):
    return lax.dot_general(a, b, (((1,), (1,)), ((), ())), preferred_element_type=F32)


def nn_dot(a, b):
    return lax.dot_general(a, b, (((1,), (0,)), ((), ())), preferred_element_type=F32)


def times_i(v):
    half = v.shape[0] // 2
    return jnp.concatenate([-v[half:], v[:half]], axis=0)


def widen(ref, n):
    v = jnp.concatenate([ref[n, 0].astype(F32), ref[n, 1].astype(F32)], axis=0)
    return jnp.concatenate([v, times_i(v)], axis=1)


def leaf_kernel(first_parent, octant, parent, x_ref, lift_ref, out_ref, rows, *, parents):
    step = pl.program_id(0)
    per_step = lift_ref.shape[0]
    boxes = x_ref.shape[0]
    parts = x_ref.shape[1] * x_ref.shape[2]
    for i in range(per_step):
        n = step * per_step + i
        xw = widen(x_ref, n).astype(BF16)
        mat = jnp.concatenate([lift_ref[i, 0], lift_ref[i, 1]], axis=1)
        rows[pl.ds(n, parts, stride=boxes), :] = nt_dot(xw, mat)

    @pl.when(step == pl.num_programs(0) - 1)
    def _():
        out_ref[: parts * boxes] = rows[...].astype(BF16)
        lane = lax.rem(lax.broadcasted_iota(jnp.int32, (boxes, LANES), 1), boxes)
        row = lax.broadcasted_iota(jnp.int32, (boxes, LANES), 0)
        across = jnp.zeros((boxes, LANES), F32)
        down = jnp.zeros((boxes, LANES), F32)
        for n in range(boxes):
            slot = (octant[n] * parents + parent[n] - first_parent[0]).astype(F32)
            across = jnp.where(lane == n, slot, across)
            down = jnp.where(row == n, slot, down)
        out_ref[parts * boxes : (parts + 1) * boxes] = across.astype(BF16)
        out_ref[(parts + 1) * boxes : (parts + 2) * boxes] = down.astype(BF16)


def up_kernel(*refs, pieces, boxes, parents, parts):
    msgs = refs[:pieces]
    interp_ref, phase_ref, out_ref, place_ref, raised, folded = refs[pieces:]
    leaves = pieces * boxes
    slots = 8 * parents
    samples = interp_ref.shape[0]
    per_tile = LANES // boxes
    at = parts * boxes
    tiles = []
    for t in range(0, pieces, per_tile):
        lane = lax.broadcasted_iota(jnp.int32, (boxes, LANES), 1) // boxes
        code = msgs[t][at : at + boxes].astype(F32)
        for d in range(1, min(per_tile, pieces - t)):
            code = jnp.where(lane == d, msgs[t + d][at : at + boxes].astype(F32), code)
        code = jnp.concatenate([code] * (slots // boxes), axis=0)
        want = lax.broadcasted_iota(jnp.int32, (slots, LANES), 0).astype(F32)
        width = min(per_tile, pieces - t) * boxes
        tiles.append(jnp.where(code == want, 1.0, 0.0)[:, :width])
    sorter = jnp.concatenate(tiles, axis=1).astype(BF16)
    code = jnp.concatenate([m[at + boxes : at + 2 * boxes].astype(F32) for m in msgs], axis=0)
    tiles = []
    for t in range(0, slots, LANES):
        width = min(LANES, slots - t)
        want = (lax.broadcasted_iota(jnp.int32, (leaves, LANES), 1) + t).astype(F32)
        tiles.append(jnp.where(code == want, 1.0, 0.0)[:, :width])
    place_ref[...] = jnp.concatenate(tiles, axis=1).astype(BF16)
    pats = jnp.concatenate(
        [
            jnp.concatenate([m[c * boxes : (c + 1) * boxes] for m in msgs], axis=0)
            for c in range(parts)
        ],
        axis=1,
    )
    ordered = nn_dot(sorter, pats).astype(BF16)
    for c in range(parts):
        raised[c * slots : (c + 1) * slots] = nt_dot(
            ordered[:, c * LANES : (c + 1) * LANES], interp_ref[...]
        )
    half = parts // 2
    for t in range(samples // LANES):
        lanes = slice(t * LANES, (t + 1) * LANES)
        for r in range(half):
            re = im = None
            for o in range(8):
                ph_r = phase_ref[o, 0:1, lanes]
                ph_i = phase_ref[o, 1:2, lanes]
                base_r = r * slots + o * parents
                base_i = (half + r) * slots + o * parents
                xr = raised[base_r : base_r + parents, lanes]
                xi = raised[base_i : base_i + parents, lanes]
                dr = ph_r * xr - ph_i * xi
                di = ph_r * xi + ph_i * xr
                re = dr if re is None else re + dr
                im = di if im is None else im + di
            folded[t, r * parents : (r + 1) * parents] = re
            folded[t, (half + r) * parents : (half + r + 1) * parents] = im
        for p in range(0, parents, 2):
            both = jnp.concatenate(
                [folded[t, pl.ds(p + e, parts, stride=parents), :] for e in range(2)], axis=0
            )
            out_ref[p * parts : (p + 2) * parts, lanes] = both.astype(BF16)


def down_kernel(
    first_parent, inter, trans, own, left, right, table, interp_ref, phase_ref, place_ref, *refs,
    pieces, boxes, parents, total, parts,
):
    outs = refs[:pieces]
    window, incoming, shifted = refs[pieces:]
    samples = interp_ref.shape[0]
    slots = 8 * parents
    half = parts // 2
    for i, src in enumerate((left, own, right)):
        window[i * parents : (i + 1) * parents] = (
            src[...].astype(F32).reshape(parents, parts, samples)
        )
    base = first_parent[0]

    def one(p, carry):
        acc_r = jnp.zeros((parts, samples), F32)
        acc_i = jnp.zeros((parts, samples), F32)
        for k in range(inter.shape[1]):
            j = lax.rem(inter[p, k] - base + parents + total, total)
            m = trans[p, k]
            x = window[j]
            acc_r += table[m, 0:1, :] * x
            acc_i += table[m, 1:2, :] * x
        got = (acc_r + times_i(acc_i)).astype(BF16).astype(F32)
        for t in range(samples // LANES):
            incoming[t, pl.ds(p * parts, parts), :] = got[:, t * LANES : (t + 1) * LANES]
        return carry

    lax.fori_loop(0, parents, one, 0)
    for t in range(samples // LANES):
        lanes = slice(t * LANES, (t + 1) * LANES)
        for r in range(half):
            ir = incoming[t, pl.ds(r, parents, stride=parts), :]
            ii = incoming[t, pl.ds(half + r, parents, stride=parts), :]
            re, im = [], []
            for o in range(8):
                ph_r = phase_ref[o, 0:1, lanes]
                ph_i = phase_ref[o, 1:2, lanes]
                re.append(ph_r * ir - ph_i * ii)
                im.append(ph_r * ii + ph_i * ir)
            shifted[r * slots : (r + 1) * slots, lanes] = jnp.concatenate(re, axis=0).astype(BF16)
            shifted[(half + r) * slots : (half + r + 1) * slots, lanes] = jnp.concatenate(
                im, axis=0
            ).astype(BF16)
    field = nn_dot(shifted[...], interp_ref[...]).astype(BF16)
    spread = jnp.concatenate([field[c * slots : (c + 1) * slots] for c in range(parts)], axis=1)
    leaves = nn_dot(place_ref[...], spread).astype(BF16)
    for d in range(pieces):
        for c in range(parts):
            outs[d][c * boxes : (c + 1) * boxes] = leaves[
                d * boxes : (d + 1) * boxes, c * LANES : (c + 1) * LANES
            ]


def near_kernel(first_box, neighbours, left, own, right, mats, out_ref, window, *, total):
    step = pl.program_id(0)
    per_step, near_count = mats.shape[:2]
    reach = left.shape[0]
    boxes = own.shape[0]

    @pl.when(step == 0)
    def _():
        for i in range(reach):
            window[i] = widen(left, i)
            window[reach + boxes + i] = widen(right, i)
        for i in range(boxes):
            window[reach + i] = widen(own, i)

    for i in range(per_step):
        n = step * per_step + i
        acc = None
        for k in range(near_count):
            j = lax.rem(neighbours[n, k] - first_box[0] + reach + total, total)
            mat = jnp.concatenate([mats[i, k, 0], mats[i, k, 1]], axis=1)
            y = nt_dot(window[j].astype(BF16), mat)
            acc = y if acc is None else acc + y
        out_ref[i] = acc


def final_kernel(*refs, pieces):
    parts_in = refs[:pieces]
    near_ref, mats, out_ref, field = refs[pieces:]
    boxes, halves, rhs = out_ref.shape[:3]
    parts = halves * rhs
    total = parts_in[0][...].astype(F32)
    for m in parts_in[1:]:
        total += m[...].astype(F32)
    field[...] = total.astype(BF16).astype(F32)
    for n in range(boxes):
        v = field[pl.ds(n, parts, stride=boxes), :]
        wide = jnp.concatenate([v, times_i(v)], axis=1).astype(BF16)
        y = nt_dot(wide, jnp.concatenate([mats[n, 0], mats[n, 1]], axis=1)) + near_ref[n]
        out_ref[n, 0] = y[:rhs]
        out_ref[n, 1] = y[rhs:]


def whole_in(kind):
    return pl.BlockSpec(memory_space=kind)


VM = pltpu.VMEM
SM = pltpu.SMEM
PARAMS = pltpu.CompilerParams(vmem_limit_bytes=24 * 1024 * 1024)


def on_device(
    xvec,
    near_blocks,
    neighbours,
    lift,
    place,
    interp,
    phases,
    octant,
    leaf_parent_index,
    translators,
    inter_list,
    trans_id,
):
    boxes, halves, rhs, unknowns = xvec.shape
    parts = halves * rhs
    nsamp = lax.axis_size("samp")
    nbox = lax.axis_size("box")
    box_index = lax.axis_index("box").astype(jnp.int32)
    samp_index = lax.axis_index("samp").astype(jnp.int32)
    total = boxes * nsamp * nbox
    reach = boxes // 2
    parents = boxes * nsamp // 8
    all_parents = parents * nbox
    samples = interp.shape[0] // nsamp
    slots = 8 * parents
    leaves = boxes * nsamp
    first_parent = (box_index * parents).reshape(1)
    first_box = ((box_index * nsamp + samp_index) * boxes).reshape(1)
    units = nsamp * nbox

    up_ring = [(i, (i + 1) % units) for i in range(units)]
    down_ring = [((i + 1) % units, i) for i in range(units)]
    x_left = lax.ppermute(xvec[boxes - reach :], ("box", "samp"), up_ring)
    x_right = lax.ppermute(xvec[:reach], ("box", "samp"), down_ring)

    lift_steps = 4
    message_rows = (parts + 2) * boxes
    message = pl.pallas_call(
        lambda *refs: leaf_kernel(*refs, parents=parents),
        grid_spec=pltpu.PrefetchScalarGridSpec(
            num_scalar_prefetch=3,
            grid=(lift_steps,),
            in_specs=[
                pl.BlockSpec(xvec.shape, lambda i, *_: (0, 0, 0, 0)),
                pl.BlockSpec(
                    (boxes // lift_steps,) + lift.shape[1:], lambda i, *_: (i, 0, 0, 0)
                ),
            ],
            out_specs=pl.BlockSpec((message_rows, LANES), lambda i, *_: (0, 0)),
            scratch_shapes=[VM((parts * boxes, LANES), F32)],
        ),
        out_shape=jax.ShapeDtypeStruct((message_rows, LANES), BF16),
        compiler_params=PARAMS,
        name="leaf",
    )(first_parent, octant, leaf_parent_index, xvec, lift)

    messages = [message] + [
        lax.ppermute(message, "samp", [(i, (i + d) % nsamp) for i in range(nsamp)])
        for d in range(1, nsamp)
    ]

    near_steps = boxes // 2
    near = pl.pallas_call(
        lambda *refs: near_kernel(*refs, total=total),
        grid_spec=pltpu.PrefetchScalarGridSpec(
            num_scalar_prefetch=2,
            grid=(near_steps,),
            in_specs=[
                pl.BlockSpec(x_left.shape, lambda i, *_: (0, 0, 0, 0)),
                pl.BlockSpec(xvec.shape, lambda i, *_: (0, 0, 0, 0)),
                pl.BlockSpec(x_right.shape, lambda i, *_: (0, 0, 0, 0)),
                pl.BlockSpec(
                    (boxes // near_steps,) + near_blocks.shape[1:],
                    lambda i, *_: (i, 0, 0, 0, 0),
                ),
            ],
            out_specs=pl.BlockSpec(
                (boxes // near_steps, parts, unknowns), lambda i, *_: (i, 0, 0)
            ),
            scratch_shapes=[VM((boxes + 2 * reach, parts, 2 * unknowns), F32)],
        ),
        out_shape=jax.ShapeDtypeStruct((boxes, parts, unknowns), F32),
        compiler_params=PARAMS,
        cost_estimate=pl.CostEstimate(
            flops=2 * parts * near_blocks.size,
            bytes_accessed=2 * near_blocks.size,
            transcendentals=0,
        ),
        name="near",
    )(first_box, neighbours, x_left, xvec, x_right, near_blocks)

    my_interp = lax.dynamic_slice_in_dim(interp, samp_index * samples, samples, axis=0)
    my_phases = lax.dynamic_slice_in_dim(phases, samp_index * samples, samples, axis=2)

    parent_pat, place_onehot = pl.pallas_call(
        lambda *refs: up_kernel(
            *refs, pieces=nsamp, boxes=boxes, parents=parents, parts=parts
        ),
        in_specs=[whole_in(VM)] * (nsamp + 2),
        out_specs=[whole_in(VM)] * 2,
        out_shape=[
            jax.ShapeDtypeStruct((parents * parts, samples), BF16),
            jax.ShapeDtypeStruct((leaves, slots), BF16),
        ],
        scratch_shapes=[
            VM((parts * slots, samples), F32),
            VM((samples // LANES, parts * parents, LANES), F32),
        ],
        compiler_params=PARAMS,
        name="up",
    )(*messages, my_interp, my_phases)

    from_left = lax.ppermute(parent_pat, "box", [(i, (i + 1) % nbox) for i in range(nbox)])
    from_right = lax.ppermute(parent_pat, "box", [((i + 1) % nbox, i) for i in range(nbox)])

    fields = pl.pallas_call(
        lambda *refs: down_kernel(
            *refs, pieces=nsamp, boxes=boxes, parents=parents, total=all_parents, parts=parts
        ),
        in_specs=[whole_in(SM)] * 3 + [whole_in(VM)] * 7,
        out_specs=[whole_in(VM)] * nsamp,
        out_shape=[jax.ShapeDtypeStruct((parts * boxes, LANES), BF16)] * nsamp,
        scratch_shapes=[
            VM((3 * parents, parts, samples), F32),
            VM((samples // LANES, parents * parts, LANES), F32),
            VM((parts * slots, samples), BF16),
        ],
        compiler_params=PARAMS,
        name="down",
    )(
        first_parent,
        inter_list,
        trans_id,
        parent_pat,
        from_left,
        from_right,
        translators,
        my_interp,
        my_phases,
        place_onehot,
    )

    partial = [fields[0]] + [
        lax.ppermute(fields[d], "samp", [((i + d) % nsamp, i) for i in range(nsamp)])
        for d in range(1, nsamp)
    ]

    return pl.pallas_call(
        lambda *refs: final_kernel(*refs, pieces=nsamp),
        in_specs=[whole_in(VM)] * (nsamp + 2),
        out_specs=whole_in(VM),
        out_shape=jax.ShapeDtypeStruct(xvec.shape, F32),
        scratch_shapes=[VM((parts * boxes, LANES), F32)],
        compiler_params=PARAMS,
        name="final",
    )(*partial, near, place)


def solution(mesh):
    in_specs = (
        P(("box", "samp"), None, None, None),
        P(("box", "samp"), None, None, None, None),
        P(("box", "samp"), None),
        P(("box", "samp"), None, None, None),
        P(("box", "samp"), None, None, None),
        P(),
        P(),
        P(("box", "samp")),
        P(("box", "samp")),
        P(None, None, "samp"),
        P("box", None),
        P("box", None),
    )
    out_specs = P(("box", "samp"), None, None, None)
    return jax.shard_map(
        on_device, mesh=mesh, in_specs=in_specs, out_specs=out_specs, check_vma=False
    )
```

```python
import jax
import jax.numpy as jnp
from jax import lax
from jax.experimental import pallas as pl
from jax.experimental.pallas import tpu as pltpu
from jax.sharding import PartitionSpec as P

F32 = jnp.float32
BF16 = jnp.bfloat16
LANES = 128


def nt_dot(a, b):
    return lax.dot_general(a, b, (((1,), (1,)), ((), ())), preferred_element_type=F32)


def nn_dot(a, b):
    return lax.dot_general(a, b, (((1,), (0,)), ((), ())), preferred_element_type=F32)


def times_i(v):
    half = v.shape[0] // 2
    return jnp.concatenate([-v[half:], v[:half]], axis=0)


def widen(ref, n):
    v = jnp.concatenate([ref[n, 0].astype(F32), ref[n, 1].astype(F32)], axis=0)
    return jnp.concatenate([v, times_i(v)], axis=1)


def leaf_kernel(octant, parent, x_hbm, lift_hbm, out_ref, x_ref, rows, lift, oct_s, par_s, sems, *, parents):
    boxes, halves, rhs, _ = x_ref.shape
    parts = halves * rhs
    chunks = sems.shape[0] - 3
    per = boxes // chunks
    small = [
        pltpu.make_async_copy(x_hbm, x_ref, sems.at[chunks]),
        pltpu.make_async_copy(octant, oct_s, sems.at[chunks + 1]),
        pltpu.make_async_copy(parent, par_s, sems.at[chunks + 2]),
    ]
    big = [
        pltpu.make_async_copy(
            lift_hbm.at[pl.ds(i * per, per)], lift.at[pl.ds(i * per, per)], sems.at[i]
        )
        for i in range(chunks)
    ]
    small[0].start()
    for copy in big:
        copy.start()
    small[1].start()
    small[2].start()
    small[0].wait()
    for n in range(boxes):
        if n % per == 0:
            big[n // per].wait()
        xw = widen(x_ref, n).astype(BF16)
        mat = jnp.concatenate([lift[n, 0], lift[n, 1]], axis=1)
        rows[pl.ds(n, parts, stride=boxes), :] = nt_dot(xw, mat)
    out_ref[: parts * boxes] = rows[...].astype(BF16)
    small[1].wait()
    small[2].wait()
    lane = lax.rem(lax.broadcasted_iota(jnp.int32, (boxes, LANES), 1), boxes)
    across = jnp.zeros((boxes, LANES), F32)
    for n in range(boxes):
        slot = (oct_s[n] * parents + lax.rem(par_s[n], parents)).astype(F32)
        across = jnp.where(lane == n, slot, across)
    out_ref[parts * boxes :] = across.astype(BF16)


def up_kernel(*refs, pieces, boxes, parents, parts):
    msgs = refs[:pieces]
    interp_ref, phase_ref, out_ref, place_ref, raised, folded = refs[pieces:]
    slots = 8 * parents
    samples = interp_ref.shape[0]
    per_tile = LANES // boxes
    at = parts * boxes
    tiles = []
    for t in range(0, pieces, per_tile):
        lane = lax.broadcasted_iota(jnp.int32, (boxes, LANES), 1) // boxes
        code = msgs[t][at : at + boxes].astype(F32)
        for d in range(1, min(per_tile, pieces - t)):
            code = jnp.where(lane == d, msgs[t + d][at : at + boxes].astype(F32), code)
        code = jnp.concatenate([code] * (slots // boxes), axis=0)
        want = lax.broadcasted_iota(jnp.int32, (slots, LANES), 0).astype(F32)
        width = min(per_tile, pieces - t) * boxes
        tiles.append(jnp.where(code == want, 1.0, 0.0)[:, :width])
    sorter = jnp.concatenate(tiles, axis=1)
    place_ref[...] = sorter.T.astype(BF16)
    sorter = sorter.astype(BF16)
    pats = jnp.concatenate(
        [
            jnp.concatenate([m[c * boxes : (c + 1) * boxes] for m in msgs], axis=0)
            for c in range(parts)
        ],
        axis=1,
    )
    ordered = nn_dot(sorter, pats).astype(BF16)
    for c in range(parts):
        raised[c * slots : (c + 1) * slots] = nt_dot(
            ordered[:, c * LANES : (c + 1) * LANES], interp_ref[...]
        )
    half = parts // 2
    for t in range(samples // LANES):
        lanes = slice(t * LANES, (t + 1) * LANES)
        for r in range(half):
            re = im = None
            for o in range(8):
                ph_r = phase_ref[o, 0:1, lanes]
                ph_i = phase_ref[o, 1:2, lanes]
                base_r = r * slots + o * parents
                base_i = (half + r) * slots + o * parents
                xr = raised[base_r : base_r + parents, lanes]
                xi = raised[base_i : base_i + parents, lanes]
                dr = ph_r * xr - ph_i * xi
                di = ph_r * xi + ph_i * xr
                re = dr if re is None else re + dr
                im = di if im is None else im + di
            folded[t, r * parents : (r + 1) * parents] = re
            folded[t, (half + r) * parents : (half + r + 1) * parents] = im
        for p in range(0, parents, 2):
            both = jnp.concatenate(
                [folded[t, pl.ds(p + e, parts, stride=parents), :] for e in range(2)], axis=0
            )
            out_ref[p * parts : (p + 2) * parts, lanes] = both.astype(BF16)


def down_kernel(
    parity, own, across, beside, dense, interp_ref, phase_ref, place_ref, *refs, pieces, boxes, parents, parts
):
    outs = refs[:pieces]
    window, incoming, shifted = refs[pieces:]
    samples = interp_ref.shape[0]
    slots = 8 * parents
    half = parts // 2
    odd = parity[0]
    window[parents : 2 * parents] = own[...].astype(F32).reshape(parents, parts, samples)
    window[pl.ds(2 * parents * odd, parents)] = (
        across[...].astype(F32).reshape(parents, parts, samples)
    )
    window[pl.ds(2 * parents * (1 - odd), parents)] = (
        beside[...].astype(F32).reshape(parents, parts, samples)
    )
    offsets = zone(parents)

    def one(p):
        for t in range(samples // LANES):
            lanes = slice(t * LANES, (t + 1) * LANES)
            acc_r = acc_i = None
            for i, d in enumerate(offsets):
                x = window[parents + p + d, :, lanes]
                yr = dense[p, i, 0:1, lanes] * x
                yi = dense[p, i, 1:2, lanes] * x
                acc_r = yr if acc_r is None else acc_r + yr
                acc_i = yi if acc_i is None else acc_i + yi
            got = (acc_r + times_i(acc_i)).astype(BF16).astype(F32)
            incoming[t, pl.ds(p * parts, parts), :] = got

    if parents <= 8:
        for p in range(parents):
            one(p)
    else:
        lax.fori_loop(0, parents, lambda p, c: (one(p), c)[1], 0)
    for t in range(samples // LANES):
        lanes = slice(t * LANES, (t + 1) * LANES)
        for r in range(half):
            ir = incoming[t, pl.ds(r, parents, stride=parts), :]
            ii = incoming[t, pl.ds(half + r, parents, stride=parts), :]
            re, im = [], []
            for o in range(8):
                ph_r = phase_ref[o, 0:1, lanes]
                ph_i = phase_ref[o, 1:2, lanes]
                re.append(ph_r * ir - ph_i * ii)
                im.append(ph_r * ii + ph_i * ir)
            shifted[r * slots : (r + 1) * slots, lanes] = jnp.concatenate(re, axis=0).astype(BF16)
            shifted[(half + r) * slots : (half + r + 1) * slots, lanes] = jnp.concatenate(
                im, axis=0
            ).astype(BF16)
    field = nn_dot(shifted[...], interp_ref[...]).astype(BF16)
    spread = jnp.concatenate([field[c * slots : (c + 1) * slots] for c in range(parts)], axis=1)
    leaves = nn_dot(place_ref[...], spread).astype(BF16)
    for d in range(pieces):
        for c in range(parts):
            outs[d][c * boxes : (c + 1) * boxes] = leaves[
                d * boxes : (d + 1) * boxes, c * LANES : (c + 1) * LANES
            ]


def zone(parents):
    return [d for d in range(-parents, parents + 1) if abs(d) >= 2]


def near_kernel(
    where, neighbours, own, beside, across, mats_hbm, after, *refs, first, count, total, table_args
):
    step_in = refs[:3] if table_args else ()
    refs = refs[len(step_in) :]
    out_ref = refs[0]
    dense = refs[1] if table_args else None
    refs = refs[1 + bool(table_args) :]
    window, mats, nbr, sems = refs[:4]
    boxes = own.shape[0]
    reach = boxes // 2
    near_count = mats.shape[1]
    first_box, odd = where[0], where[1]
    list_copy = pltpu.make_async_copy(neighbours, nbr, sems.at[count])
    list_copy.start()
    copies = [
        pltpu.make_async_copy(mats_hbm.at[first + i], mats.at[i], sems.at[i]) for i in range(count)
    ]
    if table_args:
        parents, all_parents = table_args
        inter, trans, table_hbm = step_in
        inter_s, trans_s, table, more = refs[4:]
        extra = [
            pltpu.make_async_copy(inter, inter_s, more.at[0]),
            pltpu.make_async_copy(trans, trans_s, more.at[1]),
            pltpu.make_async_copy(table_hbm, table, more.at[2]),
        ]
        for copy in extra:
            copy.start()
    for copy in copies:
        copy.start()
    for i in range(boxes):
        window[reach + i] = widen(own, i)
    for i in range(reach):
        window[(reach + boxes) * (1 - odd) + i] = widen(beside, reach * odd + i)
        window[(reach + boxes) * odd + i] = widen(across, reach * (1 - odd) + i)
    if table_args:
        for copy in extra:
            copy.wait()
        if len(zone(parents)) > inter.shape[1]:
            dense[...] = jnp.zeros_like(dense)

        def fill(p, carry):
            for k in range(inter.shape[1]):
                rel = lax.rem(inter_s[p, k] - where[2] - p + parents + all_parents, all_parents)
                at = jnp.where(rel < parents, rel, rel - 3)
                dense[p, at] = table[trans_s[p, k]]
            return carry

        lax.fori_loop(0, parents, fill, 0)
    list_copy.wait()
    for i in range(count):
        copies[i].wait()
        xs, zs = [], []
        for k in range(near_count):
            j = lax.rem(nbr[k, first + i] - first_box + reach + total, total)
            xs.append(window[j])
            zs += [mats[i, k, 0], mats[i, k, 1]]
        out_ref[i] = nt_dot(
            jnp.concatenate(xs, axis=1).astype(BF16), jnp.concatenate(zs, axis=1)
        )


def final_kernel(*refs, pieces):
    parts_in = refs[:pieces]
    near_refs = refs[pieces : pieces + 2]
    mats, out_ref, field = refs[pieces + 2 :]
    nears = [(ref, i) for ref in near_refs for i in range(ref.shape[0])]
    boxes, halves, rhs = out_ref.shape[:3]
    parts = halves * rhs
    total = parts_in[0][...].astype(F32)
    for m in parts_in[1:]:
        total += m[...].astype(F32)
    field[...] = total.astype(BF16).astype(F32)
    for n in range(boxes):
        v = field[pl.ds(n, parts, stride=boxes), :]
        wide = jnp.concatenate([v, times_i(v)], axis=1).astype(BF16)
        y = nt_dot(wide, jnp.concatenate([mats[n, 0], mats[n, 1]], axis=1))
        ref, i = nears[n]
        y = y + ref[i]
        out_ref[n, 0] = y[:rhs]
        out_ref[n, 1] = y[rhs:]


def whole_in(kind):
    return pl.BlockSpec(memory_space=kind)


VM = pltpu.VMEM
SM = pltpu.SMEM
HBM = pltpu.HBM
DMA = pltpu.SemaphoreType.DMA
PARAMS = pltpu.CompilerParams(vmem_limit_bytes=24 * 1024 * 1024)


def swap(x, axis, pairs):
    return lax.ppermute(x, axis, pairs)


def on_device(
    xvec,
    near_blocks,
    neighbours,
    lift,
    place,
    interp,
    phases,
    octant,
    leaf_parent_index,
    translators,
    inter_list,
    trans_id,
):
    boxes, halves, rhs, unknowns = xvec.shape
    parts = halves * rhs
    nsamp = lax.axis_size("samp")
    nbox = lax.axis_size("box")
    box_index = lax.axis_index("box").astype(jnp.int32)
    samp_index = lax.axis_index("samp").astype(jnp.int32)
    total = boxes * nsamp * nbox
    reach = boxes // 2
    parents = boxes * nsamp // 8
    all_parents = parents * nbox
    samples = interp.shape[0] // nsamp
    slots = 8 * parents
    leaves = boxes * nsamp
    units = nsamp * nbox
    near_count = near_blocks.shape[1]
    where = jnp.stack(
        [(box_index * nsamp + samp_index) * boxes, samp_index % 2, box_index * parents]
    )
    parity = (box_index % 2).reshape(1)

    lift_chunks = 4
    message, x_here = pl.pallas_call(
        lambda *refs: leaf_kernel(*refs, parents=parents),
        in_specs=[whole_in(HBM)] * 4,
        out_specs=[whole_in(VM)] * 2,
        out_shape=[
            jax.ShapeDtypeStruct(((parts + 1) * boxes, LANES), BF16),
            jax.ShapeDtypeStruct(xvec.shape, BF16),
        ],
        scratch_shapes=[
            VM((parts * boxes, LANES), F32),
            VM(lift.shape, BF16),
            SM((boxes,), jnp.int32),
            SM((boxes,), jnp.int32),
            DMA((lift_chunks + 3,)),
        ],
        compiler_params=PARAMS,
        name="leaf",
    )(octant, leaf_parent_index, xvec, lift)

    messages = [message] + [None] * (nsamp - 1)
    for d in reversed(range(1, nsamp)):
        messages[d] = swap(message, "samp", [(i, i ^ d) for i in range(nsamp)])

    both = ("box", "samp")
    x_beside = swap(x_here, both, [(i, i ^ 1) for i in range(units)])
    x_across = swap(
        x_here, both, [(i, (i + (1 if i % 2 else -1)) % units) for i in range(units)]
    )

    my_interp = lax.dynamic_slice_in_dim(interp, samp_index * samples, samples, axis=0)
    my_phases = lax.dynamic_slice_in_dim(phases, samp_index * samples, samples, axis=2)

    parent_pat, place_onehot = pl.pallas_call(
        lambda *refs: up_kernel(
            *refs, pieces=nsamp, boxes=boxes, parents=parents, parts=parts
        ),
        in_specs=[whole_in(VM)] * (nsamp + 2),
        out_specs=[whole_in(VM)] * 2,
        out_shape=[
            jax.ShapeDtypeStruct((parents * parts, samples), BF16),
            jax.ShapeDtypeStruct((leaves, slots), BF16),
        ],
        scratch_shapes=[
            VM((parts * slots, samples), F32),
            VM((samples // LANES, parts * parents, LANES), F32),
        ],
        compiler_params=PARAMS,
        name="up",
    )(*messages, my_interp, my_phases)

    across = swap(
        parent_pat, "box", [(i, (i + (1 if i % 2 else -1)) % nbox) for i in range(nbox)]
    )
    beside = swap(parent_pat, "box", [(i, i ^ 1) for i in range(nbox)])

    def near_part(first, count, after, table):
        zone_size = len(zone(parents))
        out_shape = [jax.ShapeDtypeStruct((count, parts, unknowns), F32)]
        scratch = [
            VM((boxes + 2 * reach, parts, 2 * unknowns), F32),
            VM((count,) + near_blocks.shape[1:], BF16),
            SM((near_count, boxes), jnp.int32),
            DMA((count + 1,)),
        ]
        if table:
            out_shape.append(jax.ShapeDtypeStruct((parents, zone_size, 2, samples), F32))
            scratch += [
                SM(inter_list.shape, jnp.int32),
                SM(trans_id.shape, jnp.int32),
                VM(translators.shape, F32),
                DMA((3,)),
            ]
        return pl.pallas_call(
            lambda *refs: near_kernel(
                *refs,
                first=first,
                count=count,
                total=total,
                table_args=(parents, all_parents) if table else None,
            ),
            in_specs=[whole_in(SM), whole_in(HBM)]
            + [whole_in(VM)] * 3
            + [whole_in(HBM), whole_in(VM)]
            + [whole_in(HBM)] * len(table),
            out_specs=[whole_in(VM)] * len(out_shape),
            out_shape=out_shape,
            scratch_shapes=scratch,
            compiler_params=PARAMS,
            cost_estimate=pl.CostEstimate(
                flops=2 * parts * near_blocks.size * count // boxes,
                bytes_accessed=2 * near_blocks.size * count // boxes,
                transcendentals=0,
            ),
            name="near",
        )(where, neighbours.T, x_here, x_beside, x_across, near_blocks, after, *table)

    split = boxes // 2
    near_a, dense = near_part(0, split, place_onehot, (inter_list, trans_id, translators))

    fields = pl.pallas_call(
        lambda *refs: down_kernel(
            *refs, pieces=nsamp, boxes=boxes, parents=parents, parts=parts
        ),
        in_specs=[whole_in(SM)] + [whole_in(VM)] * 7,
        out_specs=[whole_in(VM)] * nsamp,
        out_shape=[jax.ShapeDtypeStruct((parts * boxes, LANES), BF16)] * nsamp,
        scratch_shapes=[
            VM((3 * parents, parts, samples), F32),
            VM((samples // LANES, parents * parts, LANES), F32),
            VM((parts * slots, samples), BF16),
        ],
        compiler_params=PARAMS,
        name="down",
    )(parity, parent_pat, across, beside, dense, my_interp, my_phases, place_onehot)

    partial = [fields[0]] + [None] * (nsamp - 1)
    for d in reversed(range(1, nsamp)):
        partial[d] = swap(fields[d], "samp", [(i, i ^ d) for i in range(nsamp)])

    (near_b,) = near_part(split, boxes - split, fields[0], ())

    return pl.pallas_call(
        lambda *refs: final_kernel(*refs, pieces=nsamp),
        in_specs=[whole_in(VM)] * (nsamp + 3),
        out_specs=whole_in(VM),
        out_shape=jax.ShapeDtypeStruct(xvec.shape, F32),
        scratch_shapes=[VM((parts * boxes, LANES), F32)],
        compiler_params=PARAMS,
        name="final",
    )(*partial, near_a, near_b, place)


def solution(mesh):
    in_specs = (
        P(("box", "samp"), None, None, None),
        P(("box", "samp"), None, None, None, None),
        P(("box", "samp"), None),
        P(("box", "samp"), None, None, None),
        P(("box", "samp"), None, None, None),
        P(),
        P(),
        P(("box", "samp")),
        P(("box", "samp")),
        P(None, None, "samp"),
        P("box", None),
        P("box", None),
    )
    out_specs = P(("box", "samp"), None, None, None)
    return jax.shard_map(
        on_device, mesh=mesh, in_specs=in_specs, out_specs=out_specs, check_vma=False
    )
```

```python
import jax
import jax.numpy as jnp
from jax import lax
from jax.experimental import pallas as pl
from jax.experimental.pallas import tpu as pltpu
from jax.sharding import PartitionSpec as P

F32 = jnp.float32
BF16 = jnp.bfloat16
LANES = 128


def nt_dot(a, b):
    return lax.dot_general(a, b, (((1,), (1,)), ((), ())), preferred_element_type=F32)


def nn_dot(a, b):
    return lax.dot_general(a, b, (((1,), (0,)), ((), ())), preferred_element_type=F32)


def times_i(v):
    half = v.shape[0] // 2
    return jnp.concatenate([-v[half:], v[:half]], axis=0)


def widen(ref, n):
    v = jnp.concatenate([ref[n, 0].astype(F32), ref[n, 1].astype(F32)], axis=0)
    return jnp.concatenate([v, times_i(v)], axis=1)


def leaf_kernel(
    octant, parent, x_hbm, lift_hbm, interp_hbm, phase_hbm,
    out_ref, x_ref, interp_ref, phase_ref,
    rows, lift, oct_s, par_s, sems, *, parents, copies_out,
):
    boxes, halves, rhs, _ = x_ref.shape
    parts = halves * rhs
    chunks = sems.shape[0] - 5
    samples = interp_ref.shape[0]
    mine = pl.ds(pl.multiple_of(lax.axis_index("samp") * samples, samples), samples)
    per = boxes // chunks
    small = [
        pltpu.make_async_copy(x_hbm, x_ref, sems.at[chunks]),
        pltpu.make_async_copy(octant, oct_s, sems.at[chunks + 1]),
        pltpu.make_async_copy(parent, par_s, sems.at[chunks + 2]),
        pltpu.make_async_copy(interp_hbm.at[mine], interp_ref, sems.at[chunks + 3]),
        pltpu.make_async_copy(phase_hbm.at[:, :, mine], phase_ref, sems.at[chunks + 4]),
    ]
    big = [
        pltpu.make_async_copy(
            lift_hbm.at[pl.ds(i * per, per)], lift.at[pl.ds(i * per, per)], sems.at[i]
        )
        for i in range(chunks)
    ]
    small[0].start()
    for copy in big:
        copy.start()
    for copy in small[1:]:
        copy.start()
    small[0].wait()
    for n in range(boxes):
        if n % per == 0:
            big[n // per].wait()
        xw = widen(x_ref, n).astype(BF16)
        mat = jnp.concatenate([lift[n, 0], lift[n, 1]], axis=1)
        rows[pl.ds(n, parts, stride=boxes), :] = nt_dot(xw, mat)
    pattern = rows[...].astype(BF16)
    for copy in small[1:]:
        copy.wait()
    lane = lax.rem(lax.broadcasted_iota(jnp.int32, (boxes, LANES), 1), boxes)
    across = jnp.zeros((boxes, LANES), F32)
    for n in range(boxes):
        slot = (oct_s[n] * parents + lax.rem(par_s[n], parents)).astype(F32)
        across = jnp.where(lane == n, slot, across)
    codes = across.astype(BF16)
    for i in range(copies_out):
        at = i * (parts + 1) * boxes
        out_ref[at : at + parts * boxes] = pattern
        out_ref[at + parts * boxes : at + (parts + 1) * boxes] = codes


def up_kernel(*refs, pieces, boxes, parents, parts):
    every, interp_ref, phase_ref, out_ref, place_ref, raised, folded = refs
    rows_each = (parts + 1) * boxes
    msgs = [every.at[d * rows_each : (d + 1) * rows_each] for d in range(pieces)]
    slots = 8 * parents
    samples = interp_ref.shape[0]
    per_tile = LANES // boxes
    at = parts * boxes
    tiles = []
    for t in range(0, pieces, per_tile):
        lane = lax.broadcasted_iota(jnp.int32, (boxes, LANES), 1) // boxes
        code = msgs[t][at : at + boxes].astype(F32)
        for d in range(1, min(per_tile, pieces - t)):
            code = jnp.where(lane == d, msgs[t + d][at : at + boxes].astype(F32), code)
        code = jnp.concatenate([code] * (slots // boxes), axis=0)
        want = lax.broadcasted_iota(jnp.int32, (slots, LANES), 0).astype(F32)
        width = min(per_tile, pieces - t) * boxes
        tiles.append(jnp.where(code == want, 1.0, 0.0)[:, :width])
    sorter = jnp.concatenate(tiles, axis=1)
    place_ref[...] = sorter.T.astype(BF16)
    sorter = sorter.astype(BF16)
    pats = jnp.concatenate(
        [
            jnp.concatenate([m[c * boxes : (c + 1) * boxes] for m in msgs], axis=0)
            for c in range(parts)
        ],
        axis=1,
    )
    ordered = nn_dot(sorter, pats).astype(BF16)
    for c in range(parts):
        raised[c * slots : (c + 1) * slots] = nt_dot(
            ordered[:, c * LANES : (c + 1) * LANES], interp_ref[...]
        )
    half = parts // 2
    for t in range(samples // LANES):
        lanes = slice(t * LANES, (t + 1) * LANES)
        for r in range(half):
            re = im = None
            for o in range(8):
                ph_r = phase_ref[o, 0:1, lanes]
                ph_i = phase_ref[o, 1:2, lanes]
                base_r = r * slots + o * parents
                base_i = (half + r) * slots + o * parents
                xr = raised[base_r : base_r + parents, lanes]
                xi = raised[base_i : base_i + parents, lanes]
                dr = ph_r * xr - ph_i * xi
                di = ph_r * xi + ph_i * xr
                re = dr if re is None else re + dr
                im = di if im is None else im + di
            folded[t, r * parents : (r + 1) * parents] = re
            folded[t, (half + r) * parents : (half + r + 1) * parents] = im
        for p in range(0, parents, 2):
            both = jnp.concatenate(
                [folded[t, pl.ds(p + e, parts, stride=parents), :] for e in range(2)], axis=0
            )
            out_ref[p * parts : (p + 2) * parts, lanes] = both.astype(BF16)


def down_kernel(
    own, across, beside, dense, interp_ref, phase_ref, place_ref, out_ref,
    window, incoming, shifted, *, pieces, boxes, parents, parts
):
    samples = interp_ref.shape[0]
    slots = 8 * parents
    half = parts // 2
    odd = lax.rem(lax.axis_index("box"), 2)
    window[parents : 2 * parents] = own[...].astype(F32).reshape(parents, parts, samples)
    window[pl.ds(2 * parents * odd, parents)] = (
        across[...].astype(F32).reshape(parents, parts, samples)
    )
    window[pl.ds(2 * parents * (1 - odd), parents)] = (
        beside[...].astype(F32).reshape(parents, parts, samples)
    )
    offsets = zone(parents)

    def one(p):
        for t in range(samples // LANES):
            lanes = slice(t * LANES, (t + 1) * LANES)
            acc_r = acc_i = None
            for i, d in enumerate(offsets):
                x = window[parents + p + d, :, lanes]
                yr = dense[p, i, 0:1, lanes] * x
                yi = dense[p, i, 1:2, lanes] * x
                acc_r = yr if acc_r is None else acc_r + yr
                acc_i = yi if acc_i is None else acc_i + yi
            got = (acc_r + times_i(acc_i)).astype(BF16).astype(F32)
            incoming[t, pl.ds(p * parts, parts), :] = got

    if parents <= 8:
        for p in range(parents):
            one(p)
    else:
        lax.fori_loop(0, parents, lambda p, c: (one(p), c)[1], 0)
    for t in range(samples // LANES):
        lanes = slice(t * LANES, (t + 1) * LANES)
        for r in range(half):
            ir = incoming[t, pl.ds(r, parents, stride=parts), :]
            ii = incoming[t, pl.ds(half + r, parents, stride=parts), :]
            re, im = [], []
            for o in range(8):
                ph_r = phase_ref[o, 0:1, lanes]
                ph_i = phase_ref[o, 1:2, lanes]
                re.append(ph_r * ir - ph_i * ii)
                im.append(ph_r * ii + ph_i * ir)
            shifted[r * slots : (r + 1) * slots, lanes] = jnp.concatenate(re, axis=0).astype(BF16)
            shifted[(half + r) * slots : (half + r + 1) * slots, lanes] = jnp.concatenate(
                im, axis=0
            ).astype(BF16)
    field = nn_dot(shifted[...], interp_ref[...]).astype(BF16)
    spread = jnp.concatenate([field[c * slots : (c + 1) * slots] for c in range(parts)], axis=1)
    leaves = nn_dot(place_ref[...], spread).astype(BF16)
    for d in range(pieces):
        for c in range(parts):
            at = (d * parts + c) * boxes
            out_ref[at : at + boxes] = leaves[
                d * boxes : (d + 1) * boxes, c * LANES : (c + 1) * LANES
            ]


def zone(parents):
    return [d for d in range(-parents, parents + 1) if abs(d) >= 2]


def near_kernel(
    neighbours, own, beside, across, mats_hbm, after, *refs, first, count, total, table_args
):
    step_in = refs[:3] if table_args else ()
    refs = refs[len(step_in) :]
    out_ref = refs[0]
    dense = refs[1] if table_args else None
    refs = refs[1 + bool(table_args) :]
    window, mats, nbr, sems = refs[:4]
    boxes = own.shape[0]
    reach = boxes // 2
    near_count = mats.shape[1]
    samp = lax.axis_index("samp")
    box = lax.axis_index("box")
    first_box = (box * lax.axis_size("samp") + samp) * boxes
    odd = lax.rem(samp, 2)
    list_copy = pltpu.make_async_copy(neighbours, nbr, sems.at[count])
    list_copy.start()
    copies = [
        pltpu.make_async_copy(mats_hbm.at[first + i], mats.at[i], sems.at[i]) for i in range(count)
    ]
    if table_args:
        parents, all_parents = table_args
        inter, trans, table_hbm = step_in
        inter_s, trans_s, table, more = refs[4:]
        extra = [
            pltpu.make_async_copy(inter, inter_s, more.at[0]),
            pltpu.make_async_copy(trans, trans_s, more.at[1]),
            pltpu.make_async_copy(table_hbm, table, more.at[2]),
        ]
        for copy in extra:
            copy.start()
    for copy in copies:
        copy.start()
    for i in range(boxes):
        window[reach + i] = widen(own, i)
    for i in range(reach):
        window[(reach + boxes) * (1 - odd) + i] = widen(beside, reach * odd + i)
        window[(reach + boxes) * odd + i] = widen(across, reach * (1 - odd) + i)
    if table_args:
        for copy in extra:
            copy.wait()
        if len(zone(parents)) > inter.shape[1]:
            dense[...] = jnp.zeros_like(dense)

        def fill(p, carry):
            for k in range(inter.shape[1]):
                rel = lax.rem(inter_s[p, k] - box * parents - p + parents + all_parents, all_parents)
                at = jnp.where(rel < parents, rel, rel - 3)
                dense[p, at] = table[trans_s[p, k]]
            return carry

        lax.fori_loop(0, parents, fill, 0)
    list_copy.wait()
    for i in range(count):
        copies[i].wait()
        xs, zs = [], []
        for k in range(near_count):
            j = lax.rem(nbr[k, first + i] - first_box + reach + total, total)
            xs.append(window[j])
            zs += [mats[i, k, 0], mats[i, k, 1]]
        out_ref[i] = nt_dot(
            jnp.concatenate(xs, axis=1).astype(BF16), jnp.concatenate(zs, axis=1)
        )


def final_kernel(*refs, pieces):
    every, *near_refs, mats, out_ref, field = refs
    nears = [(ref, i) for ref in near_refs for i in range(ref.shape[0])]
    boxes, halves, rhs = out_ref.shape[:3]
    parts = halves * rhs
    rows_each = field.shape[0]
    total = every[:rows_each].astype(F32)
    for d in range(1, pieces):
        total += every[d * rows_each : (d + 1) * rows_each].astype(F32)
    field[...] = total.astype(BF16).astype(F32)
    for n in range(boxes):
        v = field[pl.ds(n, parts, stride=boxes), :]
        wide = jnp.concatenate([v, times_i(v)], axis=1).astype(BF16)
        y = nt_dot(wide, jnp.concatenate([mats[n, 0], mats[n, 1]], axis=1))
        ref, i = nears[n]
        y = y + ref[i]
        out_ref[n, 0] = y[:rhs]
        out_ref[n, 1] = y[rhs:]


def whole_in(kind):
    return pl.BlockSpec(memory_space=kind)


VM = pltpu.VMEM
SM = pltpu.SMEM
HBM = pltpu.HBM
DMA = pltpu.SemaphoreType.DMA
PARAMS = pltpu.CompilerParams(vmem_limit_bytes=24 * 1024 * 1024)


def swap(x, axis, pairs):
    return lax.ppermute(x, axis, pairs)


def stay(x):
    return pltpu.with_memory_space_constraint(x, HBM)


def on_device(
    xvec,
    near_blocks,
    neighbours,
    lift,
    place,
    interp,
    phases,
    octant,
    leaf_parent_index,
    translators,
    inter_list,
    trans_id,
):
    boxes, halves, rhs, unknowns = xvec.shape
    parts = halves * rhs
    nsamp = lax.axis_size("samp")
    nbox = lax.axis_size("box")
    total = boxes * nsamp * nbox
    reach = boxes // 2
    parents = boxes * nsamp // 8
    all_parents = parents * nbox
    samples = interp.shape[0] // nsamp
    slots = 8 * parents
    leaves = boxes * nsamp
    units = nsamp * nbox
    near_count = near_blocks.shape[1]
    lift_chunks = 4
    message, x_here, my_interp, my_phases = pl.pallas_call(
        lambda *refs: leaf_kernel(*refs, parents=parents, copies_out=nsamp),
        in_specs=[whole_in(HBM)] * 6,
        out_specs=[whole_in(VM)] * 4,
        out_shape=[
            jax.ShapeDtypeStruct((nsamp * (parts + 1) * boxes, LANES), BF16),
            jax.ShapeDtypeStruct(xvec.shape, BF16),
            jax.ShapeDtypeStruct((samples, LANES), BF16),
            jax.ShapeDtypeStruct((8, 2, samples), F32),
        ],
        scratch_shapes=[
            VM((parts * boxes, LANES), F32),
            VM(lift.shape, BF16),
            SM((boxes,), jnp.int32),
            SM((boxes,), jnp.int32),
            DMA((lift_chunks + 5,)),
        ],
        compiler_params=PARAMS,
        name="leaf",
    )(*[stay(a) for a in (octant, leaf_parent_index, xvec, lift, interp, phases)])

    messages = lax.all_to_all(message, "samp", 0, 0, tiled=True)

    both = ("box", "samp")
    x_beside = swap(x_here, both, [(i, i ^ 1) for i in range(units)])
    x_across = swap(
        x_here, both, [(i, (i + (1 if i % 2 else -1)) % units) for i in range(units)]
    )

    parent_pat, place_onehot = pl.pallas_call(
        lambda *refs: up_kernel(
            *refs, pieces=nsamp, boxes=boxes, parents=parents, parts=parts
        ),
        in_specs=[whole_in(VM)] * 3,
        out_specs=[whole_in(VM)] * 2,
        out_shape=[
            jax.ShapeDtypeStruct((parents * parts, samples), BF16),
            jax.ShapeDtypeStruct((leaves, slots), BF16),
        ],
        scratch_shapes=[
            VM((parts * slots, samples), F32),
            VM((samples // LANES, parts * parents, LANES), F32),
        ],
        compiler_params=PARAMS,
        name="up",
    )(messages, my_interp, my_phases)

    across = swap(
        parent_pat, "box", [(i, (i + (1 if i % 2 else -1)) % nbox) for i in range(nbox)]
    )
    beside = swap(parent_pat, "box", [(i, i ^ 1) for i in range(nbox)])

    def near_part(first, count, after, table):
        zone_size = len(zone(parents))
        out_shape = [jax.ShapeDtypeStruct((count, parts, unknowns), F32)]
        scratch = [
            VM((boxes + 2 * reach, parts, 2 * unknowns), F32),
            VM((count,) + near_blocks.shape[1:], BF16),
            SM((near_count, boxes), jnp.int32),
            DMA((count + 1,)),
        ]
        if table:
            out_shape.append(jax.ShapeDtypeStruct((parents, zone_size, 2, samples), F32))
            scratch += [
                SM(inter_list.shape, jnp.int32),
                SM(trans_id.shape, jnp.int32),
                VM(translators.shape, F32),
                DMA((3,)),
            ]
        return pl.pallas_call(
            lambda *refs: near_kernel(
                *refs,
                first=first,
                count=count,
                total=total,
                table_args=(parents, all_parents) if table else None,
            ),
            in_specs=[whole_in(HBM)]
            + [whole_in(VM)] * 3
            + [whole_in(HBM), whole_in(VM)]
            + [whole_in(HBM)] * len(table),
            out_specs=[whole_in(VM)] * len(out_shape),
            out_shape=out_shape,
            scratch_shapes=scratch,
            compiler_params=PARAMS,
            cost_estimate=pl.CostEstimate(
                flops=2 * parts * near_blocks.size * count // boxes,
                bytes_accessed=2 * near_blocks.size * count // boxes,
                transcendentals=0,
            ),
            name="near",
        )(
            stay(neighbours.T),
            x_here,
            x_beside,
            x_across,
            stay(near_blocks),
            after,
            *[stay(a) for a in table],
        )

    split = boxes // 2
    near_a, dense = near_part(0, split, place_onehot, (inter_list, trans_id, translators))

    fields = pl.pallas_call(
        lambda *refs: down_kernel(
            *refs, pieces=nsamp, boxes=boxes, parents=parents, parts=parts
        ),
        in_specs=[whole_in(VM)] * 7,
        out_specs=whole_in(VM),
        out_shape=jax.ShapeDtypeStruct((nsamp * parts * boxes, LANES), BF16),
        scratch_shapes=[
            VM((3 * parents, parts, samples), F32),
            VM((samples // LANES, parents * parts, LANES), F32),
            VM((parts * slots, samples), BF16),
        ],
        compiler_params=PARAMS,
        name="down",
    )(parent_pat, across, beside, dense, my_interp, my_phases, place_onehot)

    partial = lax.all_to_all(fields, "samp", 0, 0, tiled=True)

    (near_b,) = near_part(split, boxes - split, fields, ())

    return pl.pallas_call(
        lambda *refs: final_kernel(*refs, pieces=nsamp),
        in_specs=[whole_in(VM)] * 4,
        out_specs=whole_in(VM),
        out_shape=jax.ShapeDtypeStruct(xvec.shape, F32),
        scratch_shapes=[VM((parts * boxes, LANES), F32)],
        compiler_params=PARAMS,
        name="final",
    )(partial, near_a, near_b, place)


def solution(mesh):
    in_specs = (
        P(("box", "samp"), None, None, None),
        P(("box", "samp"), None, None, None, None),
        P(("box", "samp"), None),
        P(("box", "samp"), None, None, None),
        P(("box", "samp"), None, None, None),
        P(),
        P(),
        P(("box", "samp")),
        P(("box", "samp")),
        P(None, None, "samp"),
        P("box", None),
        P("box", None),
    )
    out_specs = P(("box", "samp"), None, None, None)
    return jax.shard_map(
        on_device, mesh=mesh, in_specs=in_specs, out_specs=out_specs, check_vma=False
    )
```

```python
import jax
import jax.numpy as jnp
from jax import lax
from jax.experimental import pallas as pl
from jax.experimental.pallas import tpu as pltpu
from jax.sharding import PartitionSpec as P

F32 = jnp.float32
BF16 = jnp.bfloat16
LANES = 128


def nt_dot(a, b):
    return lax.dot_general(a, b, (((1,), (1,)), ((), ())), preferred_element_type=F32)


def nn_dot(a, b):
    return lax.dot_general(a, b, (((1,), (0,)), ((), ())), preferred_element_type=F32)


def times_i(v):
    half = v.shape[0] // 2
    return jnp.concatenate([-v[half:], v[:half]], axis=0)


def widen(v):
    return jnp.concatenate([v, times_i(v)], axis=1)


def leaf_kernel(
    octant, parent, x_hbm, lift_hbm, plain, to_beside, to_far, x_rows,
    x_ref, rows, lift, oct_s, par_s, sems, *, parents,
):
    boxes, halves, rhs, _ = x_ref.shape
    parts = halves * rhs
    reach = boxes // 2
    chunks = sems.shape[0] - 3
    per = boxes // chunks
    small = [
        pltpu.make_async_copy(x_hbm, x_ref, sems.at[chunks]),
        pltpu.make_async_copy(octant, oct_s, sems.at[chunks + 1]),
        pltpu.make_async_copy(parent, par_s, sems.at[chunks + 2]),
    ]
    big = [
        pltpu.make_async_copy(
            lift_hbm.at[pl.ds(i * per, per)], lift.at[pl.ds(i * per, per)], sems.at[i]
        )
        for i in range(chunks)
    ]
    small[0].start()
    for copy in big:
        copy.start()
    small[1].start()
    small[2].start()
    small[0].wait()
    own = [
        jnp.concatenate([x_ref[n, 0].astype(F32), x_ref[n, 1].astype(F32)], axis=0)
        for n in range(boxes)
    ]
    for n in range(boxes):
        if n % per == 0:
            big[n // per].wait()
        mat = jnp.concatenate([lift[n, 0], lift[n, 1]], axis=1)
        rows[pl.ds(n, parts, stride=boxes), :] = nt_dot(widen(own[n]).astype(BF16), mat)
    small[1].wait()
    small[2].wait()
    lane = lax.rem(lax.broadcasted_iota(jnp.int32, (boxes, LANES), 1), boxes)
    across = jnp.zeros((boxes, LANES), F32)
    for n in range(boxes):
        slot = (oct_s[n] * parents + lax.rem(par_s[n], parents)).astype(F32)
        across = jnp.where(lane == n, slot, across)
    pattern = rows[...].astype(BF16)
    codes = across.astype(BF16)
    at = parts * boxes
    for ref in (plain, to_beside, to_far):
        ref[:at] = pattern
        ref[at : at + boxes] = codes
    at += boxes
    x_rows[...] = jnp.concatenate(own, axis=0).astype(BF16)
    first = jnp.concatenate(own[:reach], axis=0)
    last = jnp.concatenate(own[reach:], axis=0)
    odd = lax.rem(lax.axis_index("samp"), 2) == 1
    to_beside[at:] = jnp.where(odd, first, last).astype(BF16)
    to_far[at:] = jnp.where(odd, last, first).astype(BF16)


def up_kernel(*refs, pieces, boxes, parents, parts):
    msgs = refs[:pieces]
    interp_ref, phase_ref, out_ref, place_ref, raised, folded = refs[pieces:]
    forward = msgs[-1]
    slots = 8 * parents
    samples = interp_ref.shape[0]
    per_tile = LANES // boxes
    at = parts * boxes
    tiles = []
    for t in range(0, pieces, per_tile):
        lane = lax.broadcasted_iota(jnp.int32, (boxes, LANES), 1) // boxes
        code = msgs[t][at : at + boxes].astype(F32)
        for d in range(1, min(per_tile, pieces - t)):
            code = jnp.where(lane == d, msgs[t + d][at : at + boxes].astype(F32), code)
        code = jnp.concatenate([code] * (slots // boxes), axis=0)
        want = lax.broadcasted_iota(jnp.int32, (slots, LANES), 0).astype(F32)
        width = min(per_tile, pieces - t) * boxes
        tiles.append(jnp.where(code == want, 1.0, 0.0)[:, :width])
    sorter = jnp.concatenate(tiles, axis=1)
    place_ref[...] = sorter.T.astype(BF16)
    sorter = sorter.astype(BF16)
    pats = jnp.concatenate(
        [
            jnp.concatenate([m[c * boxes : (c + 1) * boxes] for m in msgs], axis=0)
            for c in range(parts)
        ],
        axis=1,
    )
    ordered = nn_dot(sorter, pats).astype(BF16)
    for c in range(parts):
        raised[c * slots : (c + 1) * slots] = nt_dot(
            ordered[:, c * LANES : (c + 1) * LANES], interp_ref[...]
        )
    half = parts // 2
    for t in range(samples // LANES):
        lanes = slice(t * LANES, (t + 1) * LANES)
        for r in range(half):
            re = im = None
            for o in range(8):
                ph_r = phase_ref[o, 0:1, lanes]
                ph_i = phase_ref[o, 1:2, lanes]
                base_r = r * slots + o * parents
                base_i = (half + r) * slots + o * parents
                xr = raised[base_r : base_r + parents, lanes]
                xi = raised[base_i : base_i + parents, lanes]
                dr = ph_r * xr - ph_i * xi
                di = ph_r * xi + ph_i * xr
                re = dr if re is None else re + dr
                im = di if im is None else im + di
            folded[t, r * parents : (r + 1) * parents] = re
            folded[t, (half + r) * parents : (half + r + 1) * parents] = im
        for p in range(0, parents, 2):
            both = jnp.concatenate(
                [folded[t, pl.ds(p + e, parts, stride=parents), :] for e in range(2)], axis=0
            )
            out_ref[p * parts : (p + 2) * parts, lanes] = both.astype(BF16)
        extra = out_ref.shape[0] - parents * parts
        start = forward.shape[0] - extra * (samples // LANES - t)
        out_ref[parents * parts :, lanes] = forward[start : start + extra]


def zone(parents):
    return [d for d in range(-parents, parents + 1) if abs(d) >= 2]


def prep_kernel(
    inter, trans, table_hbm, interp_hbm, phase_hbm, after, dense, interp_ref, phase_ref,
    inter_s, trans_s, table, sems, *, parents, all_parents,
):
    samples = interp_ref.shape[0]
    mine = pl.ds(pl.multiple_of(lax.axis_index("samp") * samples, samples), samples)
    copies = [
        pltpu.make_async_copy(inter, inter_s, sems.at[0]),
        pltpu.make_async_copy(trans, trans_s, sems.at[1]),
        pltpu.make_async_copy(table_hbm, table, sems.at[2]),
        pltpu.make_async_copy(interp_hbm.at[mine], interp_ref, sems.at[3]),
        pltpu.make_async_copy(phase_hbm.at[:, :, mine], phase_ref, sems.at[4]),
    ]
    for copy in copies:
        copy.start()
    for copy in copies:
        copy.wait()
    if len(zone(parents)) > inter.shape[1]:
        dense[...] = jnp.zeros_like(dense)
    first = lax.axis_index("box") * parents

    def fill(p, carry):
        for k in range(inter.shape[1]):
            rel = lax.rem(inter_s[p, k] - first - p + parents + all_parents, all_parents)
            at = jnp.where(rel < parents, rel, rel - 3)
            dense[p, at] = table[trans_s[p, k]]
        return carry

    lax.fori_loop(0, parents, fill, 0)


def down_kernel(
    own, across, beside, dense, interp_ref, phase_ref, place_ref, *refs, pieces, boxes, parents, parts
):
    outs = refs[:pieces]
    window, incoming, shifted = refs[pieces:]
    samples = interp_ref.shape[0]
    slots = 8 * parents
    half = parts // 2
    odd = lax.rem(lax.axis_index("box"), 2)
    rows = parents * parts
    window[parents : 2 * parents] = own[:rows].astype(F32).reshape(parents, parts, samples)
    window[pl.ds(2 * parents * odd, parents)] = (
        across[:rows].astype(F32).reshape(parents, parts, samples)
    )
    window[pl.ds(2 * parents * (1 - odd), parents)] = (
        beside[:rows].astype(F32).reshape(parents, parts, samples)
    )
    offsets = zone(parents)

    def one(p):
        for t in range(samples // LANES):
            lanes = slice(t * LANES, (t + 1) * LANES)
            acc_r = acc_i = None
            for i, d in enumerate(offsets):
                x = window[parents + p + d, :, lanes]
                yr = dense[p, i, 0:1, lanes] * x
                yi = dense[p, i, 1:2, lanes] * x
                acc_r = yr if acc_r is None else acc_r + yr
                acc_i = yi if acc_i is None else acc_i + yi
            got = (acc_r + times_i(acc_i)).astype(BF16).astype(F32)
            incoming[t, pl.ds(p * parts, parts), :] = got

    if parents <= 8:
        for p in range(parents):
            one(p)
    else:
        lax.fori_loop(0, parents, lambda p, c: (one(p), c)[1], 0)
    for t in range(samples // LANES):
        lanes = slice(t * LANES, (t + 1) * LANES)
        for r in range(half):
            ir = incoming[t, pl.ds(r, parents, stride=parts), :]
            ii = incoming[t, pl.ds(half + r, parents, stride=parts), :]
            re, im = [], []
            for o in range(8):
                ph_r = phase_ref[o, 0:1, lanes]
                ph_i = phase_ref[o, 1:2, lanes]
                re.append(ph_r * ir - ph_i * ii)
                im.append(ph_r * ii + ph_i * ir)
            shifted[r * slots : (r + 1) * slots, lanes] = jnp.concatenate(re, axis=0).astype(BF16)
            shifted[(half + r) * slots : (half + r + 1) * slots, lanes] = jnp.concatenate(
                im, axis=0
            ).astype(BF16)
    field = nn_dot(shifted[...], interp_ref[...]).astype(BF16)
    spread = jnp.concatenate([field[c * slots : (c + 1) * slots] for c in range(parts)], axis=1)
    leaves = nn_dot(place_ref[...], spread).astype(BF16)
    for d in range(pieces):
        for c in range(parts):
            outs[d][c * boxes : (c + 1) * boxes] = leaves[
                d * boxes : (d + 1) * boxes, c * LANES : (c + 1) * LANES
            ]


def near_kernel(
    neighbours, own, mats_hbm, after, *refs, late, nsamp, total, halo_rows, parent_rows
):
    far = nsamp.bit_length() - 2
    from_beside, from_far, refs = refs[0], refs[1 : 1 + far], refs[1 + far :]
    if late:
        across, beside, refs = refs[0], refs[1], refs[2:]
    out_ref, window, mats, nbr, sems = refs
    count, parts, unknowns = out_ref.shape
    boxes = own.shape[0] // parts
    near_count = mats.shape[1]
    samp = lax.axis_index("samp")
    box = lax.axis_index("box")
    odd = lax.rem(samp, 2) == 1
    final = samp == nsamp - 1
    upper = jnp.logical_not(final) if not late else final
    first = jnp.where(upper, boxes - count, 0)
    list_copy = pltpu.make_async_copy(neighbours, nbr, sems.at[count])
    list_copy.start()
    copies = [
        pltpu.make_async_copy(mats_hbm.at[first + i], mats.at[i], sems.at[i]) for i in range(count)
    ]
    for copy in copies:
        copy.start()

    def piece(ref):
        return ref[ref.shape[0] - halo_rows :].astype(F32)

    distant = piece(from_far[0])
    step = samp ^ (samp - 1) if late else samp ^ (samp + 1)
    for i in range(1, far):
        distant = jnp.where(step == (4 << i) - 1, piece(from_far[i]), distant)
    near_by = piece(from_beside)
    if late:
        def forwarded(ref):
            return jnp.concatenate(
                [
                    ref[parent_rows:, t * LANES : (t + 1) * LANES].astype(F32)
                    for t in range(ref.shape[1] // LANES)
                ],
                axis=0,
            )

        box_odd = lax.rem(box, 2) == 1
        from_left = samp == 0
        passed = jnp.where(box_odd == from_left, forwarded(beside), forwarded(across))
        halo = jnp.where(odd, near_by, distant)
        halo = jnp.where(jnp.logical_or(from_left, final), passed, halo)
    else:
        halo = jnp.where(jnp.logical_and(odd, jnp.logical_not(final)), distant, near_by)
    at = jnp.where(upper, boxes + count, 0)
    for i in range(count):
        window[at + i] = widen(halo[i * parts : (i + 1) * parts])
    mine = own[...].astype(F32)
    for i in range(boxes):
        window[count + i] = widen(mine[i * parts : (i + 1) * parts])
    list_copy.wait()
    base = (box * nsamp + samp) * boxes
    for i in range(count):
        copies[i].wait()
        acc = None
        for k in range(near_count):
            j = lax.rem(nbr[k, first + i] - base + count + total, total)
            mat = jnp.concatenate([mats[i, k, 0], mats[i, k, 1]], axis=1)
            y = nt_dot(window[j].astype(BF16), mat)
            acc = y if acc is None else acc + y
        out_ref[i] = acc


def final_kernel(*refs, pieces):
    parts_in = refs[:pieces]
    near_early, near_late, mats, out_ref, field = refs[pieces:]
    boxes, halves, rhs = out_ref.shape[:3]
    parts = halves * rhs
    half = boxes // 2
    flip = lax.axis_index("samp") == lax.axis_size("samp") - 1
    total = parts_in[0][...].astype(F32)
    for m in parts_in[1:]:
        total += m[...].astype(F32)
    field[...] = total.astype(BF16).astype(F32)
    for n in range(boxes):
        v = field[pl.ds(n, parts, stride=boxes), :]
        wide = jnp.concatenate([v, times_i(v)], axis=1).astype(BF16)
        y = nt_dot(wide, jnp.concatenate([mats[n, 0], mats[n, 1]], axis=1))
        i = n % half
        y = y + jnp.where(flip == (n < half), near_early[i], near_late[i])
        out_ref[n, 0] = y[:rhs]
        out_ref[n, 1] = y[rhs:]


def whole_in(kind):
    return pl.BlockSpec(memory_space=kind)


VM = pltpu.VMEM
SM = pltpu.SMEM
HBM = pltpu.HBM
DMA = pltpu.SemaphoreType.DMA
PARAMS = pltpu.CompilerParams(vmem_limit_bytes=24 * 1024 * 1024)


def stay(x):
    return pltpu.with_memory_space_constraint(x, HBM)


def on_device(
    xvec,
    near_blocks,
    neighbours,
    lift,
    place,
    interp,
    phases,
    octant,
    leaf_parent_index,
    translators,
    inter_list,
    trans_id,
):
    boxes, halves, rhs, unknowns = xvec.shape
    parts = halves * rhs
    nsamp = lax.axis_size("samp")
    nbox = lax.axis_size("box")
    total = boxes * nsamp * nbox
    reach = boxes // 2
    parents = boxes * nsamp // 8
    all_parents = parents * nbox
    samples = interp.shape[0] // nsamp
    slots = 8 * parents
    leaves = boxes * nsamp
    near_count = near_blocks.shape[1]
    halo_rows = reach * parts
    parent_rows = parents * parts
    plain_rows = (parts + 1) * boxes

    def shape(dims, dtype=BF16):
        return jax.ShapeDtypeStruct(dims, dtype)

    lift_chunks = 4
    plain, to_beside, to_far, x_rows = pl.pallas_call(
        lambda *refs: leaf_kernel(*refs, parents=parents),
        in_specs=[whole_in(HBM)] * 4,
        out_specs=[whole_in(VM)] * 4,
        out_shape=[
            shape((plain_rows, LANES)),
            shape((plain_rows + halo_rows, LANES)),
            shape((plain_rows + halo_rows, LANES)),
            shape((boxes * parts, LANES)),
        ],
        scratch_shapes=[
            VM(xvec.shape, BF16),
            VM((parts * boxes, LANES), F32),
            VM(lift.shape, BF16),
            SM((boxes,), jnp.int32),
            SM((boxes,), jnp.int32),
            DMA((lift_chunks + 3,)),
        ],
        compiler_params=PARAMS,
        name="leaf",
    )(*[stay(a) for a in (octant, leaf_parent_index, xvec, lift)])

    def exchange(x, d):
        return lax.ppermute(x, "samp", [(i, i ^ d) for i in range(nsamp)])

    messages = [plain] + [None] * (nsamp - 1)
    far = [(4 << i) - 1 for i in range(nsamp.bit_length() - 2)]
    for d in reversed(range(1, nsamp)):
        messages[d] = exchange(to_beside if d == 1 else to_far if d in far else plain, d)
    far_messages = [messages[d] for d in far]

    dense, my_interp, my_phases = pl.pallas_call(
        lambda *refs: prep_kernel(*refs, parents=parents, all_parents=all_parents),
        in_specs=[whole_in(HBM)] * 5 + [whole_in(VM)],
        out_specs=[whole_in(VM)] * 3,
        out_shape=[
            shape((parents, len(zone(parents)), 2, samples), F32),
            shape((samples, LANES)),
            shape((8, 2, samples), F32),
        ],
        scratch_shapes=[
            SM(inter_list.shape, jnp.int32),
            SM(trans_id.shape, jnp.int32),
            VM(translators.shape, F32),
            DMA((5,)),
        ],
        compiler_params=PARAMS,
        cost_estimate=pl.CostEstimate(
            flops=0, bytes_accessed=4 * 1024 * 1024, transcendentals=0
        ),
        name="prep",
    )(*[stay(a) for a in (inter_list, trans_id, translators, interp, phases)], x_rows)

    parent_pat, place_onehot = pl.pallas_call(
        lambda *refs: up_kernel(
            *refs, pieces=nsamp, boxes=boxes, parents=parents, parts=parts
        ),
        in_specs=[whole_in(VM)] * (nsamp + 2),
        out_specs=[whole_in(VM)] * 2,
        out_shape=[
            shape((parent_rows + halo_rows * LANES // samples, samples)),
            shape((leaves, slots)),
        ],
        scratch_shapes=[
            VM((parts * slots, samples), F32),
            VM((samples // LANES, parent_rows, LANES), F32),
        ],
        compiler_params=PARAMS,
        name="up",
    )(*messages, my_interp, my_phases)

    across = lax.ppermute(
        parent_pat, "box", [(i, (i + (1 if i % 2 else -1)) % nbox) for i in range(nbox)]
    )
    beside = lax.ppermute(parent_pat, "box", [(i, i ^ 1) for i in range(nbox)])

    def near_half(late, after, sources):
        return pl.pallas_call(
            lambda *refs: near_kernel(
                *refs,
                late=late,
                nsamp=nsamp,
                total=total,
                halo_rows=halo_rows,
                parent_rows=parent_rows,
            ),
            in_specs=[whole_in(HBM), whole_in(VM), whole_in(HBM), whole_in(VM)]
            + [whole_in(VM)] * len(sources),
            out_specs=whole_in(VM),
            out_shape=shape((reach, parts, unknowns), F32),
            scratch_shapes=[
                VM((boxes + 2 * reach, parts, 2 * unknowns), F32),
                VM((reach,) + near_blocks.shape[1:], BF16),
                SM((near_count, boxes), jnp.int32),
                DMA((reach + 1,)),
            ],
            compiler_params=PARAMS,
            cost_estimate=pl.CostEstimate(
                flops=parts * near_blocks.size,
                bytes_accessed=near_blocks.size,
                transcendentals=0,
            ),
            name="near",
        )(stay(neighbours.T), x_rows, stay(near_blocks), after, *sources)

    near_early = near_half(False, place_onehot, [messages[1], *far_messages])

    fields = pl.pallas_call(
        lambda *refs: down_kernel(
            *refs, pieces=nsamp, boxes=boxes, parents=parents, parts=parts
        ),
        in_specs=[whole_in(VM)] * 7,
        out_specs=[whole_in(VM)] * nsamp,
        out_shape=[shape((parts * boxes, LANES))] * nsamp,
        scratch_shapes=[
            VM((3 * parents, parts, samples), F32),
            VM((samples // LANES, parent_rows, LANES), F32),
            VM((parts * slots, samples), BF16),
        ],
        compiler_params=PARAMS,
        name="down",
    )(parent_pat, across, beside, dense, my_interp, my_phases, place_onehot)

    partial = [fields[0]] + [None] * (nsamp - 1)
    for d in reversed(range(1, nsamp)):
        partial[d] = exchange(fields[d], d)

    near_late = near_half(
        True, fields[0], [messages[1], *far_messages, across, beside]
    )

    return pl.pallas_call(
        lambda *refs: final_kernel(*refs, pieces=nsamp),
        in_specs=[whole_in(VM)] * (nsamp + 3),
        out_specs=whole_in(VM),
        out_shape=shape(xvec.shape, F32),
        scratch_shapes=[VM((parts * boxes, LANES), F32)],
        compiler_params=PARAMS,
        name="final",
    )(*partial, near_early, near_late, place)


def solution(mesh):
    in_specs = (
        P(("box", "samp"), None, None, None),
        P(("box", "samp"), None, None, None, None),
        P(("box", "samp"), None),
        P(("box", "samp"), None, None, None),
        P(("box", "samp"), None, None, None),
        P(),
        P(),
        P(("box", "samp")),
        P(("box", "samp")),
        P(None, None, "samp"),
        P("box", None),
        P("box", None),
    )
    out_specs = P(("box", "samp"), None, None, None)
    return jax.shard_map(
        on_device, mesh=mesh, in_specs=in_specs, out_specs=out_specs, check_vma=False
    )
```

```python
import jax
import jax.numpy as jnp
from jax import lax
from jax.experimental import pallas as pl
from jax.experimental.pallas import tpu as pltpu
from jax.sharding import PartitionSpec as P

F32 = jnp.float32
BF16 = jnp.bfloat16
LANES = 128


def nt_dot(a, b):
    return lax.dot_general(a, b, (((1,), (1,)), ((), ())), preferred_element_type=F32)


def nn_dot(a, b):
    return lax.dot_general(a, b, (((1,), (0,)), ((), ())), preferred_element_type=F32)


def times_i(v):
    half = v.shape[0] // 2
    return jnp.concatenate([-v[half:], v[:half]], axis=0)


def widen(v):
    return jnp.concatenate([v, times_i(v)], axis=1)


def leaf_kernel(
    octant, parent, x_hbm, lift_hbm, plain, to_beside, to_far, x_rows,
    x_ref, rows, lift, oct_s, par_s, sems, *, parents,
):
    boxes, halves, rhs, _ = x_ref.shape
    parts = halves * rhs
    reach = boxes // 2
    chunks = sems.shape[0] - 3
    per = boxes // chunks
    small = [
        pltpu.make_async_copy(x_hbm, x_ref, sems.at[chunks]),
        pltpu.make_async_copy(octant, oct_s, sems.at[chunks + 1]),
        pltpu.make_async_copy(parent, par_s, sems.at[chunks + 2]),
    ]
    big = [
        pltpu.make_async_copy(
            lift_hbm.at[pl.ds(i * per, per)], lift.at[pl.ds(i * per, per)], sems.at[i]
        )
        for i in range(chunks)
    ]
    small[0].start()
    for copy in big:
        copy.start()
    small[1].start()
    small[2].start()
    small[0].wait()
    own = [
        jnp.concatenate([x_ref[n, 0].astype(F32), x_ref[n, 1].astype(F32)], axis=0)
        for n in range(boxes)
    ]
    for n in range(boxes):
        if n % per == 0:
            big[n // per].wait()
        mat = jnp.concatenate([lift[n, 0], lift[n, 1]], axis=1)
        rows[pl.ds(n, parts, stride=boxes), :] = nt_dot(widen(own[n]).astype(BF16), mat)
    small[1].wait()
    small[2].wait()
    lane = lax.rem(lax.broadcasted_iota(jnp.int32, (boxes, LANES), 1), boxes)
    across = jnp.zeros((boxes, LANES), F32)
    for n in range(boxes):
        slot = (oct_s[n] * parents + lax.rem(par_s[n], parents)).astype(F32)
        across = jnp.where(lane == n, slot, across)
    pattern = rows[...].astype(BF16)
    codes = across.astype(BF16)
    at = parts * boxes
    for ref in (plain, to_beside, to_far):
        ref[:at] = pattern
        ref[at : at + boxes] = codes
    at += boxes
    x_rows[...] = jnp.concatenate(own, axis=0).astype(BF16)
    first = jnp.concatenate(own[:reach], axis=0)
    last = jnp.concatenate(own[reach:], axis=0)
    odd = lax.rem(lax.axis_index("samp"), 2) == 1
    to_beside[at:] = jnp.where(odd, first, last).astype(BF16)
    to_far[at:] = jnp.where(odd, last, first).astype(BF16)


def up_kernel(*refs, pieces, boxes, parents, parts):
    msgs = refs[:pieces]
    interp_ref, phase_ref, out_ref, place_ref, raised, folded = refs[pieces:]
    forward = msgs[-1]
    slots = 8 * parents
    samples = interp_ref.shape[0]
    per_tile = LANES // boxes
    at = parts * boxes
    tiles = []
    for t in range(0, pieces, per_tile):
        lane = lax.broadcasted_iota(jnp.int32, (boxes, LANES), 1) // boxes
        code = msgs[t][at : at + boxes].astype(F32)
        for d in range(1, min(per_tile, pieces - t)):
            code = jnp.where(lane == d, msgs[t + d][at : at + boxes].astype(F32), code)
        code = jnp.concatenate([code] * (slots // boxes), axis=0)
        want = lax.broadcasted_iota(jnp.int32, (slots, LANES), 0).astype(F32)
        width = min(per_tile, pieces - t) * boxes
        tiles.append(jnp.where(code == want, 1.0, 0.0)[:, :width])
    sorter = jnp.concatenate(tiles, axis=1)
    place_ref[...] = sorter.T.astype(BF16)
    sorter = sorter.astype(BF16)
    pats = jnp.concatenate(
        [
            jnp.concatenate([m[c * boxes : (c + 1) * boxes] for m in msgs], axis=0)
            for c in range(parts)
        ],
        axis=1,
    )
    ordered = nn_dot(sorter, pats).astype(BF16)
    for c in range(parts):
        raised[c * slots : (c + 1) * slots] = nt_dot(
            ordered[:, c * LANES : (c + 1) * LANES], interp_ref[...]
        )
    half = parts // 2
    for t in range(samples // LANES):
        lanes = slice(t * LANES, (t + 1) * LANES)
        for r in range(half):
            re = im = None
            for o in range(8):
                ph_r = phase_ref[o, 0:1, lanes]
                ph_i = phase_ref[o, 1:2, lanes]
                base_r = r * slots + o * parents
                base_i = (half + r) * slots + o * parents
                xr = raised[base_r : base_r + parents, lanes]
                xi = raised[base_i : base_i + parents, lanes]
                dr = ph_r * xr - ph_i * xi
                di = ph_r * xi + ph_i * xr
                re = dr if re is None else re + dr
                im = di if im is None else im + di
            folded[t, r * parents : (r + 1) * parents] = re
            folded[t, (half + r) * parents : (half + r + 1) * parents] = im
        for p in range(0, parents, 2):
            both = jnp.concatenate(
                [folded[t, pl.ds(p + e, parts, stride=parents), :] for e in range(2)], axis=0
            )
            out_ref[p * parts : (p + 2) * parts, lanes] = both.astype(BF16)
        extra = out_ref.shape[0] - parents * parts
        start = forward.shape[0] - extra * (samples // LANES - t)
        out_ref[parents * parts :, lanes] = forward[start : start + extra]


def zone(parents):
    return [d for d in range(-parents, parents + 1) if abs(d) >= 2]


def half_of(mats, late):
    count = mats.shape[0]
    odd = lax.rem(lax.axis_index("samp"), 2)
    return pl.ds(count * (odd if late else 1 - odd), count)


def prep_kernel(
    inter, trans, table_hbm, interp_hbm, phase_hbm, neighbours, mats_hbm, after,
    dense, interp_ref, phase_ref, nbr, mats, inter_s, trans_s, table, sems, *, parents, all_parents,
):
    samples = interp_ref.shape[0]
    mine = pl.ds(pl.multiple_of(lax.axis_index("samp") * samples, samples), samples)
    copies = [
        pltpu.make_async_copy(inter, inter_s, sems.at[0]),
        pltpu.make_async_copy(trans, trans_s, sems.at[1]),
        pltpu.make_async_copy(table_hbm, table, sems.at[2]),
        pltpu.make_async_copy(interp_hbm.at[mine], interp_ref, sems.at[3]),
        pltpu.make_async_copy(phase_hbm.at[:, :, mine], phase_ref, sems.at[4]),
        pltpu.make_async_copy(neighbours, nbr, sems.at[5]),
        pltpu.make_async_copy(mats_hbm.at[half_of(mats, False)], mats, sems.at[6]),
    ]
    for copy in copies:
        copy.start()
    for copy in copies[:3]:
        copy.wait()
    if len(zone(parents)) > inter.shape[1]:
        dense[...] = jnp.zeros_like(dense)
    first = lax.axis_index("box") * parents

    def fill(p, carry):
        for k in range(inter.shape[1]):
            rel = lax.rem(inter_s[p, k] - first - p + parents + all_parents, all_parents)
            at = jnp.where(rel < parents, rel, rel - 3)
            dense[p, at] = table[trans_s[p, k]]
        return carry

    lax.fori_loop(0, parents, fill, 0)
    for copy in copies[3:]:
        copy.wait()


def down_kernel(
    own, across, beside, dense, interp_ref, phase_ref, place_ref, after, *refs, pieces, boxes, parents, parts
):
    outs = refs[:pieces]
    window, incoming, shifted = refs[pieces:]
    samples = interp_ref.shape[0]
    slots = 8 * parents
    half = parts // 2
    odd = lax.rem(lax.axis_index("box"), 2)
    rows = parents * parts
    window[parents : 2 * parents] = own[:rows].astype(F32).reshape(parents, parts, samples)
    window[pl.ds(2 * parents * odd, parents)] = (
        across[:rows].astype(F32).reshape(parents, parts, samples)
    )
    window[pl.ds(2 * parents * (1 - odd), parents)] = (
        beside[:rows].astype(F32).reshape(parents, parts, samples)
    )
    offsets = zone(parents)

    def one(p):
        for t in range(samples // LANES):
            lanes = slice(t * LANES, (t + 1) * LANES)
            acc_r = acc_i = None
            for i, d in enumerate(offsets):
                x = window[parents + p + d, :, lanes]
                yr = dense[p, i, 0:1, lanes] * x
                yi = dense[p, i, 1:2, lanes] * x
                acc_r = yr if acc_r is None else acc_r + yr
                acc_i = yi if acc_i is None else acc_i + yi
            got = (acc_r + times_i(acc_i)).astype(BF16).astype(F32)
            incoming[t, pl.ds(p * parts, parts), :] = got

    if parents <= 8:
        for p in range(parents):
            one(p)
    else:
        lax.fori_loop(0, parents, lambda p, c: (one(p), c)[1], 0)
    for t in range(samples // LANES):
        lanes = slice(t * LANES, (t + 1) * LANES)
        for r in range(half):
            ir = incoming[t, pl.ds(r, parents, stride=parts), :]
            ii = incoming[t, pl.ds(half + r, parents, stride=parts), :]
            re, im = [], []
            for o in range(8):
                ph_r = phase_ref[o, 0:1, lanes]
                ph_i = phase_ref[o, 1:2, lanes]
                re.append(ph_r * ir - ph_i * ii)
                im.append(ph_r * ii + ph_i * ir)
            shifted[r * slots : (r + 1) * slots, lanes] = jnp.concatenate(re, axis=0).astype(BF16)
            shifted[(half + r) * slots : (half + r + 1) * slots, lanes] = jnp.concatenate(
                im, axis=0
            ).astype(BF16)
    field = nn_dot(shifted[...], interp_ref[...]).astype(BF16)
    spread = jnp.concatenate([field[c * slots : (c + 1) * slots] for c in range(parts)], axis=1)
    leaves = nn_dot(place_ref[...], spread).astype(BF16)
    for d in range(pieces):
        for c in range(parts):
            outs[d][c * boxes : (c + 1) * boxes] = leaves[
                d * boxes : (d + 1) * boxes, c * LANES : (c + 1) * LANES
            ]


def near_kernel(*refs, late, nsamp, total, halo_rows, parent_rows):
    if late:
        neighbours, own, mats, after, across, beside, *from_far, out_ref, window, nbr, sems = refs
    else:
        neighbours, own, mats, after, from_beside, mats_hbm, out_ref, more, window, nbr, sems = refs
        fetch = pltpu.make_async_copy(mats_hbm.at[half_of(more, True)], more, sems.at[1])
        fetch.start()
    list_copy = pltpu.make_async_copy(neighbours, nbr, sems.at[0])
    list_copy.start()
    count, parts, unknowns = out_ref.shape
    boxes = own.shape[0] // parts
    near_count = mats.shape[1]
    samp = lax.axis_index("samp")
    box = lax.axis_index("box")
    odd = lax.rem(samp, 2)
    first = count * (odd if late else 1 - odd)

    def piece(ref):
        return ref[ref.shape[0] - halo_rows :].astype(F32)

    if late:
        def forwarded(ref):
            return jnp.concatenate(
                [
                    ref[parent_rows:, t * LANES : (t + 1) * LANES].astype(F32)
                    for t in range(ref.shape[1] // LANES)
                ],
                axis=0,
            )

        partner = samp ^ (samp - 1 + 2 * odd)
        halo = piece(from_far[0])
        for i in range(1, len(from_far)):
            halo = jnp.where(partner == (4 << i) - 1, piece(from_far[i]), halo)
        box_odd = lax.rem(box, 2) == 1
        from_left = samp == 0
        passed = jnp.where(box_odd == from_left, forwarded(beside), forwarded(across))
        halo = jnp.where(jnp.logical_or(from_left, samp == nsamp - 1), passed, halo)
    else:
        halo = piece(from_beside)
    at = jnp.where(first > 0, boxes + count, 0)
    for i in range(count):
        window[at + i] = widen(halo[i * parts : (i + 1) * parts])
    mine = own[...].astype(F32)
    for i in range(boxes):
        window[count + i] = widen(mine[i * parts : (i + 1) * parts])
    list_copy.wait()
    base = (box * nsamp + samp) * boxes
    for i in range(count):
        acc = None
        for k in range(near_count):
            j = lax.rem(nbr[k, first + i] - base + count + total, total)
            mat = jnp.concatenate([mats[i, k, 0], mats[i, k, 1]], axis=1)
            y = nt_dot(window[j].astype(BF16), mat)
            acc = y if acc is None else acc + y
        out_ref[i] = acc
    if not late:
        fetch.wait()


def final_kernel(*refs, pieces):
    parts_in = refs[:pieces]
    near_early, near_late, mats, out_ref, field = refs[pieces:]
    boxes, halves, rhs = out_ref.shape[:3]
    parts = halves * rhs
    half = boxes // 2
    odd = lax.rem(lax.axis_index("samp"), 2) == 1
    total = parts_in[0][...].astype(F32)
    for m in parts_in[1:]:
        total += m[...].astype(F32)
    field[...] = total.astype(BF16).astype(F32)
    for n in range(boxes):
        v = field[pl.ds(n, parts, stride=boxes), :]
        wide = jnp.concatenate([v, times_i(v)], axis=1).astype(BF16)
        y = nt_dot(wide, jnp.concatenate([mats[n, 0], mats[n, 1]], axis=1))
        i = n % half
        y = y + jnp.where(odd == (n < half), near_early[i], near_late[i])
        out_ref[n, 0] = y[:rhs]
        out_ref[n, 1] = y[rhs:]


def whole_in(kind):
    return pl.BlockSpec(memory_space=kind)


VM = pltpu.VMEM
SM = pltpu.SMEM
HBM = pltpu.HBM
DMA = pltpu.SemaphoreType.DMA
PARAMS = pltpu.CompilerParams(vmem_limit_bytes=24 * 1024 * 1024)


def stay(x):
    return pltpu.with_memory_space_constraint(x, HBM)


def on_device(
    xvec,
    near_blocks,
    neighbours,
    lift,
    place,
    interp,
    phases,
    octant,
    leaf_parent_index,
    translators,
    inter_list,
    trans_id,
):
    boxes, halves, rhs, unknowns = xvec.shape
    parts = halves * rhs
    nsamp = lax.axis_size("samp")
    nbox = lax.axis_size("box")
    total = boxes * nsamp * nbox
    reach = boxes // 2
    parents = boxes * nsamp // 8
    all_parents = parents * nbox
    samples = interp.shape[0] // nsamp
    slots = 8 * parents
    leaves = boxes * nsamp
    near_count = near_blocks.shape[1]
    halo_rows = reach * parts
    parent_rows = parents * parts
    plain_rows = (parts + 1) * boxes

    def shape(dims, dtype=BF16):
        return jax.ShapeDtypeStruct(dims, dtype)

    lift_chunks = 4
    plain, to_beside, to_far, x_rows = pl.pallas_call(
        lambda *refs: leaf_kernel(*refs, parents=parents),
        in_specs=[whole_in(HBM)] * 4,
        out_specs=[whole_in(VM)] * 4,
        out_shape=[
            shape((plain_rows, LANES)),
            shape((plain_rows + halo_rows, LANES)),
            shape((plain_rows + halo_rows, LANES)),
            shape((boxes * parts, LANES)),
        ],
        scratch_shapes=[
            VM(xvec.shape, BF16),
            VM((parts * boxes, LANES), F32),
            VM(lift.shape, BF16),
            SM((boxes,), jnp.int32),
            SM((boxes,), jnp.int32),
            DMA((lift_chunks + 3,)),
        ],
        compiler_params=PARAMS,
        name="leaf",
    )(*[stay(a) for a in (octant, leaf_parent_index, xvec, lift)])

    def exchange(x, d):
        return lax.ppermute(x, "samp", [(i, i ^ d) for i in range(nsamp)])

    messages = [plain] + [None] * (nsamp - 1)
    far = [(4 << i) - 1 for i in range(nsamp.bit_length() - 2)]
    for d in reversed(range(1, nsamp)):
        messages[d] = exchange(to_beside if d == 1 else to_far if d in far else plain, d)
    far_messages = [messages[d] for d in far]

    dense, my_interp, my_phases, near_list, mats_early = pl.pallas_call(
        lambda *refs: prep_kernel(*refs, parents=parents, all_parents=all_parents),
        in_specs=[whole_in(HBM)] * 7 + [whole_in(VM)],
        out_specs=[whole_in(VM)] * 5,
        out_shape=[
            shape((parents, len(zone(parents)), 2, samples), F32),
            shape((samples, LANES)),
            shape((8, 2, samples), F32),
            shape((near_count, boxes), jnp.int32),
            shape((reach,) + near_blocks.shape[1:]),
        ],
        scratch_shapes=[
            SM(inter_list.shape, jnp.int32),
            SM(trans_id.shape, jnp.int32),
            VM(translators.shape, F32),
            DMA((7,)),
        ],
        compiler_params=PARAMS,
        cost_estimate=pl.CostEstimate(
            flops=0, bytes_accessed=4 * 1024 * 1024, transcendentals=0
        ),
        name="prep",
    )(
        *[stay(a) for a in (inter_list, trans_id, translators, interp, phases)],
        stay(neighbours.T),
        stay(near_blocks),
        x_rows,
    )

    parent_pat, place_onehot = pl.pallas_call(
        lambda *refs: up_kernel(
            *refs, pieces=nsamp, boxes=boxes, parents=parents, parts=parts
        ),
        in_specs=[whole_in(VM)] * (nsamp + 2),
        out_specs=[whole_in(VM)] * 2,
        out_shape=[
            shape((parent_rows + halo_rows * LANES // samples, samples)),
            shape((leaves, slots)),
        ],
        scratch_shapes=[
            VM((parts * slots, samples), F32),
            VM((samples // LANES, parent_rows, LANES), F32),
        ],
        compiler_params=PARAMS,
        name="up",
    )(*messages, my_interp, my_phases)

    across = lax.ppermute(
        parent_pat, "box", [(i, (i + (1 if i % 2 else -1)) % nbox) for i in range(nbox)]
    )
    beside = lax.ppermute(parent_pat, "box", [(i, i ^ 1) for i in range(nbox)])

    def near_half(late, args):
        out_shape = [shape((reach, parts, unknowns), F32)]
        in_specs = [whole_in(VM)] * len(args)
        if not late:
            out_shape.append(shape(mats_early.shape))
            in_specs[-1] = whole_in(HBM)
        return pl.pallas_call(
            lambda *refs: near_kernel(
                *refs,
                late=late,
                nsamp=nsamp,
                total=total,
                halo_rows=halo_rows,
                parent_rows=parent_rows,
            ),
            in_specs=[whole_in(VM)] * 2 + in_specs,
            out_specs=[whole_in(VM)] * len(out_shape),
            out_shape=out_shape,
            scratch_shapes=[
                VM((boxes + 2 * reach, parts, 2 * unknowns), F32),
                SM((near_count, boxes), jnp.int32),
                DMA((2,)),
            ],
            compiler_params=PARAMS,
            cost_estimate=pl.CostEstimate(
                flops=parts * near_blocks.size,
                bytes_accessed=near_blocks.size,
                transcendentals=0,
            ),
            name="near",
        )(near_list, x_rows, *args)

    near_early, mats_late = near_half(
        False, [mats_early, place_onehot, messages[1], stay(near_blocks)]
    )

    fields = pl.pallas_call(
        lambda *refs: down_kernel(
            *refs, pieces=nsamp, boxes=boxes, parents=parents, parts=parts
        ),
        in_specs=[whole_in(VM)] * 8,
        out_specs=[whole_in(VM)] * nsamp,
        out_shape=[shape((parts * boxes, LANES))] * nsamp,
        scratch_shapes=[
            VM((3 * parents, parts, samples), F32),
            VM((samples // LANES, parent_rows, LANES), F32),
            VM((parts * slots, samples), BF16),
        ],
        compiler_params=PARAMS,
        name="down",
    )(parent_pat, across, beside, dense, my_interp, my_phases, place_onehot, near_early)

    partial = [fields[0]] + [None] * (nsamp - 1)
    for d in reversed(range(1, nsamp)):
        partial[d] = exchange(fields[d], d)

    (near_late,) = near_half(True, [mats_late, fields[0], across, beside, *far_messages])

    return pl.pallas_call(
        lambda *refs: final_kernel(*refs, pieces=nsamp),
        in_specs=[whole_in(VM)] * (nsamp + 3),
        out_specs=whole_in(VM),
        out_shape=shape(xvec.shape, F32),
        scratch_shapes=[VM((parts * boxes, LANES), F32)],
        compiler_params=PARAMS,
        name="final",
    )(*partial, near_early, near_late, place)


def solution(mesh):
    in_specs = (
        P(("box", "samp"), None, None, None),
        P(("box", "samp"), None, None, None, None),
        P(("box", "samp"), None),
        P(("box", "samp"), None, None, None),
        P(("box", "samp"), None, None, None),
        P(),
        P(),
        P(("box", "samp")),
        P(("box", "samp")),
        P(None, None, "samp"),
        P("box", None),
        P("box", None),
    )
    out_specs = P(("box", "samp"), None, None, None)
    return jax.shard_map(
        on_device, mesh=mesh, in_specs=in_specs, out_specs=out_specs, check_vma=False
    )
```

```python
import jax
import jax.numpy as jnp
from jax import lax
from jax.experimental import pallas as pl
from jax.experimental.pallas import tpu as pltpu
from jax.sharding import PartitionSpec as P

F32 = jnp.float32
BF16 = jnp.bfloat16
LANES = 128


def nt_dot(a, b):
    return lax.dot_general(a, b, (((1,), (1,)), ((), ())), preferred_element_type=F32)


def nn_dot(a, b):
    return lax.dot_general(a, b, (((1,), (0,)), ((), ())), preferred_element_type=F32)


def times_i(v):
    half = v.shape[0] // 2
    return jnp.concatenate([-v[half:], v[:half]], axis=0)


def widen(v):
    return jnp.concatenate([v, times_i(v)], axis=1)


def leaf_kernel(
    octant, parent, x_hbm, lift_hbm, to_far, plain, to_beside, x_rows,
    x_ref, rows, lift, oct_s, par_s, sems, *, parents,
):
    boxes, halves, rhs, _ = x_ref.shape
    parts = halves * rhs
    reach = boxes // 2
    chunks = sems.shape[0] - 3
    per = boxes // chunks
    small = [
        pltpu.make_async_copy(x_hbm, x_ref, sems.at[chunks]),
        pltpu.make_async_copy(octant, oct_s, sems.at[chunks + 1]),
        pltpu.make_async_copy(parent, par_s, sems.at[chunks + 2]),
    ]
    big = [
        pltpu.make_async_copy(
            lift_hbm.at[pl.ds(i * per, per)], lift.at[pl.ds(i * per, per)], sems.at[i]
        )
        for i in range(chunks)
    ]
    for copy in small + big:
        copy.start()
    for copy in small:
        copy.wait()
    own = [
        jnp.concatenate([x_ref[n, 0].astype(F32), x_ref[n, 1].astype(F32)], axis=0)
        for n in range(boxes)
    ]
    lane = lax.rem(lax.broadcasted_iota(jnp.int32, (boxes, LANES), 1), boxes)
    codes = jnp.zeros((boxes, LANES), F32)
    for n in range(boxes):
        slot = (oct_s[n] * parents + lax.rem(par_s[n], parents)).astype(F32)
        codes = jnp.where(lane == n, slot, codes)
    codes = codes.astype(BF16)
    x_rows[...] = jnp.concatenate(own, axis=0).astype(BF16)
    first = jnp.concatenate(own[:reach], axis=0)
    last = jnp.concatenate(own[reach:], axis=0)
    odd = lax.rem(lax.axis_index("samp"), 2) == 1
    at = parts * boxes
    to_beside[at + boxes :] = jnp.where(odd, first, last).astype(BF16)
    to_far[at + boxes :] = jnp.where(odd, last, first).astype(BF16)
    for ref in (plain, to_beside, to_far):
        ref[at : at + boxes] = codes
    for n in range(boxes):
        if n % per == 0:
            big[n // per].wait()
        mat = jnp.concatenate([lift[n, 0], lift[n, 1]], axis=1)
        rows[pl.ds(n, parts, stride=boxes), :] = nt_dot(widen(own[n]).astype(BF16), mat)
    pattern = rows[...].astype(BF16)
    for ref in (plain, to_beside, to_far):
        ref[:at] = pattern


def up_kernel(*refs, pieces, boxes, parents, parts):
    msgs = refs[:pieces]
    interp_ref, phase_ref, out_ref, out_copy, place_ref, raised, folded = refs[pieces:]
    forward = msgs[1]
    slots = 8 * parents
    samples = interp_ref.shape[0]
    per_tile = LANES // boxes
    at = parts * boxes
    tiles = []
    for t in range(0, pieces, per_tile):
        lane = lax.broadcasted_iota(jnp.int32, (boxes, LANES), 1) // boxes
        code = msgs[t][at : at + boxes].astype(F32)
        for d in range(1, min(per_tile, pieces - t)):
            code = jnp.where(lane == d, msgs[t + d][at : at + boxes].astype(F32), code)
        code = jnp.concatenate([code] * (slots // boxes), axis=0)
        want = lax.broadcasted_iota(jnp.int32, (slots, LANES), 0).astype(F32)
        width = min(per_tile, pieces - t) * boxes
        tiles.append(jnp.where(code == want, 1.0, 0.0)[:, :width])
    sorter = jnp.concatenate(tiles, axis=1)
    place_ref[...] = sorter.T.astype(BF16)
    sorter = sorter.astype(BF16)
    pats = jnp.concatenate(
        [
            jnp.concatenate([m[c * boxes : (c + 1) * boxes] for m in msgs], axis=0)
            for c in range(parts)
        ],
        axis=1,
    )
    ordered = nn_dot(sorter, pats).astype(BF16)
    for c in range(parts):
        raised[c * slots : (c + 1) * slots] = nt_dot(
            ordered[:, c * LANES : (c + 1) * LANES], interp_ref[...]
        )
    half = parts // 2
    for t in range(samples // LANES):
        lanes = slice(t * LANES, (t + 1) * LANES)
        for r in range(half):
            re = im = None
            for o in range(8):
                ph_r = phase_ref[o, 0:1, lanes]
                ph_i = phase_ref[o, 1:2, lanes]
                base_r = r * slots + o * parents
                base_i = (half + r) * slots + o * parents
                xr = raised[base_r : base_r + parents, lanes]
                xi = raised[base_i : base_i + parents, lanes]
                dr = ph_r * xr - ph_i * xi
                di = ph_r * xi + ph_i * xr
                re = dr if re is None else re + dr
                im = di if im is None else im + di
            folded[t, r * parents : (r + 1) * parents] = re
            folded[t, (half + r) * parents : (half + r + 1) * parents] = im
        for p in range(0, parents, 2):
            both = jnp.concatenate(
                [folded[t, pl.ds(p + e, parts, stride=parents), :] for e in range(2)], axis=0
            )
            both = both.astype(BF16)
            for ref in (out_ref, out_copy):
                ref[p * parts : (p + 2) * parts, lanes] = both
        extra = out_ref.shape[0] - parents * parts
        start = forward.shape[0] - extra * (samples // LANES - t)
        for ref in (out_ref, out_copy):
            ref[parents * parts :, lanes] = forward[start : start + extra]


def zone(parents):
    return [d for d in range(-parents, parents + 1) if abs(d) >= 2]


def half_of(mats, late):
    count = mats.shape[0]
    odd = lax.rem(lax.axis_index("samp"), 2)
    return pl.ds(count * (odd if late else 1 - odd), count)


def prep_kernel(
    inter, trans, table_hbm, interp_hbm, phase_hbm, neighbours, mats_hbm, after,
    dense, interp_ref, phase_ref, nbr, mats, inter_s, trans_s, table, sems, *, parents, all_parents,
):
    samples = interp_ref.shape[0]
    mine = pl.ds(pl.multiple_of(lax.axis_index("samp") * samples, samples), samples)
    copies = [
        pltpu.make_async_copy(inter, inter_s, sems.at[0]),
        pltpu.make_async_copy(trans, trans_s, sems.at[1]),
        pltpu.make_async_copy(table_hbm, table, sems.at[2]),
        pltpu.make_async_copy(interp_hbm.at[mine], interp_ref, sems.at[3]),
        pltpu.make_async_copy(phase_hbm.at[:, :, mine], phase_ref, sems.at[4]),
        pltpu.make_async_copy(neighbours, nbr, sems.at[5]),
        pltpu.make_async_copy(mats_hbm.at[half_of(mats, False)], mats, sems.at[6]),
    ]
    for copy in copies:
        copy.start()
    for copy in copies[:3]:
        copy.wait()
    if len(zone(parents)) > inter.shape[1]:
        dense[...] = jnp.zeros_like(dense)
    first = lax.axis_index("box") * parents

    def fill(p, carry):
        for k in range(inter.shape[1]):
            rel = lax.rem(inter_s[p, k] - first - p + parents + all_parents, all_parents)
            at = jnp.where(rel < parents, rel, rel - 3)
            dense[p, at] = table[trans_s[p, k]]
        return carry

    lax.fori_loop(0, parents, fill, 0)
    for copy in copies[3:]:
        copy.wait()


def down_kernel(
    own, across, beside, dense, interp_ref, phase_ref, place_ref, after, *refs, pieces, boxes, parents, parts
):
    outs = refs[:pieces]
    window, incoming, shifted = refs[pieces:]
    samples = interp_ref.shape[0]
    slots = 8 * parents
    half = parts // 2
    odd = lax.rem(lax.axis_index("box"), 2)
    rows = parents * parts
    window[parents : 2 * parents] = own[:rows].astype(F32).reshape(parents, parts, samples)
    window[pl.ds(2 * parents * odd, parents)] = (
        across[:rows].astype(F32).reshape(parents, parts, samples)
    )
    window[pl.ds(2 * parents * (1 - odd), parents)] = (
        beside[:rows].astype(F32).reshape(parents, parts, samples)
    )
    offsets = zone(parents)

    def one(p):
        for t in range(samples // LANES):
            lanes = slice(t * LANES, (t + 1) * LANES)
            acc_r = acc_i = None
            for i, d in enumerate(offsets):
                x = window[parents + p + d, :, lanes]
                yr = dense[p, i, 0:1, lanes] * x
                yi = dense[p, i, 1:2, lanes] * x
                acc_r = yr if acc_r is None else acc_r + yr
                acc_i = yi if acc_i is None else acc_i + yi
            got = (acc_r + times_i(acc_i)).astype(BF16).astype(F32)
            incoming[t, pl.ds(p * parts, parts), :] = got

    if parents <= 8:
        for p in range(parents):
            one(p)
    else:
        lax.fori_loop(0, parents, lambda p, c: (one(p), c)[1], 0)
    for t in range(samples // LANES):
        lanes = slice(t * LANES, (t + 1) * LANES)
        for r in range(half):
            ir = incoming[t, pl.ds(r, parents, stride=parts), :]
            ii = incoming[t, pl.ds(half + r, parents, stride=parts), :]
            re, im = [], []
            for o in range(8):
                ph_r = phase_ref[o, 0:1, lanes]
                ph_i = phase_ref[o, 1:2, lanes]
                re.append(ph_r * ir - ph_i * ii)
                im.append(ph_r * ii + ph_i * ir)
            shifted[r * slots : (r + 1) * slots, lanes] = jnp.concatenate(re, axis=0).astype(BF16)
            shifted[(half + r) * slots : (half + r + 1) * slots, lanes] = jnp.concatenate(
                im, axis=0
            ).astype(BF16)
    field = nn_dot(shifted[...], interp_ref[...]).astype(BF16)
    spread = jnp.concatenate([field[c * slots : (c + 1) * slots] for c in range(parts)], axis=1)
    leaves = nn_dot(place_ref[...], spread).astype(BF16)
    for d in range(pieces):
        for c in range(parts):
            outs[d][c * boxes : (c + 1) * boxes] = leaves[
                d * boxes : (d + 1) * boxes, c * LANES : (c + 1) * LANES
            ]


def near_kernel(*refs, late, nsamp, total, halo_rows, parent_rows):
    if late:
        neighbours, own, mats, after, across, beside, *from_far, out_ref, window, nbr, sems = refs
    else:
        neighbours, own, mats, after, from_beside, mats_hbm, out_ref, more, window, nbr, sems = refs
        fetch = pltpu.make_async_copy(mats_hbm.at[half_of(more, True)], more, sems.at[1])
        fetch.start()
    list_copy = pltpu.make_async_copy(neighbours, nbr, sems.at[0])
    list_copy.start()
    count, parts, unknowns = out_ref.shape
    boxes = own.shape[0] // parts
    near_count = mats.shape[1]
    samp = lax.axis_index("samp")
    box = lax.axis_index("box")
    odd = lax.rem(samp, 2)
    first = count * (odd if late else 1 - odd)

    def piece(ref):
        return ref[ref.shape[0] - halo_rows :].astype(F32)

    if late:
        def forwarded(ref):
            return jnp.concatenate(
                [
                    ref[parent_rows:, t * LANES : (t + 1) * LANES].astype(F32)
                    for t in range(ref.shape[1] // LANES)
                ],
                axis=0,
            )

        partner = samp ^ (samp - 1 + 2 * odd)
        halo = piece(from_far[0])
        for i in range(1, len(from_far)):
            halo = jnp.where(partner == (4 << i) - 1, piece(from_far[i]), halo)
        box_odd = lax.rem(box, 2) == 1
        from_left = samp == 0
        passed = jnp.where(box_odd == from_left, forwarded(beside), forwarded(across))
        halo = jnp.where(jnp.logical_or(from_left, samp == nsamp - 1), passed, halo)
    else:
        halo = piece(from_beside)
    at = jnp.where(first > 0, boxes + count, 0)
    for i in range(count):
        window[at + i] = widen(halo[i * parts : (i + 1) * parts])
    mine = own[...].astype(F32)
    for i in range(boxes):
        window[count + i] = widen(mine[i * parts : (i + 1) * parts])
    list_copy.wait()
    base = (box * nsamp + samp) * boxes
    for i in range(count):
        acc = None
        for k in range(near_count):
            j = lax.rem(nbr[k, first + i] - base + count + total, total)
            mat = jnp.concatenate([mats[i, k, 0], mats[i, k, 1]], axis=1)
            y = nt_dot(window[j].astype(BF16), mat)
            acc = y if acc is None else acc + y
        out_ref[i] = acc
    if not late:
        fetch.wait()


def final_kernel(*refs, pieces):
    parts_in = refs[:pieces]
    near_early, near_late, mats, out_ref, field = refs[pieces:]
    boxes, halves, rhs = out_ref.shape[:3]
    parts = halves * rhs
    half = boxes // 2
    odd = lax.rem(lax.axis_index("samp"), 2) == 1
    total = parts_in[0][...].astype(F32)
    for m in parts_in[1:]:
        total += m[...].astype(F32)
    field[...] = total.astype(BF16).astype(F32)
    for n in range(boxes):
        v = field[pl.ds(n, parts, stride=boxes), :]
        wide = jnp.concatenate([v, times_i(v)], axis=1).astype(BF16)
        y = nt_dot(wide, jnp.concatenate([mats[n, 0], mats[n, 1]], axis=1))
        i = n % half
        y = y + jnp.where(odd == (n < half), near_early[i], near_late[i])
        out_ref[n, 0] = y[:rhs]
        out_ref[n, 1] = y[rhs:]


def whole_in(kind):
    return pl.BlockSpec(memory_space=kind)


VM = pltpu.VMEM
SM = pltpu.SMEM
HBM = pltpu.HBM
DMA = pltpu.SemaphoreType.DMA
PARAMS = pltpu.CompilerParams(vmem_limit_bytes=24 * 1024 * 1024)


def stay(x):
    return pltpu.with_memory_space_constraint(x, HBM)


def on_device(
    xvec,
    near_blocks,
    neighbours,
    lift,
    place,
    interp,
    phases,
    octant,
    leaf_parent_index,
    translators,
    inter_list,
    trans_id,
):
    boxes, halves, rhs, unknowns = xvec.shape
    parts = halves * rhs
    nsamp = lax.axis_size("samp")
    nbox = lax.axis_size("box")
    total = boxes * nsamp * nbox
    reach = boxes // 2
    parents = boxes * nsamp // 8
    all_parents = parents * nbox
    samples = interp.shape[0] // nsamp
    slots = 8 * parents
    leaves = boxes * nsamp
    near_count = near_blocks.shape[1]
    halo_rows = reach * parts
    parent_rows = parents * parts
    plain_rows = (parts + 1) * boxes

    def shape(dims, dtype=BF16):
        return jax.ShapeDtypeStruct(dims, dtype)

    lift_chunks = 4
    to_far, plain, to_beside, x_rows = pl.pallas_call(
        lambda *refs: leaf_kernel(*refs, parents=parents),
        in_specs=[whole_in(HBM)] * 4,
        out_specs=[whole_in(VM)] * 4,
        out_shape=[
            shape((plain_rows + halo_rows, LANES)),
            shape((plain_rows, LANES)),
            shape((plain_rows + halo_rows, LANES)),
            shape((boxes * parts, LANES)),
        ],
        scratch_shapes=[
            VM(xvec.shape, BF16),
            VM((parts * boxes, LANES), F32),
            VM(lift.shape, BF16),
            SM((boxes,), jnp.int32),
            SM((boxes,), jnp.int32),
            DMA((lift_chunks + 3,)),
        ],
        compiler_params=PARAMS,
        name="leaf",
    )(*[stay(a) for a in (octant, leaf_parent_index, xvec, lift)])

    def exchange(x, d):
        return lax.ppermute(x, "samp", [(i, i ^ d) for i in range(nsamp)])

    order = [0, *reversed(range(1, nsamp))]
    far = [(4 << i) - 1 for i in range(nsamp.bit_length() - 2)]
    messages = {0: plain}
    for d in order[1:]:
        messages[d] = exchange(to_beside if d == 1 else to_far if d in far else plain, d)
    far_messages = [messages[d] for d in far]

    dense, my_interp, my_phases, near_list, mats_early = pl.pallas_call(
        lambda *refs: prep_kernel(*refs, parents=parents, all_parents=all_parents),
        in_specs=[whole_in(HBM)] * 7 + [whole_in(VM)],
        out_specs=[whole_in(VM)] * 5,
        out_shape=[
            shape((parents, len(zone(parents)), 2, samples), F32),
            shape((samples, LANES)),
            shape((8, 2, samples), F32),
            shape((near_count, boxes), jnp.int32),
            shape((reach,) + near_blocks.shape[1:]),
        ],
        scratch_shapes=[
            SM(inter_list.shape, jnp.int32),
            SM(trans_id.shape, jnp.int32),
            VM(translators.shape, F32),
            DMA((7,)),
        ],
        compiler_params=PARAMS,
        cost_estimate=pl.CostEstimate(
            flops=0, bytes_accessed=4 * 1024 * 1024, transcendentals=0
        ),
        name="prep",
    )(
        *[stay(a) for a in (inter_list, trans_id, translators, interp, phases)],
        stay(neighbours.T),
        stay(near_blocks),
        x_rows,
    )

    to_across, parent_pat, place_onehot = pl.pallas_call(
        lambda *refs: up_kernel(
            *refs, pieces=nsamp, boxes=boxes, parents=parents, parts=parts
        ),
        in_specs=[whole_in(VM)] * (nsamp + 2),
        out_specs=[whole_in(VM)] * 3,
        out_shape=[
            shape((parent_rows + halo_rows * LANES // samples, samples)),
            shape((parent_rows + halo_rows * LANES // samples, samples)),
            shape((leaves, slots)),
        ],
        scratch_shapes=[
            VM((parts * slots, samples), F32),
            VM((samples // LANES, parent_rows, LANES), F32),
        ],
        compiler_params=PARAMS,
        name="up",
    )(*[messages[d] for d in order], my_interp, my_phases)

    across = lax.ppermute(
        to_across, "box", [(i, (i + (1 if i % 2 else -1)) % nbox) for i in range(nbox)]
    )
    beside = lax.ppermute(parent_pat, "box", [(i, i ^ 1) for i in range(nbox)])

    def near_half(late, args):
        out_shape = [shape((reach, parts, unknowns), F32)]
        in_specs = [whole_in(VM)] * len(args)
        if not late:
            out_shape.append(shape(mats_early.shape))
            in_specs[-1] = whole_in(HBM)
        return pl.pallas_call(
            lambda *refs: near_kernel(
                *refs,
                late=late,
                nsamp=nsamp,
                total=total,
                halo_rows=halo_rows,
                parent_rows=parent_rows,
            ),
            in_specs=[whole_in(VM)] * 2 + in_specs,
            out_specs=[whole_in(VM)] * len(out_shape),
            out_shape=out_shape,
            scratch_shapes=[
                VM((boxes + 2 * reach, parts, 2 * unknowns), F32),
                SM((near_count, boxes), jnp.int32),
                DMA((2,)),
            ],
            compiler_params=PARAMS,
            cost_estimate=pl.CostEstimate(
                flops=parts * near_blocks.size,
                bytes_accessed=near_blocks.size,
                transcendentals=0,
            ),
            name="near",
        )(near_list, x_rows, *args)

    near_early, mats_late = near_half(
        False, [mats_early, place_onehot, messages[1], stay(near_blocks)]
    )

    fields = pl.pallas_call(
        lambda *refs: down_kernel(
            *refs, pieces=nsamp, boxes=boxes, parents=parents, parts=parts
        ),
        in_specs=[whole_in(VM)] * 8,
        out_specs=[whole_in(VM)] * nsamp,
        out_shape=[shape((parts * boxes, LANES))] * nsamp,
        scratch_shapes=[
            VM((3 * parents, parts, samples), F32),
            VM((samples // LANES, parent_rows, LANES), F32),
            VM((parts * slots, samples), BF16),
        ],
        compiler_params=PARAMS,
        name="down",
    )(parent_pat, across, beside, dense, my_interp, my_phases, place_onehot, near_early)

    partial = [fields[0]] + [exchange(x, d) for x, d in zip(fields[1:], order[1:])]

    (near_late,) = near_half(True, [mats_late, fields[0], across, beside, *far_messages])

    return pl.pallas_call(
        lambda *refs: final_kernel(*refs, pieces=nsamp),
        in_specs=[whole_in(VM)] * (nsamp + 3),
        out_specs=whole_in(VM),
        out_shape=shape(xvec.shape, F32),
        scratch_shapes=[VM((parts * boxes, LANES), F32)],
        compiler_params=PARAMS,
        name="final",
    )(*partial, near_early, near_late, place)


def solution(mesh):
    in_specs = (
        P(("box", "samp"), None, None, None),
        P(("box", "samp"), None, None, None, None),
        P(("box", "samp"), None),
        P(("box", "samp"), None, None, None),
        P(("box", "samp"), None, None, None),
        P(),
        P(),
        P(("box", "samp")),
        P(("box", "samp")),
        P(None, None, "samp"),
        P("box", None),
        P("box", None),
    )
    out_specs = P(("box", "samp"), None, None, None)
    return jax.shard_map(
        on_device, mesh=mesh, in_specs=in_specs, out_specs=out_specs, check_vma=False
    )
```

```python
import jax
import jax.numpy as jnp
from jax import lax
from jax.experimental import pallas as pl
from jax.experimental.pallas import tpu as pltpu
from jax.sharding import PartitionSpec as P

F32 = jnp.float32
BF16 = jnp.bfloat16
LANES = 128


def nt_dot(a, b):
    return lax.dot_general(a, b, (((1,), (1,)), ((), ())), preferred_element_type=F32)


def nn_dot(a, b):
    return lax.dot_general(a, b, (((1,), (0,)), ((), ())), preferred_element_type=F32)


def times_i(v):
    half = v.shape[0] // 2
    return jnp.concatenate([-v[half:], v[:half]], axis=0)


def widen(v):
    return jnp.concatenate([v, times_i(v)], axis=1)


def leaf_kernel(
    octant, parent, x_hbm, lift_hbm, to_far, plain, to_beside, x_rows,
    x_ref, rows, lift, oct_s, par_s, sems, *, parents,
):
    boxes, halves, rhs, _ = x_ref.shape
    parts = halves * rhs
    reach = boxes // 2
    chunks = sems.shape[0] - 3
    per = boxes // chunks
    small = [
        pltpu.make_async_copy(x_hbm, x_ref, sems.at[chunks]),
        pltpu.make_async_copy(octant, oct_s, sems.at[chunks + 1]),
        pltpu.make_async_copy(parent, par_s, sems.at[chunks + 2]),
    ]
    big = [
        pltpu.make_async_copy(
            lift_hbm.at[pl.ds(i * per, per)], lift.at[pl.ds(i * per, per)], sems.at[i]
        )
        for i in range(chunks)
    ]
    for copy in small + big:
        copy.start()
    for copy in small:
        copy.wait()
    own = [
        jnp.concatenate([x_ref[n, 0].astype(F32), x_ref[n, 1].astype(F32)], axis=0)
        for n in range(boxes)
    ]
    lane = lax.rem(lax.broadcasted_iota(jnp.int32, (boxes, LANES), 1), boxes)
    codes = jnp.zeros((boxes, LANES), F32)
    for n in range(boxes):
        slot = (oct_s[n] * parents + lax.rem(par_s[n], parents)).astype(F32)
        codes = jnp.where(lane == n, slot, codes)
    codes = codes.astype(BF16)
    x_rows[...] = jnp.concatenate(own, axis=0).astype(BF16)
    first = jnp.concatenate(own[:reach], axis=0)
    last = jnp.concatenate(own[reach:], axis=0)
    odd = lax.rem(lax.axis_index("samp"), 2) == 1
    at = parts * boxes
    to_beside[at + boxes :] = jnp.where(odd, first, last).astype(BF16)
    to_far[at + boxes :] = jnp.where(odd, last, first).astype(BF16)
    for ref in (plain, to_beside, to_far):
        ref[at : at + boxes] = codes
    for n in range(boxes):
        if n % per == 0:
            big[n // per].wait()
        mat = jnp.concatenate([lift[n, 0], lift[n, 1]], axis=1)
        rows[pl.ds(n, parts, stride=boxes), :] = nt_dot(widen(own[n]).astype(BF16), mat)
    pattern = rows[...].astype(BF16)
    for ref in (plain, to_beside, to_far):
        ref[:at] = pattern


def up_kernel(*refs, pieces, boxes, parents, parts):
    msgs = refs[:pieces]
    interp_ref, phase_ref, after, out_ref, out_copy, place_ref, raised, folded = refs[pieces:]
    forward = msgs[1]
    slots = 8 * parents
    samples = raised.shape[1]
    first = lax.axis_index("samp") * samples
    mine = interp_ref[pl.ds(pl.multiple_of(first, samples), samples)]
    per_tile = LANES // boxes
    at = parts * boxes
    tiles = []
    for t in range(0, pieces, per_tile):
        lane = lax.broadcasted_iota(jnp.int32, (boxes, LANES), 1) // boxes
        code = msgs[t][at : at + boxes].astype(F32)
        for d in range(1, min(per_tile, pieces - t)):
            code = jnp.where(lane == d, msgs[t + d][at : at + boxes].astype(F32), code)
        code = jnp.concatenate([code] * (slots // boxes), axis=0)
        want = lax.broadcasted_iota(jnp.int32, (slots, LANES), 0).astype(F32)
        width = min(per_tile, pieces - t) * boxes
        tiles.append(jnp.where(code == want, 1.0, 0.0)[:, :width])
    sorter = jnp.concatenate(tiles, axis=1)
    place_ref[...] = sorter.T.astype(BF16)
    sorter = sorter.astype(BF16)
    pats = jnp.concatenate(
        [
            jnp.concatenate([m[c * boxes : (c + 1) * boxes] for m in msgs], axis=0)
            for c in range(parts)
        ],
        axis=1,
    )
    ordered = nn_dot(sorter, pats).astype(BF16)
    for c in range(parts):
        raised[c * slots : (c + 1) * slots] = nt_dot(
            ordered[:, c * LANES : (c + 1) * LANES], mine
        )
    half = parts // 2
    for t in range(samples // LANES):
        lanes = slice(t * LANES, (t + 1) * LANES)
        here = pl.ds(pl.multiple_of(first + t * LANES, LANES), LANES)
        for r in range(half):
            re = im = None
            for o in range(8):
                ph_r = phase_ref[o, 0:1, here]
                ph_i = phase_ref[o, 1:2, here]
                base_r = r * slots + o * parents
                base_i = (half + r) * slots + o * parents
                xr = raised[base_r : base_r + parents, lanes]
                xi = raised[base_i : base_i + parents, lanes]
                dr = ph_r * xr - ph_i * xi
                di = ph_r * xi + ph_i * xr
                re = dr if re is None else re + dr
                im = di if im is None else im + di
            folded[t, r * parents : (r + 1) * parents] = re
            folded[t, (half + r) * parents : (half + r + 1) * parents] = im
        for p in range(0, parents, 2):
            both = jnp.concatenate(
                [folded[t, pl.ds(p + e, parts, stride=parents), :] for e in range(2)], axis=0
            )
            both = both.astype(BF16)
            for ref in (out_ref, out_copy):
                ref[p * parts : (p + 2) * parts, lanes] = both
        extra = out_ref.shape[0] - parents * parts
        start = forward.shape[0] - extra * (samples // LANES - t)
        for ref in (out_ref, out_copy):
            ref[parents * parts :, lanes] = forward[start : start + extra]


def zone(parents):
    return [d for d in range(-parents, parents + 1) if abs(d) >= 2]


def prep_kernel(
    inter, trans, neighbours, table_hbm, mats_hbm, after, dense, nbr, inter_s, trans_s, table, sems,
    *, parents, all_parents,
):
    copies = [
        pltpu.make_async_copy(inter, inter_s, sems.at[0]),
        pltpu.make_async_copy(trans, trans_s, sems.at[1]),
        pltpu.make_async_copy(table_hbm, table, sems.at[2]),
        pltpu.make_async_copy(neighbours, nbr, sems.at[3]),
    ]
    for copy in copies:
        copy.start()
    for copy in copies[:3]:
        copy.wait()
    if len(zone(parents)) > inter.shape[1]:
        dense[...] = jnp.zeros_like(dense)
    first = lax.axis_index("box") * parents

    def fill(p, carry):
        for k in range(inter.shape[1]):
            rel = lax.rem(inter_s[p, k] - first - p + parents + all_parents, all_parents)
            at = jnp.where(rel < parents, rel, rel - 3)
            dense[p, at] = table[trans_s[p, k]]
        return carry

    lax.fori_loop(0, parents, fill, 0)
    copies[3].wait()


def down_kernel(
    own, across, beside, dense, interp_ref, phase_ref, place_ref, after, *refs, pieces, boxes, parents, parts
):
    outs = refs[:pieces]
    window, incoming, shifted = refs[pieces:]
    samples = window.shape[2]
    first = lax.axis_index("samp") * samples
    mine = interp_ref[pl.ds(pl.multiple_of(first, samples), samples)]
    slots = 8 * parents
    half = parts // 2
    odd = lax.rem(lax.axis_index("box"), 2)
    rows = parents * parts
    window[parents : 2 * parents] = own[:rows].astype(F32).reshape(parents, parts, samples)
    window[pl.ds(2 * parents * odd, parents)] = (
        across[:rows].astype(F32).reshape(parents, parts, samples)
    )
    window[pl.ds(2 * parents * (1 - odd), parents)] = (
        beside[:rows].astype(F32).reshape(parents, parts, samples)
    )
    offsets = zone(parents)

    def one(p):
        for t in range(samples // LANES):
            lanes = slice(t * LANES, (t + 1) * LANES)
            acc_r = acc_i = None
            for i, d in enumerate(offsets):
                x = window[parents + p + d, :, lanes]
                yr = dense[p, i, 0:1, lanes] * x
                yi = dense[p, i, 1:2, lanes] * x
                acc_r = yr if acc_r is None else acc_r + yr
                acc_i = yi if acc_i is None else acc_i + yi
            got = (acc_r + times_i(acc_i)).astype(BF16).astype(F32)
            incoming[t, pl.ds(p * parts, parts), :] = got

    if parents <= 8:
        for p in range(parents):
            one(p)
    else:
        lax.fori_loop(0, parents, lambda p, c: (one(p), c)[1], 0)
    for t in range(samples // LANES):
        lanes = slice(t * LANES, (t + 1) * LANES)
        here = pl.ds(pl.multiple_of(first + t * LANES, LANES), LANES)
        for r in range(half):
            ir = incoming[t, pl.ds(r, parents, stride=parts), :]
            ii = incoming[t, pl.ds(half + r, parents, stride=parts), :]
            re, im = [], []
            for o in range(8):
                ph_r = phase_ref[o, 0:1, here]
                ph_i = phase_ref[o, 1:2, here]
                re.append(ph_r * ir - ph_i * ii)
                im.append(ph_r * ii + ph_i * ir)
            shifted[r * slots : (r + 1) * slots, lanes] = jnp.concatenate(re, axis=0).astype(BF16)
            shifted[(half + r) * slots : (half + r + 1) * slots, lanes] = jnp.concatenate(
                im, axis=0
            ).astype(BF16)
    field = nn_dot(shifted[...], mine).astype(BF16)
    spread = jnp.concatenate([field[c * slots : (c + 1) * slots] for c in range(parts)], axis=1)
    leaves = nn_dot(place_ref[...], spread).astype(BF16)
    for d in range(pieces):
        for c in range(parts):
            outs[d][c * boxes : (c + 1) * boxes] = leaves[
                d * boxes : (d + 1) * boxes, c * LANES : (c + 1) * LANES
            ]


def near_kernel(*refs, late, nsamp, total, halo_rows, parent_rows):
    neighbours, own, mats, after, *halos, out_ref, window, nbr, sems = refs
    if late:
        across, beside, *from_far = halos
    else:
        (from_beside,) = halos
    list_copy = pltpu.make_async_copy(neighbours, nbr, sems.at[0])
    list_copy.start()
    count, parts, unknowns = out_ref.shape
    boxes = own.shape[0] // parts
    near_count = mats.shape[1]
    samp = lax.axis_index("samp")
    box = lax.axis_index("box")
    odd = lax.rem(samp, 2)
    first = count * (odd if late else 1 - odd)

    def piece(ref):
        return ref[ref.shape[0] - halo_rows :].astype(F32)

    if late:
        def forwarded(ref):
            return jnp.concatenate(
                [
                    ref[parent_rows:, t * LANES : (t + 1) * LANES].astype(F32)
                    for t in range(ref.shape[1] // LANES)
                ],
                axis=0,
            )

        partner = samp ^ (samp - 1 + 2 * odd)
        halo = piece(from_far[0])
        for i in range(1, len(from_far)):
            halo = jnp.where(partner == (4 << i) - 1, piece(from_far[i]), halo)
        box_odd = lax.rem(box, 2) == 1
        from_left = samp == 0
        passed = jnp.where(box_odd == from_left, forwarded(beside), forwarded(across))
        halo = jnp.where(jnp.logical_or(from_left, samp == nsamp - 1), passed, halo)
    else:
        halo = piece(from_beside)
    at = jnp.where(first > 0, boxes + count, 0)
    for i in range(count):
        window[at + i] = widen(halo[i * parts : (i + 1) * parts])
    mine = own[...].astype(F32)
    for i in range(boxes):
        window[count + i] = widen(mine[i * parts : (i + 1) * parts])
    list_copy.wait()
    base = (box * nsamp + samp) * boxes
    for i in range(count):
        acc = None
        for k in range(near_count):
            j = lax.rem(nbr[k, first + i] - base + count + total, total)
            mat = jnp.concatenate([mats[first + i, k, 0], mats[first + i, k, 1]], axis=1)
            y = nt_dot(window[j].astype(BF16), mat)
            acc = y if acc is None else acc + y
        out_ref[i] = acc


def final_kernel(*refs, pieces):
    parts_in = refs[:pieces]
    near_early, near_late, mats, out_ref, field = refs[pieces:]
    boxes, halves, rhs = out_ref.shape[:3]
    parts = halves * rhs
    half = boxes // 2
    odd = lax.rem(lax.axis_index("samp"), 2) == 1
    total = parts_in[0][...].astype(F32)
    for m in parts_in[1:]:
        total += m[...].astype(F32)
    field[...] = total.astype(BF16).astype(F32)
    for n in range(boxes):
        v = field[pl.ds(n, parts, stride=boxes), :]
        wide = jnp.concatenate([v, times_i(v)], axis=1).astype(BF16)
        y = nt_dot(wide, jnp.concatenate([mats[n, 0], mats[n, 1]], axis=1))
        i = n % half
        y = y + jnp.where(odd == (n < half), near_early[i], near_late[i])
        out_ref[n, 0] = y[:rhs]
        out_ref[n, 1] = y[rhs:]


def whole_in(kind):
    return pl.BlockSpec(memory_space=kind)


VM = pltpu.VMEM
SM = pltpu.SMEM
HBM = pltpu.HBM
DMA = pltpu.SemaphoreType.DMA
PARAMS = pltpu.CompilerParams(vmem_limit_bytes=24 * 1024 * 1024)


def stay(x):
    return pltpu.with_memory_space_constraint(x, HBM)


def on_device(
    xvec,
    near_blocks,
    neighbours,
    lift,
    place,
    interp,
    phases,
    octant,
    leaf_parent_index,
    translators,
    inter_list,
    trans_id,
):
    boxes, halves, rhs, unknowns = xvec.shape
    parts = halves * rhs
    nsamp = lax.axis_size("samp")
    nbox = lax.axis_size("box")
    total = boxes * nsamp * nbox
    reach = boxes // 2
    parents = boxes * nsamp // 8
    all_parents = parents * nbox
    samples = interp.shape[0] // nsamp
    slots = 8 * parents
    leaves = boxes * nsamp
    near_count = near_blocks.shape[1]
    halo_rows = reach * parts
    parent_rows = parents * parts
    plain_rows = (parts + 1) * boxes

    def shape(dims, dtype=BF16):
        return jax.ShapeDtypeStruct(dims, dtype)

    lift_chunks = 4
    to_far, plain, to_beside, x_rows = pl.pallas_call(
        lambda *refs: leaf_kernel(*refs, parents=parents),
        in_specs=[whole_in(HBM)] * 4,
        out_specs=[whole_in(VM)] * 4,
        out_shape=[
            shape((plain_rows + halo_rows, LANES)),
            shape((plain_rows, LANES)),
            shape((plain_rows + halo_rows, LANES)),
            shape((boxes * parts, LANES)),
        ],
        scratch_shapes=[
            VM(xvec.shape, BF16),
            VM((parts * boxes, LANES), F32),
            VM(lift.shape, BF16),
            SM((boxes,), jnp.int32),
            SM((boxes,), jnp.int32),
            DMA((lift_chunks + 3,)),
        ],
        compiler_params=PARAMS,
        name="leaf",
    )(*[stay(a) for a in (octant, leaf_parent_index, xvec, lift)])

    def exchange(x, d):
        return lax.ppermute(x, "samp", [(i, i ^ d) for i in range(nsamp)])

    order = [0, nsamp - 1, *range(1, nsamp - 1)]
    far = [(4 << i) - 1 for i in range(nsamp.bit_length() - 2)]
    messages = {0: plain}
    for d in order[1:]:
        messages[d] = exchange(to_beside if d == 1 else to_far if d in far else plain, d)
    far_messages = [messages[d] for d in far]

    dense, near_list = pl.pallas_call(
        lambda *refs: prep_kernel(*refs, parents=parents, all_parents=all_parents),
        in_specs=[whole_in(HBM)] * 5 + [whole_in(VM)],
        out_specs=[whole_in(VM)] * 2,
        out_shape=[
            shape((parents, len(zone(parents)), 2, samples), F32),
            shape((near_count, boxes), jnp.int32),
        ],
        scratch_shapes=[
            SM(inter_list.shape, jnp.int32),
            SM(trans_id.shape, jnp.int32),
            VM(translators.shape, F32),
            DMA((4,)),
        ],
        compiler_params=PARAMS,
        cost_estimate=pl.CostEstimate(
            flops=0, bytes_accessed=2 * near_blocks.size, transcendentals=0
        ),
        name="prep",
    )(
        stay(inter_list),
        stay(trans_id),
        stay(neighbours.T),
        stay(translators),
        stay(near_blocks),
        x_rows,
    )

    to_across, parent_pat, place_onehot = pl.pallas_call(
        lambda *refs: up_kernel(
            *refs, pieces=nsamp, boxes=boxes, parents=parents, parts=parts
        ),
        in_specs=[whole_in(VM)] * (nsamp + 3),
        out_specs=[whole_in(VM)] * 3,
        out_shape=[
            shape((parent_rows + halo_rows * LANES // samples, samples)),
            shape((parent_rows + halo_rows * LANES // samples, samples)),
            shape((leaves, slots)),
        ],
        scratch_shapes=[
            VM((parts * slots, samples), F32),
            VM((samples // LANES, parent_rows, LANES), F32),
        ],
        compiler_params=PARAMS,
        name="up",
    )(*[messages[d] for d in order], interp, phases, near_list)

    across = lax.ppermute(
        to_across, "box", [(i, (i + (1 if i % 2 else -1)) % nbox) for i in range(nbox)]
    )
    beside = lax.ppermute(parent_pat, "box", [(i, i ^ 1) for i in range(nbox)])

    def near_half(late, args):
        return pl.pallas_call(
            lambda *refs: near_kernel(
                *refs,
                late=late,
                nsamp=nsamp,
                total=total,
                halo_rows=halo_rows,
                parent_rows=parent_rows,
            ),
            in_specs=[whole_in(VM)] * (3 + len(args)),
            out_specs=whole_in(VM),
            out_shape=shape((reach, parts, unknowns), F32),
            scratch_shapes=[
                VM((boxes + 2 * reach, parts, 2 * unknowns), F32),
                SM((near_count, boxes), jnp.int32),
                DMA((1,)),
            ],
            compiler_params=PARAMS,
            cost_estimate=pl.CostEstimate(
                flops=parts * near_blocks.size,
                bytes_accessed=near_blocks.size,
                transcendentals=0,
            ),
            name="near",
        )(near_list, x_rows, near_blocks, *args)

    near_early = near_half(False, [place_onehot, messages[1]])

    fields = pl.pallas_call(
        lambda *refs: down_kernel(
            *refs, pieces=nsamp, boxes=boxes, parents=parents, parts=parts
        ),
        in_specs=[whole_in(VM)] * 8,
        out_specs=[whole_in(VM)] * nsamp,
        out_shape=[shape((parts * boxes, LANES))] * nsamp,
        scratch_shapes=[
            VM((3 * parents, parts, samples), F32),
            VM((samples // LANES, parent_rows, LANES), F32),
            VM((parts * slots, samples), BF16),
        ],
        compiler_params=PARAMS,
        name="down",
    )(parent_pat, across, beside, dense, interp, phases, place_onehot, near_early)

    pieces = dict(zip(order, fields))
    partial = [pieces[0]] + [exchange(pieces[d], d) for d in reversed(range(1, nsamp))]

    near_late = near_half(True, [fields[0], across, beside, *far_messages])

    return pl.pallas_call(
        lambda *refs: final_kernel(*refs, pieces=nsamp),
        in_specs=[whole_in(VM)] * (nsamp + 3),
        out_specs=whole_in(VM),
        out_shape=shape(xvec.shape, F32),
        scratch_shapes=[VM((parts * boxes, LANES), F32)],
        compiler_params=PARAMS,
        name="final",
    )(*partial, near_early, near_late, place)


def solution(mesh):
    in_specs = (
        P(("box", "samp"), None, None, None),
        P(("box", "samp"), None, None, None, None),
        P(("box", "samp"), None),
        P(("box", "samp"), None, None, None),
        P(("box", "samp"), None, None, None),
        P(),
        P(),
        P(("box", "samp")),
        P(("box", "samp")),
        P(None, None, "samp"),
        P("box", None),
        P("box", None),
    )
    out_specs = P(("box", "samp"), None, None, None)
    return jax.shard_map(
        on_device, mesh=mesh, in_specs=in_specs, out_specs=out_specs, check_vma=False
    )
```

```python
import jax
import jax.numpy as jnp
from jax import lax
from jax.experimental import pallas as pl
from jax.experimental.pallas import tpu as pltpu
from jax.sharding import PartitionSpec as P

F32 = jnp.float32
BF16 = jnp.bfloat16
LANES = 128
CODE_ROWS = 8


def nt_dot(a, b):
    return lax.dot_general(a, b, (((1,), (1,)), ((), ())), preferred_element_type=F32)


def nn_dot(a, b):
    return lax.dot_general(a, b, (((1,), (0,)), ((), ())), preferred_element_type=F32)


def times_i(v):
    half = v.shape[0] // 2
    return jnp.concatenate([-v[half:], v[:half]], axis=0)


def widen(v):
    return jnp.concatenate([v, times_i(v)], axis=1)


def leaf_kernel(
    octant, parent, x_hbm, lift_hbm, mats_hbm, to_far, plain, x_beside, x_rows,
    x_ref, rows, lift, oct_s, par_s, sems, *, parents,
):
    boxes, halves, rhs, _ = x_ref.shape
    parts = halves * rhs
    reach = boxes // 2
    chunks = sems.shape[0] - 3
    per = boxes // chunks
    small = [
        pltpu.make_async_copy(x_hbm, x_ref, sems.at[chunks]),
        pltpu.make_async_copy(octant, oct_s, sems.at[chunks + 1]),
        pltpu.make_async_copy(parent, par_s, sems.at[chunks + 2]),
    ]
    big = [
        pltpu.make_async_copy(
            lift_hbm.at[pl.ds(i * per, per)], lift.at[pl.ds(i * per, per)], sems.at[i]
        )
        for i in range(chunks)
    ]
    for copy in small + big:
        copy.start()
    for copy in small:
        copy.wait()
    own = [
        jnp.concatenate([x_ref[n, 0].astype(F32), x_ref[n, 1].astype(F32)], axis=0)
        for n in range(boxes)
    ]
    lane = lax.rem(lax.broadcasted_iota(jnp.int32, (boxes, LANES), 1), boxes)
    codes = jnp.zeros((boxes, LANES), F32)
    for n in range(boxes):
        slot = (oct_s[n] * parents + lax.rem(par_s[n], parents)).astype(F32)
        codes = jnp.where(lane == n, slot, codes)
    codes = codes[:CODE_ROWS].astype(BF16)
    x_rows[...] = jnp.concatenate(own, axis=0).astype(BF16)
    first = jnp.concatenate(own[:reach], axis=0)
    last = jnp.concatenate(own[reach:], axis=0)
    odd = lax.rem(lax.axis_index("samp"), 2) == 1
    at = parts * boxes
    x_beside[...] = jnp.where(odd, first, last).astype(BF16)
    to_far[at + CODE_ROWS :] = jnp.where(odd, last, first).astype(BF16)
    for ref in (plain, to_far):
        ref[at : at + CODE_ROWS] = codes
    for n in range(boxes):
        if n % per == 0:
            big[n // per].wait()
        mat = jnp.concatenate([lift[n, 0], lift[n, 1]], axis=1)
        rows[pl.ds(n, parts, stride=boxes), :] = nt_dot(widen(own[n]).astype(BF16), mat)
    pattern = rows[...].astype(BF16)
    for ref in (plain, to_far):
        ref[:at] = pattern


def up_kernel(*refs, pieces, boxes, parents, parts):
    msgs = refs[:pieces]
    interp_ref, phase_ref, out_ref, out_copy, place_ref, raised, folded = refs[pieces:]
    forward = msgs[1]
    slots = 8 * parents
    samples = raised.shape[1]
    first = lax.axis_index("samp") * samples
    mine = interp_ref[pl.ds(pl.multiple_of(first, samples), samples)]
    per_tile = LANES // boxes
    at = parts * boxes
    tiles = []
    for t in range(0, pieces, per_tile):
        lane = lax.broadcasted_iota(jnp.int32, (CODE_ROWS, LANES), 1) // boxes
        code = msgs[t][at : at + CODE_ROWS].astype(F32)
        for d in range(1, min(per_tile, pieces - t)):
            code = jnp.where(lane == d, msgs[t + d][at : at + CODE_ROWS].astype(F32), code)
        code = jnp.concatenate([code] * (slots // CODE_ROWS), axis=0)
        want = lax.broadcasted_iota(jnp.int32, (slots, LANES), 0).astype(F32)
        width = min(per_tile, pieces - t) * boxes
        tiles.append(jnp.where(code == want, 1.0, 0.0)[:, :width])
    sorter = jnp.concatenate(tiles, axis=1)
    place_ref[...] = sorter.T.astype(BF16)
    sorter = sorter.astype(BF16)
    pats = jnp.concatenate(
        [
            jnp.concatenate([m[c * boxes : (c + 1) * boxes] for m in msgs], axis=0)
            for c in range(parts)
        ],
        axis=1,
    )
    ordered = nn_dot(sorter, pats).astype(BF16)
    for c in range(parts):
        raised[c * slots : (c + 1) * slots] = nt_dot(
            ordered[:, c * LANES : (c + 1) * LANES], mine
        )
    half = parts // 2
    for t in range(samples // LANES):
        lanes = slice(t * LANES, (t + 1) * LANES)
        here = pl.ds(pl.multiple_of(first + t * LANES, LANES), LANES)
        for r in range(half):
            re = im = None
            for o in range(8):
                ph_r = phase_ref[o, 0:1, here]
                ph_i = phase_ref[o, 1:2, here]
                base_r = r * slots + o * parents
                base_i = (half + r) * slots + o * parents
                xr = raised[base_r : base_r + parents, lanes]
                xi = raised[base_i : base_i + parents, lanes]
                dr = ph_r * xr - ph_i * xi
                di = ph_r * xi + ph_i * xr
                re = dr if re is None else re + dr
                im = di if im is None else im + di
            folded[t, r * parents : (r + 1) * parents] = re
            folded[t, (half + r) * parents : (half + r + 1) * parents] = im
        for p in range(0, parents, 2):
            both = jnp.concatenate(
                [folded[t, pl.ds(p + e, parts, stride=parents), :] for e in range(2)], axis=0
            )
            both = both.astype(BF16)
            for ref in (out_ref, out_copy):
                ref[p * parts : (p + 2) * parts, lanes] = both
        extra = out_ref.shape[0] - parents * parts
        start = forward.shape[0] - extra * (samples // LANES - t)
        for ref in (out_ref, out_copy):
            ref[parents * parts :, lanes] = forward[start : start + extra]


def zone(parents):
    return [d for d in range(-parents, parents + 1) if abs(d) >= 2]


def prep_kernel(
    inter, trans, neighbours, table_hbm, mats_hbm, after, dense, nbr, inter_s, trans_s, table, sems,
    *, parents, all_parents,
):
    copies = [
        pltpu.make_async_copy(inter, inter_s, sems.at[0]),
        pltpu.make_async_copy(trans, trans_s, sems.at[1]),
        pltpu.make_async_copy(table_hbm, table, sems.at[2]),
        pltpu.make_async_copy(neighbours, nbr, sems.at[3]),
    ]
    for copy in copies:
        copy.start()
    for copy in copies[:3]:
        copy.wait()
    if len(zone(parents)) > inter.shape[1]:
        dense[...] = jnp.zeros_like(dense)
    first = lax.axis_index("box") * parents

    def fill(p, carry):
        for k in range(inter.shape[1]):
            rel = lax.rem(inter_s[p, k] - first - p + parents + all_parents, all_parents)
            at = jnp.where(rel < parents, rel, rel - 3)
            dense[p, at] = table[trans_s[p, k]]
        return carry

    lax.fori_loop(0, parents, fill, 0)
    copies[3].wait()


def down_kernel(
    own, across, beside, dense, interp_ref, phase_ref, place_ref, after, *refs, pieces, boxes, parents, parts
):
    outs = refs[:pieces]
    window, incoming, shifted = refs[pieces:]
    samples = window.shape[2]
    first = lax.axis_index("samp") * samples
    mine = interp_ref[pl.ds(pl.multiple_of(first, samples), samples)]
    slots = 8 * parents
    half = parts // 2
    odd = lax.rem(lax.axis_index("box"), 2)
    rows = parents * parts
    window[parents : 2 * parents] = own[:rows].astype(F32).reshape(parents, parts, samples)
    window[pl.ds(2 * parents * odd, parents)] = (
        across[:rows].astype(F32).reshape(parents, parts, samples)
    )
    window[pl.ds(2 * parents * (1 - odd), parents)] = (
        beside[:rows].astype(F32).reshape(parents, parts, samples)
    )
    offsets = zone(parents)

    def one(p):
        for t in range(samples // LANES):
            lanes = slice(t * LANES, (t + 1) * LANES)
            acc_r = acc_i = None
            for i, d in enumerate(offsets):
                x = window[parents + p + d, :, lanes]
                yr = dense[p, i, 0:1, lanes] * x
                yi = dense[p, i, 1:2, lanes] * x
                acc_r = yr if acc_r is None else acc_r + yr
                acc_i = yi if acc_i is None else acc_i + yi
            got = (acc_r + times_i(acc_i)).astype(BF16).astype(F32)
            incoming[t, pl.ds(p * parts, parts), :] = got

    if parents <= 8:
        for p in range(parents):
            one(p)
    else:
        lax.fori_loop(0, parents, lambda p, c: (one(p), c)[1], 0)
    for t in range(samples // LANES):
        lanes = slice(t * LANES, (t + 1) * LANES)
        here = pl.ds(pl.multiple_of(first + t * LANES, LANES), LANES)
        for r in range(half):
            ir = incoming[t, pl.ds(r, parents, stride=parts), :]
            ii = incoming[t, pl.ds(half + r, parents, stride=parts), :]
            re, im = [], []
            for o in range(8):
                ph_r = phase_ref[o, 0:1, here]
                ph_i = phase_ref[o, 1:2, here]
                re.append(ph_r * ir - ph_i * ii)
                im.append(ph_r * ii + ph_i * ir)
            shifted[r * slots : (r + 1) * slots, lanes] = jnp.concatenate(re, axis=0).astype(BF16)
            shifted[(half + r) * slots : (half + r + 1) * slots, lanes] = jnp.concatenate(
                im, axis=0
            ).astype(BF16)
    field = nn_dot(shifted[...], mine).astype(BF16)
    spread = jnp.concatenate([field[c * slots : (c + 1) * slots] for c in range(parts)], axis=1)
    leaves = nn_dot(place_ref[...], spread).astype(BF16)
    for d in range(pieces):
        for c in range(parts):
            outs[d][c * boxes : (c + 1) * boxes] = leaves[
                d * boxes : (d + 1) * boxes, c * LANES : (c + 1) * LANES
            ]


def near_kernel(*refs, late, nsamp, total, halo_rows, parent_rows):
    neighbours, own, mats, after, *halos, out_ref, window, nbr, sems = refs
    if late:
        across, beside, *from_far = halos
    else:
        (from_beside,) = halos
    list_copy = pltpu.make_async_copy(neighbours, nbr, sems.at[0])
    list_copy.start()
    count, parts, unknowns = out_ref.shape
    boxes = own.shape[0] // parts
    near_count = mats.shape[1]
    samp = lax.axis_index("samp")
    box = lax.axis_index("box")
    odd = lax.rem(samp, 2)
    first = count * (odd if late else 1 - odd)

    def piece(ref):
        return ref[ref.shape[0] - halo_rows :].astype(F32)

    if late:
        def forwarded(ref):
            return jnp.concatenate(
                [
                    ref[parent_rows:, t * LANES : (t + 1) * LANES].astype(F32)
                    for t in range(ref.shape[1] // LANES)
                ],
                axis=0,
            )

        partner = samp ^ (samp - 1 + 2 * odd)
        halo = piece(from_far[0])
        for i in range(1, len(from_far)):
            halo = jnp.where(partner == (4 << i) - 1, piece(from_far[i]), halo)
        box_odd = lax.rem(box, 2) == 1
        from_left = samp == 0
        passed = jnp.where(box_odd == from_left, forwarded(beside), forwarded(across))
        halo = jnp.where(jnp.logical_or(from_left, samp == nsamp - 1), passed, halo)
    else:
        halo = piece(from_beside)
    at = jnp.where(first > 0, boxes + count, 0)
    for i in range(count):
        window[at + i] = widen(halo[i * parts : (i + 1) * parts])
    mine = own[...].astype(F32)
    for i in range(boxes):
        window[count + i] = widen(mine[i * parts : (i + 1) * parts])
    list_copy.wait()
    base = (box * nsamp + samp) * boxes
    for i in range(count):
        acc = None
        for k in range(near_count):
            j = lax.rem(nbr[k, first + i] - base + count + total, total)
            mat = jnp.concatenate([mats[first + i, k, 0], mats[first + i, k, 1]], axis=1)
            y = nt_dot(window[j].astype(BF16), mat)
            acc = y if acc is None else acc + y
        out_ref[i] = acc


def final_kernel(*refs, pieces):
    parts_in = refs[:pieces]
    near_early, near_late, mats, out_ref, field = refs[pieces:]
    boxes, halves, rhs = out_ref.shape[:3]
    parts = halves * rhs
    half = boxes // 2
    odd = lax.rem(lax.axis_index("samp"), 2) == 1
    total = parts_in[0][...].astype(F32)
    for m in parts_in[1:]:
        total += m[...].astype(F32)
    field[...] = total.astype(BF16).astype(F32)
    for n in range(boxes):
        v = field[pl.ds(n, parts, stride=boxes), :]
        wide = jnp.concatenate([v, times_i(v)], axis=1).astype(BF16)
        y = nt_dot(wide, jnp.concatenate([mats[n, 0], mats[n, 1]], axis=1))
        i = n % half
        y = y + jnp.where(odd == (n < half), near_early[i], near_late[i])
        out_ref[n, 0] = y[:rhs]
        out_ref[n, 1] = y[rhs:]


def whole_in(kind):
    return pl.BlockSpec(memory_space=kind)


VM = pltpu.VMEM
SM = pltpu.SMEM
HBM = pltpu.HBM
DMA = pltpu.SemaphoreType.DMA
PARAMS = pltpu.CompilerParams(vmem_limit_bytes=24 * 1024 * 1024)


def stay(x):
    return pltpu.with_memory_space_constraint(x, HBM)


def on_device(
    xvec,
    near_blocks,
    neighbours,
    lift,
    place,
    interp,
    phases,
    octant,
    leaf_parent_index,
    translators,
    inter_list,
    trans_id,
):
    boxes, halves, rhs, unknowns = xvec.shape
    parts = halves * rhs
    nsamp = lax.axis_size("samp")
    nbox = lax.axis_size("box")
    total = boxes * nsamp * nbox
    reach = boxes // 2
    parents = boxes * nsamp // 8
    all_parents = parents * nbox
    samples = interp.shape[0] // nsamp
    slots = 8 * parents
    leaves = boxes * nsamp
    near_count = near_blocks.shape[1]
    halo_rows = reach * parts
    parent_rows = parents * parts
    plain_rows = parts * boxes + CODE_ROWS

    def shape(dims, dtype=BF16):
        return jax.ShapeDtypeStruct(dims, dtype)

    lift_chunks = 4
    to_far, plain, x_beside, x_rows = pl.pallas_call(
        lambda *refs: leaf_kernel(*refs, parents=parents),
        in_specs=[whole_in(HBM)] * 5,
        out_specs=[whole_in(VM)] * 4,
        out_shape=[
            shape((plain_rows + halo_rows, LANES)),
            shape((plain_rows, LANES)),
            shape((halo_rows, LANES)),
            shape((boxes * parts, LANES)),
        ],
        scratch_shapes=[
            VM(xvec.shape, BF16),
            VM((parts * boxes, LANES), F32),
            VM(lift.shape, BF16),
            SM((boxes,), jnp.int32),
            SM((boxes,), jnp.int32),
            DMA((lift_chunks + 3,)),
        ],
        compiler_params=PARAMS,
        name="leaf",
    )(*[stay(a) for a in (octant, leaf_parent_index, xvec, lift, near_blocks)])

    def exchange(x, d):
        return lax.ppermute(x, "samp", [(i, i ^ d) for i in range(nsamp)])

    order = [0, nsamp - 1, *range(1, nsamp - 1)]
    far = [(4 << i) - 1 for i in range(nsamp.bit_length() - 2)]
    messages = {0: plain}
    for d in order[1:]:
        messages[d] = exchange(to_far if d in far else plain, d)
    far_messages = [messages[d] for d in far]
    halo_beside = exchange(x_beside, 1)

    to_across, parent_pat, place_onehot = pl.pallas_call(
        lambda *refs: up_kernel(
            *refs, pieces=nsamp, boxes=boxes, parents=parents, parts=parts
        ),
        in_specs=[whole_in(VM)] * (nsamp + 2),
        out_specs=[whole_in(VM)] * 3,
        out_shape=[
            shape((parent_rows + halo_rows * LANES // samples, samples)),
            shape((parent_rows + halo_rows * LANES // samples, samples)),
            shape((leaves, slots)),
        ],
        scratch_shapes=[
            VM((parts * slots, samples), F32),
            VM((samples // LANES, parent_rows, LANES), F32),
        ],
        compiler_params=PARAMS,
        name="up",
    )(*[messages[d] for d in order], interp, phases)

    across = lax.ppermute(
        to_across, "box", [(i, (i + (1 if i % 2 else -1)) % nbox) for i in range(nbox)]
    )
    beside = lax.ppermute(parent_pat, "box", [(i, i ^ 1) for i in range(nbox)])

    dense, near_list = pl.pallas_call(
        lambda *refs: prep_kernel(*refs, parents=parents, all_parents=all_parents),
        in_specs=[whole_in(HBM)] * 5 + [whole_in(VM)],
        out_specs=[whole_in(VM)] * 2,
        out_shape=[
            shape((parents, len(zone(parents)), 2, samples), F32),
            shape((near_count, boxes), jnp.int32),
        ],
        scratch_shapes=[
            SM(inter_list.shape, jnp.int32),
            SM(trans_id.shape, jnp.int32),
            VM(translators.shape, F32),
            DMA((4,)),
        ],
        compiler_params=PARAMS,
        cost_estimate=pl.CostEstimate(
            flops=0, bytes_accessed=2 * near_blocks.size, transcendentals=0
        ),
        name="prep",
    )(
        stay(inter_list),
        stay(trans_id),
        stay(neighbours.T),
        stay(translators),
        stay(near_blocks),
        place_onehot,
    )

    def near_half(late, args):
        return pl.pallas_call(
            lambda *refs: near_kernel(
                *refs,
                late=late,
                nsamp=nsamp,
                total=total,
                halo_rows=halo_rows,
                parent_rows=parent_rows,
            ),
            in_specs=[whole_in(VM)] * (3 + len(args)),
            out_specs=whole_in(VM),
            out_shape=shape((reach, parts, unknowns), F32),
            scratch_shapes=[
                VM((boxes + 2 * reach, parts, 2 * unknowns), F32),
                SM((near_count, boxes), jnp.int32),
                DMA((1,)),
            ],
            compiler_params=PARAMS,
            cost_estimate=pl.CostEstimate(
                flops=parts * near_blocks.size,
                bytes_accessed=near_blocks.size,
                transcendentals=0,
            ),
            name="near",
        )(near_list, x_rows, near_blocks, *args)

    near_early = near_half(False, [place_onehot, halo_beside])

    fields = pl.pallas_call(
        lambda *refs: down_kernel(
            *refs, pieces=nsamp, boxes=boxes, parents=parents, parts=parts
        ),
        in_specs=[whole_in(VM)] * 8,
        out_specs=[whole_in(VM)] * nsamp,
        out_shape=[shape((parts * boxes, LANES))] * nsamp,
        scratch_shapes=[
            VM((3 * parents, parts, samples), F32),
            VM((samples // LANES, parent_rows, LANES), F32),
            VM((parts * slots, samples), BF16),
        ],
        compiler_params=PARAMS,
        name="down",
    )(parent_pat, across, beside, dense, interp, phases, place_onehot, near_early)

    pieces = dict(zip(order, fields))
    partial = [pieces[0]] + [exchange(pieces[d], d) for d in reversed(range(1, nsamp))]

    near_late = near_half(True, [fields[0], across, beside, *far_messages])

    return pl.pallas_call(
        lambda *refs: final_kernel(*refs, pieces=nsamp),
        in_specs=[whole_in(VM)] * (nsamp + 3),
        out_specs=whole_in(VM),
        out_shape=shape(xvec.shape, F32),
        scratch_shapes=[VM((parts * boxes, LANES), F32)],
        compiler_params=PARAMS,
        name="final",
    )(*partial, near_early, near_late, place)


def solution(mesh):
    in_specs = (
        P(("box", "samp"), None, None, None),
        P(("box", "samp"), None, None, None, None),
        P(("box", "samp"), None),
        P(("box", "samp"), None, None, None),
        P(("box", "samp"), None, None, None),
        P(),
        P(),
        P(("box", "samp")),
        P(("box", "samp")),
        P(None, None, "samp"),
        P("box", None),
        P("box", None),
    )
    out_specs = P(("box", "samp"), None, None, None)
    return jax.shard_map(
        on_device, mesh=mesh, in_specs=in_specs, out_specs=out_specs, check_vma=False
    )
```

```python
import jax
import jax.numpy as jnp
from jax import lax
from jax.experimental import pallas as pl
from jax.experimental.pallas import tpu as pltpu
from jax.sharding import PartitionSpec as P

F32 = jnp.float32
BF16 = jnp.bfloat16
LANES = 128
CODE_ROWS = 8


def nt_dot(a, b):
    return lax.dot_general(a, b, (((1,), (1,)), ((), ())), preferred_element_type=F32)


def nn_dot(a, b):
    return lax.dot_general(a, b, (((1,), (0,)), ((), ())), preferred_element_type=F32)


def times_i(v):
    half = v.shape[0] // 2
    return jnp.concatenate([-v[half:], v[:half]], axis=0)


def widen(v):
    return jnp.concatenate([v, times_i(v)], axis=1)


def leaf_kernel(
    octant, parent, x_hbm, lift_hbm, to_far, plain, to_beside, x_rows,
    x_ref, rows, lift, oct_s, par_s, sems, *, parents,
):
    boxes, halves, rhs, _ = x_ref.shape
    parts = halves * rhs
    reach = boxes // 2
    chunks = sems.shape[0] - 3
    per = boxes // chunks
    small = [
        pltpu.make_async_copy(x_hbm, x_ref, sems.at[chunks]),
        pltpu.make_async_copy(octant, oct_s, sems.at[chunks + 1]),
        pltpu.make_async_copy(parent, par_s, sems.at[chunks + 2]),
    ]
    big = [
        pltpu.make_async_copy(
            lift_hbm.at[pl.ds(i * per, per)], lift.at[pl.ds(i * per, per)], sems.at[i]
        )
        for i in range(chunks)
    ]
    for copy in small + big:
        copy.start()
    for copy in small:
        copy.wait()
    own = [
        jnp.concatenate([x_ref[n, 0].astype(F32), x_ref[n, 1].astype(F32)], axis=0)
        for n in range(boxes)
    ]
    lane = lax.rem(lax.broadcasted_iota(jnp.int32, (boxes, LANES), 1), boxes)
    codes = jnp.zeros((boxes, LANES), F32)
    for n in range(boxes):
        slot = (oct_s[n] * parents + lax.rem(par_s[n], parents)).astype(F32)
        codes = jnp.where(lane == n, slot, codes)
    codes = codes[:CODE_ROWS].astype(BF16)
    x_rows[...] = jnp.concatenate(own, axis=0).astype(BF16)
    first = jnp.concatenate(own[:reach], axis=0)
    last = jnp.concatenate(own[reach:], axis=0)
    odd = lax.rem(lax.axis_index("samp"), 2) == 1
    at = parts * boxes
    to_beside[at + CODE_ROWS :] = jnp.where(odd, first, last).astype(BF16)
    to_far[at + CODE_ROWS :] = jnp.where(odd, last, first).astype(BF16)
    for ref in (plain, to_beside, to_far):
        ref[at : at + CODE_ROWS] = codes
    for n in range(boxes):
        if n % per == 0:
            big[n // per].wait()
        mat = jnp.concatenate([lift[n, 0], lift[n, 1]], axis=1)
        rows[pl.ds(n, parts, stride=boxes), :] = nt_dot(widen(own[n]).astype(BF16), mat)
    pattern = rows[...].astype(BF16)
    for ref in (plain, to_beside, to_far):
        ref[:at] = pattern


def up_kernel(*refs, pieces, boxes, parents, parts):
    msgs = refs[:pieces]
    interp_ref, phase_ref, after, cross_a, cross_b, side_a, side_b, out_ref, place_ref, raised, folded = refs[pieces:]
    forward = msgs[1]
    slots = 8 * parents
    samples = raised.shape[1]
    first = lax.axis_index("samp") * samples
    mine = interp_ref[pl.ds(pl.multiple_of(first, samples), samples)]
    per_tile = LANES // boxes
    code_at = parts * boxes
    tiles = []
    for t in range(0, pieces, per_tile):
        lane = lax.broadcasted_iota(jnp.int32, (CODE_ROWS, LANES), 1) // boxes
        code = msgs[t][code_at : code_at + CODE_ROWS].astype(F32)
        for d in range(1, min(per_tile, pieces - t)):
            code = jnp.where(lane == d, msgs[t + d][code_at : code_at + CODE_ROWS].astype(F32), code)
        code = jnp.concatenate([code] * (slots // CODE_ROWS), axis=0)
        want = lax.broadcasted_iota(jnp.int32, (slots, LANES), 0).astype(F32)
        width = min(per_tile, pieces - t) * boxes
        tiles.append(jnp.where(code == want, 1.0, 0.0)[:, :width])
    sorter = jnp.concatenate(tiles, axis=1)
    place_ref[...] = sorter.T.astype(BF16)
    sorter = sorter.astype(BF16)
    pats = jnp.concatenate(
        [
            jnp.concatenate([m[c * boxes : (c + 1) * boxes] for m in msgs], axis=0)
            for c in range(parts)
        ],
        axis=1,
    )
    ordered = nn_dot(sorter, pats).astype(BF16)
    for c in range(parts):
        raised[c * slots : (c + 1) * slots] = nt_dot(
            ordered[:, c * LANES : (c + 1) * LANES], mine
        )
    half = parts // 2
    for t in range(samples // LANES):
        lanes = slice(t * LANES, (t + 1) * LANES)
        here = pl.ds(pl.multiple_of(first + t * LANES, LANES), LANES)
        for r in range(half):
            re = im = None
            for o in range(8):
                ph_r = phase_ref[o, 0:1, here]
                ph_i = phase_ref[o, 1:2, here]
                base_r = r * slots + o * parents
                base_i = (half + r) * slots + o * parents
                xr = raised[base_r : base_r + parents, lanes]
                xi = raised[base_i : base_i + parents, lanes]
                dr = ph_r * xr - ph_i * xi
                di = ph_r * xi + ph_i * xr
                re = dr if re is None else re + dr
                im = di if im is None else im + di
            folded[t, r * parents : (r + 1) * parents] = re
            folded[t, (half + r) * parents : (half + r + 1) * parents] = im
        for p in range(0, parents, 2):
            both = jnp.concatenate(
                [folded[t, pl.ds(p + e, parts, stride=parents), :] for e in range(2)], axis=0
            )
            both = both.astype(BF16)
            at = p * parts
            out_ref[at : at + 2 * parts, lanes] = both
            split = parents * parts // 2
            both_refs, at = ((cross_a, side_a), at) if at < split else ((cross_b, side_b), at - split)
            for ref in both_refs:
                ref[at : at + 2 * parts, lanes] = both
        extra = cross_a.shape[0] - parents * parts // 2
        start = forward.shape[0] - extra * (samples // LANES - t)
        for ref in (cross_a, cross_b, side_a, side_b):
            ref[ref.shape[0] - extra :, lanes] = forward[start : start + extra]


def zone(parents):
    return [d for d in range(-parents, parents + 1) if abs(d) >= 2]


def prep_kernel(
    inter, trans, neighbours, table_hbm, mats_hbm, after, dense, nbr, inter_s, trans_s, table, sems,
    *, parents, all_parents,
):
    copies = [
        pltpu.make_async_copy(inter, inter_s, sems.at[0]),
        pltpu.make_async_copy(trans, trans_s, sems.at[1]),
        pltpu.make_async_copy(table_hbm, table, sems.at[2]),
        pltpu.make_async_copy(neighbours, nbr, sems.at[3]),
    ]
    for copy in copies:
        copy.start()
    for copy in copies[:3]:
        copy.wait()
    if len(zone(parents)) > inter.shape[1]:
        dense[...] = jnp.zeros_like(dense)
    first = lax.axis_index("box") * parents

    def fill(p, carry):
        for k in range(inter.shape[1]):
            rel = lax.rem(inter_s[p, k] - first - p + parents + all_parents, all_parents)
            at = jnp.where(rel < parents, rel, rel - 3)
            dense[p, at] = table[trans_s[p, k]]
        return carry

    lax.fori_loop(0, parents, fill, 0)
    copies[3].wait()


def down_kernel(
    own, across_a, across_b, beside_a, beside_b, dense, interp_ref, phase_ref, place_ref, after, *refs, pieces, boxes, parents, parts
):
    outs = refs[:pieces]
    window, incoming, shifted = refs[pieces:]
    samples = window.shape[2]
    first = lax.axis_index("samp") * samples
    mine = interp_ref[pl.ds(pl.multiple_of(first, samples), samples)]
    slots = 8 * parents
    half = parts // 2
    odd = lax.rem(lax.axis_index("box"), 2)
    rows = parents * parts
    window[parents : 2 * parents] = own[:rows].astype(F32).reshape(parents, parts, samples)
    some = parents // 2
    for near_pair, side in (((across_a, across_b), odd), ((beside_a, beside_b), 1 - odd)):
        for i, ref in enumerate(near_pair):
            window[pl.ds(2 * parents * side + i * some, some)] = (
                ref[: some * parts].astype(F32).reshape(some, parts, samples)
            )
    offsets = zone(parents)

    def one(p):
        for t in range(samples // LANES):
            lanes = slice(t * LANES, (t + 1) * LANES)
            acc_r = acc_i = None
            for i, d in enumerate(offsets):
                x = window[parents + p + d, :, lanes]
                yr = dense[p, i, 0:1, lanes] * x
                yi = dense[p, i, 1:2, lanes] * x
                acc_r = yr if acc_r is None else acc_r + yr
                acc_i = yi if acc_i is None else acc_i + yi
            got = (acc_r + times_i(acc_i)).astype(BF16).astype(F32)
            incoming[t, pl.ds(p * parts, parts), :] = got

    if parents <= 8:
        for p in range(parents):
            one(p)
    else:
        lax.fori_loop(0, parents, lambda p, c: (one(p), c)[1], 0)
    for t in range(samples // LANES):
        lanes = slice(t * LANES, (t + 1) * LANES)
        here = pl.ds(pl.multiple_of(first + t * LANES, LANES), LANES)
        for r in range(half):
            ir = incoming[t, pl.ds(r, parents, stride=parts), :]
            ii = incoming[t, pl.ds(half + r, parents, stride=parts), :]
            re, im = [], []
            for o in range(8):
                ph_r = phase_ref[o, 0:1, here]
                ph_i = phase_ref[o, 1:2, here]
                re.append(ph_r * ir - ph_i * ii)
                im.append(ph_r * ii + ph_i * ir)
            shifted[r * slots : (r + 1) * slots, lanes] = jnp.concatenate(re, axis=0).astype(BF16)
            shifted[(half + r) * slots : (half + r + 1) * slots, lanes] = jnp.concatenate(
                im, axis=0
            ).astype(BF16)
    field = nn_dot(shifted[...], mine).astype(BF16)
    spread = jnp.concatenate([field[c * slots : (c + 1) * slots] for c in range(parts)], axis=1)
    leaves = nn_dot(place_ref[...], spread).astype(BF16)
    for d in range(pieces):
        for c in range(parts):
            outs[d][c * boxes : (c + 1) * boxes] = leaves[
                d * boxes : (d + 1) * boxes, c * LANES : (c + 1) * LANES
            ]


def near_kernel(*refs, late, nsamp, total, halo_rows, extra_rows):
    neighbours, own, mats, after, *halos, out_ref, window, nbr, sems = refs
    if late:
        across, beside, *from_far = halos
    else:
        (from_beside,) = halos
    list_copy = pltpu.make_async_copy(neighbours, nbr, sems.at[0])
    list_copy.start()
    count, parts, unknowns = out_ref.shape
    boxes = own.shape[0] // parts
    near_count = mats.shape[1]
    samp = lax.axis_index("samp")
    box = lax.axis_index("box")
    odd = lax.rem(samp, 2)
    first = count * (odd if late else 1 - odd)

    def piece(ref):
        return ref[ref.shape[0] - halo_rows :].astype(F32)

    if late:
        def forwarded(ref):
            return jnp.concatenate(
                [
                    ref[ref.shape[0] - extra_rows :, t * LANES : (t + 1) * LANES].astype(F32)
                    for t in range(ref.shape[1] // LANES)
                ],
                axis=0,
            )

        partner = samp ^ (samp - 1 + 2 * odd)
        halo = piece(from_far[0])
        for i in range(1, len(from_far)):
            halo = jnp.where(partner == (4 << i) - 1, piece(from_far[i]), halo)
        box_odd = lax.rem(box, 2) == 1
        from_left = samp == 0
        passed = jnp.where(box_odd == from_left, forwarded(beside), forwarded(across))
        halo = jnp.where(jnp.logical_or(from_left, samp == nsamp - 1), passed, halo)
    else:
        halo = piece(from_beside)
    at = jnp.where(first > 0, boxes + count, 0)
    for i in range(count):
        window[at + i] = widen(halo[i * parts : (i + 1) * parts])
    mine = own[...].astype(F32)
    for i in range(boxes):
        window[count + i] = widen(mine[i * parts : (i + 1) * parts])
    list_copy.wait()
    base = (box * nsamp + samp) * boxes
    for i in range(count):
        acc = None
        for k in range(near_count):
            j = lax.rem(nbr[k, first + i] - base + count + total, total)
            mat = jnp.concatenate([mats[first + i, k, 0], mats[first + i, k, 1]], axis=1)
            y = nt_dot(window[j].astype(BF16), mat)
            acc = y if acc is None else acc + y
        out_ref[i] = acc


def final_kernel(*refs, pieces):
    parts_in = refs[:pieces]
    near_early, near_late, mats, out_hbm, field, out, sems = refs[pieces:]
    boxes, halves, rhs = out.shape[:3]
    parts = halves * rhs
    half = boxes // 2
    odd = lax.rem(lax.axis_index("samp"), 2) == 1
    total = parts_in[0][...].astype(F32)
    for m in parts_in[1:]:
        total += m[...].astype(F32)
    field[...] = total.astype(BF16).astype(F32)
    copies = [
        pltpu.make_async_copy(
            out.at[pl.ds(i * half, half)], out_hbm.at[pl.ds(i * half, half)], sems.at[i]
        )
        for i in range(2)
    ]
    for n in range(boxes):
        v = field[pl.ds(n, parts, stride=boxes), :]
        wide = jnp.concatenate([v, times_i(v)], axis=1).astype(BF16)
        y = nt_dot(wide, jnp.concatenate([mats[n, 0], mats[n, 1]], axis=1))
        i = n % half
        y = y + jnp.where(odd == (n < half), near_early[i], near_late[i])
        out[n, 0] = y[:rhs]
        out[n, 1] = y[rhs:]
        if i == half - 1:
            copies[n // half].start()
    for copy in copies:
        copy.wait()


def whole_in(kind):
    return pl.BlockSpec(memory_space=kind)


VM = pltpu.VMEM
SM = pltpu.SMEM
HBM = pltpu.HBM
DMA = pltpu.SemaphoreType.DMA
PARAMS = pltpu.CompilerParams(vmem_limit_bytes=24 * 1024 * 1024)


def stay(x):
    return pltpu.with_memory_space_constraint(x, HBM)


def on_device(
    xvec,
    near_blocks,
    neighbours,
    lift,
    place,
    interp,
    phases,
    octant,
    leaf_parent_index,
    translators,
    inter_list,
    trans_id,
):
    boxes, halves, rhs, unknowns = xvec.shape
    parts = halves * rhs
    nsamp = lax.axis_size("samp")
    nbox = lax.axis_size("box")
    total = boxes * nsamp * nbox
    reach = boxes // 2
    parents = boxes * nsamp // 8
    all_parents = parents * nbox
    samples = interp.shape[0] // nsamp
    slots = 8 * parents
    leaves = boxes * nsamp
    near_count = near_blocks.shape[1]
    halo_rows = reach * parts
    parent_rows = parents * parts
    plain_rows = parts * boxes + CODE_ROWS

    def shape(dims, dtype=BF16):
        return jax.ShapeDtypeStruct(dims, dtype)

    lift_chunks = 4
    to_far, plain, to_beside, x_rows = pl.pallas_call(
        lambda *refs: leaf_kernel(*refs, parents=parents),
        in_specs=[whole_in(HBM)] * 4,
        out_specs=[whole_in(VM)] * 4,
        out_shape=[
            shape((plain_rows + halo_rows, LANES)),
            shape((plain_rows, LANES)),
            shape((plain_rows + halo_rows, LANES)),
            shape((boxes * parts, LANES)),
        ],
        scratch_shapes=[
            VM(xvec.shape, BF16),
            VM((parts * boxes, LANES), F32),
            VM(lift.shape, BF16),
            SM((boxes,), jnp.int32),
            SM((boxes,), jnp.int32),
            DMA((lift_chunks + 3,)),
        ],
        compiler_params=PARAMS,
        name="leaf",
    )(*[stay(a) for a in (octant, leaf_parent_index, xvec, lift)])

    def exchange(x, d):
        return lax.ppermute(x, "samp", [(i, i ^ d) for i in range(nsamp)])

    order = [0, nsamp - 1, *range(1, nsamp - 1)]
    far = [(4 << i) - 1 for i in range(nsamp.bit_length() - 2)]
    messages = {0: plain}
    for d in order[1:]:
        messages[d] = exchange(to_beside if d == 1 else to_far if d in far else plain, d)
    far_messages = [messages[d] for d in far]

    dense, near_list = pl.pallas_call(
        lambda *refs: prep_kernel(*refs, parents=parents, all_parents=all_parents),
        in_specs=[whole_in(HBM)] * 5 + [whole_in(VM)],
        out_specs=[whole_in(VM)] * 2,
        out_shape=[
            shape((parents, len(zone(parents)), 2, samples), F32),
            shape((near_count, boxes), jnp.int32),
        ],
        scratch_shapes=[
            SM(inter_list.shape, jnp.int32),
            SM(trans_id.shape, jnp.int32),
            VM(translators.shape, F32),
            DMA((4,)),
        ],
        compiler_params=PARAMS,
        cost_estimate=pl.CostEstimate(
            flops=0, bytes_accessed=2 * near_blocks.size, transcendentals=0
        ),
        name="prep",
    )(
        stay(inter_list),
        stay(trans_id),
        stay(neighbours.T),
        stay(translators),
        stay(near_blocks),
        x_rows,
    )

    half_rows = parent_rows // 2
    extra_rows = halo_rows * LANES // samples
    cross_a, cross_b, side_a, side_b, parent_pat, place_onehot = pl.pallas_call(
        lambda *refs: up_kernel(
            *refs, pieces=nsamp, boxes=boxes, parents=parents, parts=parts
        ),
        in_specs=[whole_in(VM)] * (nsamp + 3),
        out_specs=[whole_in(VM)] * 6,
        out_shape=[
            shape((half_rows + extra_rows, samples)),
            shape((half_rows + extra_rows, samples)),
            shape((half_rows + extra_rows, samples)),
            shape((half_rows + extra_rows, samples)),
            shape((parent_rows, samples)),
            shape((leaves, slots)),
        ],
        scratch_shapes=[
            VM((parts * slots, samples), F32),
            VM((samples // LANES, parent_rows, LANES), F32),
        ],
        compiler_params=PARAMS,
        name="up",
    )(*[messages[d] for d in order], interp, phases, near_list)

    cross = [(i, (i + (1 if i % 2 else -1)) % nbox) for i in range(nbox)]
    across_a = lax.ppermute(cross_a, "box", cross)
    across_b = lax.ppermute(cross_b, "box", cross)
    pair = [(i, i ^ 1) for i in range(nbox)]
    beside_a = lax.ppermute(side_a, "box", pair)
    beside_b = lax.ppermute(side_b, "box", pair)

    def near_half(late, args):
        return pl.pallas_call(
            lambda *refs: near_kernel(
                *refs,
                late=late,
                nsamp=nsamp,
                total=total,
                halo_rows=halo_rows,
                extra_rows=extra_rows,
            ),
            in_specs=[whole_in(VM)] * (3 + len(args)),
            out_specs=whole_in(VM),
            out_shape=shape((reach, parts, unknowns), F32),
            scratch_shapes=[
                VM((boxes + 2 * reach, parts, 2 * unknowns), F32),
                SM((near_count, boxes), jnp.int32),
                DMA((1,)),
            ],
            compiler_params=PARAMS,
            cost_estimate=pl.CostEstimate(
                flops=parts * near_blocks.size,
                bytes_accessed=near_blocks.size,
                transcendentals=0,
            ),
            name="near",
        )(near_list, x_rows, near_blocks, *args)

    near_early = near_half(False, [place_onehot, messages[1]])

    fields = pl.pallas_call(
        lambda *refs: down_kernel(
            *refs, pieces=nsamp, boxes=boxes, parents=parents, parts=parts
        ),
        in_specs=[whole_in(VM)] * 10,
        out_specs=[whole_in(VM)] * nsamp,
        out_shape=[shape((parts * boxes, LANES))] * nsamp,
        scratch_shapes=[
            VM((3 * parents, parts, samples), F32),
            VM((samples // LANES, parent_rows, LANES), F32),
            VM((parts * slots, samples), BF16),
        ],
        compiler_params=PARAMS,
        name="down",
    )(parent_pat, across_a, across_b, beside_a, beside_b, dense, interp, phases, place_onehot, near_early)

    pieces = dict(zip(order, fields))
    partial = [pieces[0]] + [exchange(pieces[d], d) for d in reversed(range(1, nsamp))]

    near_late = near_half(True, [fields[0], across_b, beside_b, *far_messages])

    return pl.pallas_call(
        lambda *refs: final_kernel(*refs, pieces=nsamp),
        in_specs=[whole_in(VM)] * (nsamp + 3),
        out_specs=whole_in(HBM),
        out_shape=shape(xvec.shape, F32),
        scratch_shapes=[
            VM((parts * boxes, LANES), F32),
            VM(xvec.shape, F32),
            DMA((2,)),
        ],
        compiler_params=PARAMS,
        name="final",
    )(*partial, near_early, near_late, place)


def solution(mesh):
    in_specs = (
        P(("box", "samp"), None, None, None),
        P(("box", "samp"), None, None, None, None),
        P(("box", "samp"), None),
        P(("box", "samp"), None, None, None),
        P(("box", "samp"), None, None, None),
        P(),
        P(),
        P(("box", "samp")),
        P(("box", "samp")),
        P(None, None, "samp"),
        P("box", None),
        P("box", None),
    )
    out_specs = P(("box", "samp"), None, None, None)
    return jax.shard_map(
        on_device, mesh=mesh, in_specs=in_specs, out_specs=out_specs, check_vma=False
    )
```

```python
import jax
import jax.numpy as jnp
from jax import lax
from jax.experimental import pallas as pl
from jax.experimental.pallas import tpu as pltpu
from jax.sharding import PartitionSpec as P

F32 = jnp.float32
BF16 = jnp.bfloat16
LANES = 128
CODE_ROWS = 8


def nt_dot(a, b):
    return lax.dot_general(a, b, (((1,), (1,)), ((), ())), preferred_element_type=F32)


def nn_dot(a, b):
    return lax.dot_general(a, b, (((1,), (0,)), ((), ())), preferred_element_type=F32)


def times_i(v):
    half = v.shape[0] // 2
    return jnp.concatenate([-v[half:], v[:half]], axis=0)


def widen(v):
    return jnp.concatenate([v, times_i(v)], axis=1)


def leaf_kernel(
    octant, parent, x_hbm, lift_hbm, to_far, plain, to_beside, x_rows,
    x_ref, rows, lift, oct_s, par_s, sems, *, parents,
):
    boxes, halves, rhs, _ = x_ref.shape
    parts = halves * rhs
    reach = boxes // 2
    chunks = sems.shape[0] - 3
    per = boxes // chunks
    small = [
        pltpu.make_async_copy(x_hbm, x_ref, sems.at[chunks]),
        pltpu.make_async_copy(octant, oct_s, sems.at[chunks + 1]),
        pltpu.make_async_copy(parent, par_s, sems.at[chunks + 2]),
    ]
    big = [
        pltpu.make_async_copy(
            lift_hbm.at[pl.ds(i * per, per)], lift.at[pl.ds(i * per, per)], sems.at[i]
        )
        for i in range(chunks)
    ]
    for copy in small + big:
        copy.start()
    for copy in small:
        copy.wait()
    own = [
        jnp.concatenate([x_ref[n, 0].astype(F32), x_ref[n, 1].astype(F32)], axis=0)
        for n in range(boxes)
    ]
    lane = lax.rem(lax.broadcasted_iota(jnp.int32, (boxes, LANES), 1), boxes)
    codes = jnp.zeros((boxes, LANES), F32)
    for n in range(boxes):
        slot = (oct_s[n] * parents + lax.rem(par_s[n], parents)).astype(F32)
        codes = jnp.where(lane == n, slot, codes)
    codes = codes[:CODE_ROWS].astype(BF16)
    x_rows[...] = jnp.concatenate(own, axis=0).astype(BF16)
    first = jnp.concatenate(own[:reach], axis=0)
    last = jnp.concatenate(own[reach:], axis=0)
    odd = lax.rem(lax.axis_index("samp"), 2) == 1
    at = parts * boxes
    to_beside[at + CODE_ROWS :] = jnp.where(odd, first, last).astype(BF16)
    to_far[at + CODE_ROWS :] = jnp.where(odd, last, first).astype(BF16)
    for ref in (plain, to_beside, to_far):
        ref[at : at + CODE_ROWS] = codes
    for n in range(boxes):
        if n % per == 0:
            big[n // per].wait()
        mat = jnp.concatenate([lift[n, 0], lift[n, 1]], axis=1)
        rows[pl.ds(n, parts, stride=boxes), :] = nt_dot(widen(own[n]).astype(BF16), mat)
    pattern = rows[...].astype(BF16)
    for ref in (plain, to_beside, to_far):
        ref[:at] = pattern


def up_kernel(*refs, pieces, boxes, parents, parts):
    msgs = refs[:pieces]
    interp_ref, phase_ref, after, out_ref, out_copy, pass_a, pass_b, place_ref, raised, folded = refs[pieces:]
    forward = msgs[1]
    slots = 8 * parents
    samples = raised.shape[1]
    first = lax.axis_index("samp") * samples
    mine = interp_ref[pl.ds(pl.multiple_of(first, samples), samples)]
    per_tile = LANES // boxes
    at = parts * boxes
    tiles = []
    for t in range(0, pieces, per_tile):
        lane = lax.broadcasted_iota(jnp.int32, (CODE_ROWS, LANES), 1) // boxes
        code = msgs[t][at : at + CODE_ROWS].astype(F32)
        for d in range(1, min(per_tile, pieces - t)):
            code = jnp.where(lane == d, msgs[t + d][at : at + CODE_ROWS].astype(F32), code)
        code = jnp.concatenate([code] * (slots // CODE_ROWS), axis=0)
        want = lax.broadcasted_iota(jnp.int32, (slots, LANES), 0).astype(F32)
        width = min(per_tile, pieces - t) * boxes
        tiles.append(jnp.where(code == want, 1.0, 0.0)[:, :width])
    sorter = jnp.concatenate(tiles, axis=1)
    place_ref[...] = sorter.T.astype(BF16)
    sorter = sorter.astype(BF16)
    pats = jnp.concatenate(
        [
            jnp.concatenate([m[c * boxes : (c + 1) * boxes] for m in msgs], axis=0)
            for c in range(parts)
        ],
        axis=1,
    )
    ordered = nn_dot(sorter, pats).astype(BF16)
    for c in range(parts):
        raised[c * slots : (c + 1) * slots] = nt_dot(
            ordered[:, c * LANES : (c + 1) * LANES], mine
        )
    half = parts // 2
    for t in range(samples // LANES):
        lanes = slice(t * LANES, (t + 1) * LANES)
        here = pl.ds(pl.multiple_of(first + t * LANES, LANES), LANES)
        for r in range(half):
            re = im = None
            for o in range(8):
                ph_r = phase_ref[o, 0:1, here]
                ph_i = phase_ref[o, 1:2, here]
                base_r = r * slots + o * parents
                base_i = (half + r) * slots + o * parents
                xr = raised[base_r : base_r + parents, lanes]
                xi = raised[base_i : base_i + parents, lanes]
                dr = ph_r * xr - ph_i * xi
                di = ph_r * xi + ph_i * xr
                re = dr if re is None else re + dr
                im = di if im is None else im + di
            folded[t, r * parents : (r + 1) * parents] = re
            folded[t, (half + r) * parents : (half + r + 1) * parents] = im
        for p in range(0, parents, 2):
            both = jnp.concatenate(
                [folded[t, pl.ds(p + e, parts, stride=parents), :] for e in range(2)], axis=0
            )
            both = both.astype(BF16)
            for ref in (out_ref, out_copy):
                ref[p * parts : (p + 2) * parts, lanes] = both
    pass_a[...] = forward[forward.shape[0] - pass_a.shape[0] :]
    pass_b[...] = forward[forward.shape[0] - pass_b.shape[0] :]


def zone(parents):
    return [d for d in range(-parents, parents + 1) if abs(d) >= 2]


def prep_kernel(
    inter, trans, neighbours, table_hbm, mats_hbm, after, dense, nbr, inter_s, trans_s, table, sems,
    *, parents, all_parents,
):
    copies = [
        pltpu.make_async_copy(inter, inter_s, sems.at[0]),
        pltpu.make_async_copy(trans, trans_s, sems.at[1]),
        pltpu.make_async_copy(table_hbm, table, sems.at[2]),
        pltpu.make_async_copy(neighbours, nbr, sems.at[3]),
    ]
    for copy in copies:
        copy.start()
    for copy in copies[:3]:
        copy.wait()
    if len(zone(parents)) > inter.shape[1]:
        dense[...] = jnp.zeros_like(dense)
    first = lax.axis_index("box") * parents

    def fill(p, carry):
        for k in range(inter.shape[1]):
            rel = lax.rem(inter_s[p, k] - first - p + parents + all_parents, all_parents)
            at = jnp.where(rel < parents, rel, rel - 3)
            dense[p, at] = table[trans_s[p, k]]
        return carry

    lax.fori_loop(0, parents, fill, 0)
    copies[3].wait()


def down_kernel(
    own, across, beside, dense, interp_ref, phase_ref, place_ref, *refs, pieces, boxes, parents, parts
):
    outs = refs[3 : 3 + pieces]
    window, incoming, shifted = refs[3 + pieces :]
    samples = window.shape[2]
    first = lax.axis_index("samp") * samples
    mine = interp_ref[pl.ds(pl.multiple_of(first, samples), samples)]
    slots = 8 * parents
    half = parts // 2
    odd = lax.rem(lax.axis_index("box"), 2)
    rows = parents * parts
    window[parents : 2 * parents] = own[:rows].astype(F32).reshape(parents, parts, samples)
    window[pl.ds(2 * parents * odd, parents)] = (
        across[:rows].astype(F32).reshape(parents, parts, samples)
    )
    window[pl.ds(2 * parents * (1 - odd), parents)] = (
        beside[:rows].astype(F32).reshape(parents, parts, samples)
    )
    offsets = zone(parents)

    def one(p):
        for t in range(samples // LANES):
            lanes = slice(t * LANES, (t + 1) * LANES)
            acc_r = acc_i = None
            for i, d in enumerate(offsets):
                x = window[parents + p + d, :, lanes]
                yr = dense[p, i, 0:1, lanes] * x
                yi = dense[p, i, 1:2, lanes] * x
                acc_r = yr if acc_r is None else acc_r + yr
                acc_i = yi if acc_i is None else acc_i + yi
            got = (acc_r + times_i(acc_i)).astype(BF16).astype(F32)
            incoming[t, pl.ds(p * parts, parts), :] = got

    if parents <= 8:
        for p in range(parents):
            one(p)
    else:
        lax.fori_loop(0, parents, lambda p, c: (one(p), c)[1], 0)
    for t in range(samples // LANES):
        lanes = slice(t * LANES, (t + 1) * LANES)
        here = pl.ds(pl.multiple_of(first + t * LANES, LANES), LANES)
        for r in range(half):
            ir = incoming[t, pl.ds(r, parents, stride=parts), :]
            ii = incoming[t, pl.ds(half + r, parents, stride=parts), :]
            re, im = [], []
            for o in range(8):
                ph_r = phase_ref[o, 0:1, here]
                ph_i = phase_ref[o, 1:2, here]
                re.append(ph_r * ir - ph_i * ii)
                im.append(ph_r * ii + ph_i * ir)
            shifted[r * slots : (r + 1) * slots, lanes] = jnp.concatenate(re, axis=0).astype(BF16)
            shifted[(half + r) * slots : (half + r + 1) * slots, lanes] = jnp.concatenate(
                im, axis=0
            ).astype(BF16)
    field = nn_dot(shifted[...], mine).astype(BF16)
    spread = jnp.concatenate([field[c * slots : (c + 1) * slots] for c in range(parts)], axis=1)
    leaves = nn_dot(place_ref[...], spread).astype(BF16)
    for d in range(pieces):
        for c in range(parts):
            outs[d][c * boxes : (c + 1) * boxes] = leaves[
                d * boxes : (d + 1) * boxes, c * LANES : (c + 1) * LANES
            ]


def near_kernel(*refs, late, nsamp, total, halo_rows):
    neighbours, own, mats, after, *halos, out_ref, window, nbr, sems = refs
    if late:
        across, beside, *from_far = halos
    else:
        (from_beside,) = halos
    list_copy = pltpu.make_async_copy(neighbours, nbr, sems.at[0])
    list_copy.start()
    count, parts, unknowns = out_ref.shape
    boxes = own.shape[0] // parts
    near_count = mats.shape[1]
    samp = lax.axis_index("samp")
    box = lax.axis_index("box")
    odd = lax.rem(samp, 2)
    first = count * (odd if late else 1 - odd)

    def piece(ref):
        return ref[ref.shape[0] - halo_rows :].astype(F32)

    if late:
        partner = samp ^ (samp - 1 + 2 * odd)
        halo = piece(from_far[0])
        for i in range(1, len(from_far)):
            halo = jnp.where(partner == (4 << i) - 1, piece(from_far[i]), halo)
        box_odd = lax.rem(box, 2) == 1
        from_left = samp == 0
        passed = jnp.where(box_odd == from_left, piece(beside), piece(across))
        halo = jnp.where(jnp.logical_or(from_left, samp == nsamp - 1), passed, halo)
    else:
        halo = piece(from_beside)
    at = jnp.where(first > 0, boxes + count, 0)
    for i in range(count):
        window[at + i] = widen(halo[i * parts : (i + 1) * parts])
    mine = own[...].astype(F32)
    for i in range(boxes):
        window[count + i] = widen(mine[i * parts : (i + 1) * parts])
    list_copy.wait()
    base = (box * nsamp + samp) * boxes
    for i in range(count):
        acc = None
        for k in range(near_count):
            j = lax.rem(nbr[k, first + i] - base + count + total, total)
            mat = jnp.concatenate([mats[first + i, k, 0], mats[first + i, k, 1]], axis=1)
            y = nt_dot(window[j].astype(BF16), mat)
            acc = y if acc is None else acc + y
        out_ref[i] = acc


def final_kernel(*refs, pieces):
    parts_in = refs[:pieces]
    near_early, near_late, mats, out_ref, field = refs[pieces:]
    boxes, halves, rhs = out_ref.shape[:3]
    parts = halves * rhs
    half = boxes // 2
    odd = lax.rem(lax.axis_index("samp"), 2) == 1
    total = parts_in[0][...].astype(F32)
    for m in parts_in[1:]:
        total += m[...].astype(F32)
    field[...] = total.astype(BF16).astype(F32)
    for n in range(boxes):
        v = field[pl.ds(n, parts, stride=boxes), :]
        wide = jnp.concatenate([v, times_i(v)], axis=1).astype(BF16)
        y = nt_dot(wide, jnp.concatenate([mats[n, 0], mats[n, 1]], axis=1))
        i = n % half
        y = y + jnp.where(odd == (n < half), near_early[i], near_late[i])
        out_ref[n, 0] = y[:rhs]
        out_ref[n, 1] = y[rhs:]


def whole_in(kind):
    return pl.BlockSpec(memory_space=kind)


VM = pltpu.VMEM
SM = pltpu.SMEM
HBM = pltpu.HBM
DMA = pltpu.SemaphoreType.DMA
PARAMS = pltpu.CompilerParams(vmem_limit_bytes=24 * 1024 * 1024)


def stay(x):
    return pltpu.with_memory_space_constraint(x, HBM)


def on_device(
    xvec,
    near_blocks,
    neighbours,
    lift,
    place,
    interp,
    phases,
    octant,
    leaf_parent_index,
    translators,
    inter_list,
    trans_id,
):
    boxes, halves, rhs, unknowns = xvec.shape
    parts = halves * rhs
    nsamp = lax.axis_size("samp")
    nbox = lax.axis_size("box")
    total = boxes * nsamp * nbox
    reach = boxes // 2
    parents = boxes * nsamp // 8
    all_parents = parents * nbox
    samples = interp.shape[0] // nsamp
    slots = 8 * parents
    leaves = boxes * nsamp
    near_count = near_blocks.shape[1]
    halo_rows = reach * parts
    parent_rows = parents * parts
    plain_rows = parts * boxes + CODE_ROWS

    def shape(dims, dtype=BF16):
        return jax.ShapeDtypeStruct(dims, dtype)

    lift_chunks = 2
    to_far, plain, to_beside, x_rows = pl.pallas_call(
        lambda *refs: leaf_kernel(*refs, parents=parents),
        in_specs=[whole_in(HBM)] * 4,
        out_specs=[whole_in(VM)] * 4,
        out_shape=[
            shape((plain_rows + halo_rows, LANES)),
            shape((plain_rows, LANES)),
            shape((plain_rows + halo_rows, LANES)),
            shape((boxes * parts, LANES)),
        ],
        scratch_shapes=[
            VM(xvec.shape, BF16),
            VM((parts * boxes, LANES), F32),
            VM(lift.shape, BF16),
            SM((boxes,), jnp.int32),
            SM((boxes,), jnp.int32),
            DMA((lift_chunks + 3,)),
        ],
        compiler_params=PARAMS,
        name="leaf",
    )(*[stay(a) for a in (octant, leaf_parent_index, xvec, lift)])

    def exchange(x, d):
        return lax.ppermute(x, "samp", [(i, i ^ d) for i in range(nsamp)])

    order = [0, nsamp - 1, *range(1, nsamp - 1)]
    far = [(4 << i) - 1 for i in range(nsamp.bit_length() - 2)]
    messages = {0: plain}
    for d in order[1:]:
        messages[d] = exchange(to_beside if d == 1 else to_far if d in far else plain, d)
    far_messages = [messages[d] for d in far]

    dense, near_list = pl.pallas_call(
        lambda *refs: prep_kernel(*refs, parents=parents, all_parents=all_parents),
        in_specs=[whole_in(HBM)] * 5 + [whole_in(VM)],
        out_specs=[whole_in(VM)] * 2,
        out_shape=[
            shape((parents, len(zone(parents)), 2, samples), F32),
            shape((near_count, boxes), jnp.int32),
        ],
        scratch_shapes=[
            SM(inter_list.shape, jnp.int32),
            SM(trans_id.shape, jnp.int32),
            VM(translators.shape, F32),
            DMA((4,)),
        ],
        compiler_params=PARAMS,
        cost_estimate=pl.CostEstimate(
            flops=0, bytes_accessed=2 * near_blocks.size, transcendentals=0
        ),
        name="prep",
    )(
        stay(inter_list),
        stay(trans_id),
        stay(neighbours.T),
        stay(translators),
        stay(near_blocks),
        x_rows,
    )

    to_across, parent_pat, pass_a, pass_b, place_onehot = pl.pallas_call(
        lambda *refs: up_kernel(
            *refs, pieces=nsamp, boxes=boxes, parents=parents, parts=parts
        ),
        in_specs=[whole_in(VM)] * (nsamp + 3),
        out_specs=[whole_in(VM)] * 5,
        out_shape=[
            shape((parent_rows, samples)),
            shape((parent_rows, samples)),
            shape((halo_rows, LANES)),
            shape((halo_rows, LANES)),
            shape((leaves, slots)),
        ],
        scratch_shapes=[
            VM((parts * slots, samples), F32),
            VM((samples // LANES, parent_rows, LANES), F32),
        ],
        compiler_params=PARAMS,
        name="up",
    )(*[messages[d] for d in order], interp, phases, near_list)

    cross = [(i, (i + (1 if i % 2 else -1)) % nbox) for i in range(nbox)]
    pair = [(i, i ^ 1) for i in range(nbox)]
    across = lax.ppermute(to_across, "box", cross)
    beside = lax.ppermute(parent_pat, "box", pair)
    pass_across = lax.ppermute(pass_a, "box", cross)
    pass_beside = lax.ppermute(pass_b, "box", pair)

    def near_half(late, args):
        return pl.pallas_call(
            lambda *refs: near_kernel(
                *refs,
                late=late,
                nsamp=nsamp,
                total=total,
                halo_rows=halo_rows,
            ),
            in_specs=[whole_in(VM)] * (3 + len(args)),
            out_specs=whole_in(VM),
            out_shape=shape((reach, parts, unknowns), F32),
            scratch_shapes=[
                VM((boxes + 2 * reach, parts, 2 * unknowns), F32),
                SM((near_count, boxes), jnp.int32),
                DMA((1,)),
            ],
            compiler_params=PARAMS,
            cost_estimate=pl.CostEstimate(
                flops=parts * near_blocks.size,
                bytes_accessed=near_blocks.size,
                transcendentals=0,
            ),
            name="near",
        )(near_list, x_rows, near_blocks, *args)

    near_early = near_half(False, [place_onehot, messages[1]])

    fields = pl.pallas_call(
        lambda *refs: down_kernel(
            *refs, pieces=nsamp, boxes=boxes, parents=parents, parts=parts
        ),
        in_specs=[whole_in(VM)] * 10,
        out_specs=[whole_in(VM)] * nsamp,
        out_shape=[shape((parts * boxes, LANES))] * nsamp,
        scratch_shapes=[
            VM((3 * parents, parts, samples), F32),
            VM((samples // LANES, parent_rows, LANES), F32),
            VM((parts * slots, samples), BF16),
        ],
        compiler_params=PARAMS,
        name="down",
    )(parent_pat, across, beside, dense, interp, phases, place_onehot, near_early, pass_across, pass_beside)

    pieces = dict(zip(order, fields))
    partial = [pieces[0]] + [exchange(pieces[d], d) for d in reversed(range(1, nsamp))]

    near_late = near_half(True, [fields[0], pass_across, pass_beside, *far_messages])

    return pl.pallas_call(
        lambda *refs: final_kernel(*refs, pieces=nsamp),
        in_specs=[whole_in(VM)] * (nsamp + 3),
        out_specs=whole_in(VM),
        out_shape=shape(xvec.shape, F32),
        scratch_shapes=[VM((parts * boxes, LANES), F32)],
        compiler_params=PARAMS,
        name="final",
    )(*partial, near_early, near_late, place)


def solution(mesh):
    in_specs = (
        P(("box", "samp"), None, None, None),
        P(("box", "samp"), None, None, None, None),
        P(("box", "samp"), None),
        P(("box", "samp"), None, None, None),
        P(("box", "samp"), None, None, None),
        P(),
        P(),
        P(("box", "samp")),
        P(("box", "samp")),
        P(None, None, "samp"),
        P("box", None),
        P("box", None),
    )
    out_specs = P(("box", "samp"), None, None, None)
    return jax.shard_map(
        on_device, mesh=mesh, in_specs=in_specs, out_specs=out_specs, check_vma=False
    )
```

```python
import jax
import jax.numpy as jnp
from jax import lax
from jax.experimental import pallas as pl
from jax.experimental.pallas import tpu as pltpu
from jax.sharding import PartitionSpec as P

F32 = jnp.float32
BF16 = jnp.bfloat16
LANES = 128
CODE_ROWS = 8


def nt_dot(a, b):
    return lax.dot_general(a, b, (((1,), (1,)), ((), ())), preferred_element_type=F32)


def nn_dot(a, b):
    return lax.dot_general(a, b, (((1,), (0,)), ((), ())), preferred_element_type=F32)


def times_i(v):
    half = v.shape[0] // 2
    return jnp.concatenate([-v[half:], v[:half]], axis=0)


def widen(v):
    return jnp.concatenate([v, times_i(v)], axis=1)


def leaf_kernel(
    octant, parent, x_hbm, lift_hbm, to_far, plain, to_beside, x_rows,
    x_ref, rows, lift, oct_s, par_s, sems, *, parents,
):
    boxes, halves, rhs, _ = x_ref.shape
    parts = halves * rhs
    reach = boxes // 2
    chunks = sems.shape[0] - 3
    per = boxes // chunks
    small = [
        pltpu.make_async_copy(x_hbm, x_ref, sems.at[chunks]),
        pltpu.make_async_copy(octant, oct_s, sems.at[chunks + 1]),
        pltpu.make_async_copy(parent, par_s, sems.at[chunks + 2]),
    ]
    big = [
        pltpu.make_async_copy(
            lift_hbm.at[pl.ds(i * per, per)], lift.at[pl.ds(i * per, per)], sems.at[i]
        )
        for i in range(chunks)
    ]
    for copy in small + big:
        copy.start()
    for copy in small:
        copy.wait()
    own = [
        jnp.concatenate([x_ref[n, 0].astype(F32), x_ref[n, 1].astype(F32)], axis=0)
        for n in range(boxes)
    ]
    lane = lax.rem(lax.broadcasted_iota(jnp.int32, (boxes, LANES), 1), boxes)
    codes = jnp.zeros((boxes, LANES), F32)
    for n in range(boxes):
        slot = (oct_s[n] * parents + lax.rem(par_s[n], parents)).astype(F32)
        codes = jnp.where(lane == n, slot, codes)
    codes = codes[:CODE_ROWS].astype(BF16)
    x_rows[...] = jnp.concatenate(own, axis=0).astype(BF16)
    first = jnp.concatenate(own[:reach], axis=0)
    last = jnp.concatenate(own[reach:], axis=0)
    odd = lax.rem(lax.axis_index("samp"), 2) == 1
    at = parts * boxes
    to_beside[at + CODE_ROWS :] = jnp.where(odd, first, last).astype(BF16)
    to_far[at + CODE_ROWS :] = jnp.where(odd, last, first).astype(BF16)
    for ref in (plain, to_beside, to_far):
        ref[at : at + CODE_ROWS] = codes
    for n in range(boxes):
        if n % per == 0:
            big[n // per].wait()
        mat = jnp.concatenate([lift[n, 0], lift[n, 1]], axis=1)
        rows[pl.ds(n, parts, stride=boxes), :] = nt_dot(widen(own[n]).astype(BF16), mat)
    pattern = rows[...].astype(BF16)
    for ref in (plain, to_beside, to_far):
        ref[:at] = pattern


def up_kernel(*refs, pieces, boxes, parents, parts):
    msgs = refs[:pieces]
    interp_ref, phase_ref, after, out_ref, out_copy, place_ref, raised, folded = refs[pieces:]
    forward = msgs[1]
    slots = 8 * parents
    samples = raised.shape[1]
    first = lax.axis_index("samp") * samples
    mine = interp_ref[pl.ds(pl.multiple_of(first, samples), samples)]
    per_tile = LANES // boxes
    at = parts * boxes
    tiles = []
    for t in range(0, pieces, per_tile):
        lane = lax.broadcasted_iota(jnp.int32, (CODE_ROWS, LANES), 1) // boxes
        code = msgs[t][at : at + CODE_ROWS].astype(F32)
        for d in range(1, min(per_tile, pieces - t)):
            code = jnp.where(lane == d, msgs[t + d][at : at + CODE_ROWS].astype(F32), code)
        code = jnp.concatenate([code] * (slots // CODE_ROWS), axis=0)
        want = lax.broadcasted_iota(jnp.int32, (slots, LANES), 0).astype(F32)
        width = min(per_tile, pieces - t) * boxes
        tiles.append(jnp.where(code == want, 1.0, 0.0)[:, :width])
    sorter = jnp.concatenate(tiles, axis=1)
    place_ref[...] = sorter.T.astype(BF16)
    sorter = sorter.astype(BF16)
    pats = jnp.concatenate(
        [
            jnp.concatenate([m[c * boxes : (c + 1) * boxes] for m in msgs], axis=0)
            for c in range(parts)
        ],
        axis=1,
    )
    ordered = nn_dot(sorter, pats).astype(BF16)
    stacked = jnp.concatenate(
        [ordered[:, c * LANES : (c + 1) * LANES] for c in range(parts)], axis=0
    )
    raised[...] = nt_dot(stacked, mine)
    half = parts // 2
    for t in range(samples // LANES):
        lanes = slice(t * LANES, (t + 1) * LANES)
        here = pl.ds(pl.multiple_of(first + t * LANES, LANES), LANES)
        for r in range(half):
            re = im = None
            for o in range(8):
                ph_r = phase_ref[o, 0:1, here]
                ph_i = phase_ref[o, 1:2, here]
                base_r = r * slots + o * parents
                base_i = (half + r) * slots + o * parents
                xr = raised[base_r : base_r + parents, lanes]
                xi = raised[base_i : base_i + parents, lanes]
                dr = ph_r * xr - ph_i * xi
                di = ph_r * xi + ph_i * xr
                re = dr if re is None else re + dr
                im = di if im is None else im + di
            folded[t, r * parents : (r + 1) * parents] = re
            folded[t, (half + r) * parents : (half + r + 1) * parents] = im
        for p in range(0, parents, 2):
            both = jnp.concatenate(
                [folded[t, pl.ds(p + e, parts, stride=parents), :] for e in range(2)], axis=0
            )
            both = both.astype(BF16)
            for ref in (out_ref, out_copy):
                ref[p * parts : (p + 2) * parts, lanes] = both
        extra = out_ref.shape[0] - parents * parts
        start = forward.shape[0] - extra * (samples // LANES - t)
        for ref in (out_ref, out_copy):
            ref[parents * parts :, lanes] = forward[start : start + extra]


def zone(parents):
    return [d for d in range(-parents, parents + 1) if abs(d) >= 2]


def prep_kernel(
    inter, trans, neighbours, table_hbm, mats_hbm, after, dense, nbr, inter_s, trans_s, table, sems,
    *, parents, all_parents,
):
    copies = [
        pltpu.make_async_copy(inter, inter_s, sems.at[0]),
        pltpu.make_async_copy(trans, trans_s, sems.at[1]),
        pltpu.make_async_copy(table_hbm, table, sems.at[2]),
        pltpu.make_async_copy(neighbours, nbr, sems.at[3]),
    ]
    for copy in copies:
        copy.start()
    for copy in copies[:3]:
        copy.wait()
    if len(zone(parents)) > inter.shape[1]:
        dense[...] = jnp.zeros_like(dense)
    first = lax.axis_index("box") * parents

    def fill(p, carry):
        for k in range(inter.shape[1]):
            rel = lax.rem(inter_s[p, k] - first - p + parents + all_parents, all_parents)
            at = jnp.where(rel < parents, rel, rel - 3)
            dense[p, at] = table[trans_s[p, k]]
        return carry

    lax.fori_loop(0, parents, fill, 0)
    copies[3].wait()


def down_kernel(
    own, across, beside, dense, interp_ref, phase_ref, place_ref, after, *refs, pieces, boxes, parents, parts
):
    outs = refs[:pieces]
    window, incoming, shifted = refs[pieces:]
    samples = window.shape[2]
    first = lax.axis_index("samp") * samples
    mine = interp_ref[pl.ds(pl.multiple_of(first, samples), samples)]
    slots = 8 * parents
    half = parts // 2
    odd = lax.rem(lax.axis_index("box"), 2)
    rows = parents * parts
    window[parents : 2 * parents] = own[:rows].astype(F32).reshape(parents, parts, samples)
    window[pl.ds(2 * parents * odd, parents)] = (
        across[:rows].astype(F32).reshape(parents, parts, samples)
    )
    window[pl.ds(2 * parents * (1 - odd), parents)] = (
        beside[:rows].astype(F32).reshape(parents, parts, samples)
    )
    offsets = zone(parents)

    def one(p, t, source):
        lanes = slice(t * LANES, (t + 1) * LANES)
        acc_r = acc_i = None
        for i, d in enumerate(offsets):
            x = source(p + d)
            yr = dense[p, i, 0:1, lanes] * x
            yi = dense[p, i, 1:2, lanes] * x
            acc_r = yr if acc_r is None else acc_r + yr
            acc_i = yi if acc_i is None else acc_i + yi
        got = (acc_r + times_i(acc_i)).astype(BF16).astype(F32)
        incoming[t, pl.ds(p * parts, parts), :] = got

    for t in range(samples // LANES):
        lanes = slice(t * LANES, (t + 1) * LANES)
        if parents <= 8:
            held = [window[j, :, lanes] for j in range(3 * parents)]
            for p in range(parents):
                one(p, t, lambda j: held[parents + j])
        else:
            lax.fori_loop(
                0,
                parents,
                lambda p, c: (one(p, t, lambda j: window[parents + j, :, lanes]), c)[1],
                0,
            )
    for t in range(samples // LANES):
        lanes = slice(t * LANES, (t + 1) * LANES)
        here = pl.ds(pl.multiple_of(first + t * LANES, LANES), LANES)
        for r in range(half):
            re = im = None
            for o in range(8):
                ph_r = phase_ref[o, 0:1, here]
                ph_i = phase_ref[o, 1:2, here]
                base_r = r * slots + o * parents
                base_i = (half + r) * slots + o * parents
                xr = raised[base_r : base_r + parents, lanes]
                xi = raised[base_i : base_i + parents, lanes]
                dr = ph_r * xr - ph_i * xi
                di = ph_r * xi + ph_i * xr
                re = dr if re is None else re + dr
                im = di if im is None else im + di
            folded[t, r * parents : (r + 1) * parents] = re
            folded[t, (half + r) * parents : (half + r + 1) * parents] = im
        for p in range(0, parents, 2):
            both = jnp.concatenate(
                [folded[t, pl.ds(p + e, parts, stride=parents), :] for e in range(2)], axis=0
            )
            both = both.astype(BF16)
            for ref in (out_ref, out_copy):
                ref[p * parts : (p + 2) * parts, lanes] = both
        extra = out_ref.shape[0] - parents * parts
        start = forward.shape[0] - extra * (samples // LANES - t)
        for ref in (out_ref, out_copy):
            ref[parents * parts :, lanes] = forward[start : start + extra]


def zone(parents):
    return [d for d in range(-parents, parents + 1) if abs(d) >= 2]


def prep_kernel(
    inter, trans, neighbours, table_hbm, mats_hbm, after, dense, nbr, inter_s, trans_s, table, sems,
    *, parents, all_parents,
):
    copies = [
        pltpu.make_async_copy(inter, inter_s, sems.at[0]),
        pltpu.make_async_copy(trans, trans_s, sems.at[1]),
        pltpu.make_async_copy(table_hbm, table, sems.at[2]),
        pltpu.make_async_copy(neighbours, nbr, sems.at[3]),
    ]
    for copy in copies:
        copy.start()
    for copy in copies[:3]:
        copy.wait()
    if len(zone(parents)) > inter.shape[1]:
        dense[...] = jnp.zeros_like(dense)
    first = lax.axis_index("box") * parents

    def fill(p, carry):
        for k in range(inter.shape[1]):
            rel = lax.rem(inter_s[p, k] - first - p + parents + all_parents, all_parents)
            at = jnp.where(rel < parents, rel, rel - 3)
            dense[p, at] = table[trans_s[p, k]]
        return carry

    lax.fori_loop(0, parents, fill, 0)
    copies[3].wait()


def down_kernel(
    own, across, beside, dense, interp_ref, phase_ref, place_ref, after, *refs, pieces, boxes, parents, parts
):
    outs = refs[:pieces]
    window, incoming, shifted = refs[pieces:]
    samples = window.shape[2]
    first = lax.axis_index("samp") * samples
    mine = interp_ref[pl.ds(pl.multiple_of(first, samples), samples)]
    slots = 8 * parents
    half = parts // 2
    odd = lax.rem(lax.axis_index("box"), 2)
    rows = parents * parts
    window[parents : 2 * parents] = own[:rows].astype(F32).reshape(parents, parts, samples)
    window[pl.ds(2 * parents * odd, parents)] = (
        across[:rows].astype(F32).reshape(parents, parts, samples)
    )
    window[pl.ds(2 * parents * (1 - odd), parents)] = (
        beside[:rows].astype(F32).reshape(parents, parts, samples)
    )
    offsets = zone(parents)

    def one(p):
        for t in range(samples // LANES):
            lanes = slice(t * LANES, (t + 1) * LANES)
            acc_r = acc_i = None
            for i, d in enumerate(offsets):
                x = window[parents + p + d, :, lanes]
                yr = dense[p, i, 0:1, lanes] * x
                yi = dense[p, i, 1:2, lanes] * x
                acc_r = yr if acc_r is None else acc_r + yr
                acc_i = yi if acc_i is None else acc_i + yi
            got = (acc_r + times_i(acc_i)).astype(BF16).astype(F32)
            incoming[t, pl.ds(p * parts, parts), :] = got

    if parents <= 8:
        for p in range(parents):
            one(p)
    else:
        lax.fori_loop(0, parents, lambda p, c: (one(p), c)[1], 0)
    for t in range(samples // LANES):
        lanes = slice(t * LANES, (t + 1) * LANES)
        here = pl.ds(pl.multiple_of(first + t * LANES, LANES), LANES)
        for r in range(half):
            ir = incoming[t, pl.ds(r, parents, stride=parts), :]
            ii = incoming[t, pl.ds(half + r, parents, stride=parts), :]
            re, im = [], []
            for o in range(8):
                ph_r = phase_ref[o, 0:1, here]
                ph_i = phase_ref[o, 1:2, here]
                re.append(ph_r * ir - ph_i * ii)
                im.append(ph_r * ii + ph_i * ir)
            shifted[r * slots : (r + 1) * slots, lanes] = jnp.concatenate(re, axis=0).astype(BF16)
            shifted[(half + r) * slots : (half + r + 1) * slots, lanes] = jnp.concatenate(
                im, axis=0
            ).astype(BF16)
    field = nn_dot(shifted[...], mine).astype(BF16)
    spread = jnp.concatenate([field[c * slots : (c + 1) * slots] for c in range(parts)], axis=1)
    leaves = nn_dot(place_ref[...], spread).astype(BF16)
    for d in range(pieces):
        for c in range(parts):
            outs[d][c * boxes : (c + 1) * boxes] = leaves[
                d * boxes : (d + 1) * boxes, c * LANES : (c + 1) * LANES
            ]


def near_kernel(*refs, late, nsamp, total, halo_rows, parent_rows):
    neighbours, own, mats, after, *halos, out_ref, window, nbr, sems = refs
    if late:
        across, beside, *from_far = halos
    else:
        (from_beside,) = halos
    list_copy = pltpu.make_async_copy(neighbours, nbr, sems.at[0])
    list_copy.start()
    count, parts, unknowns = out_ref.shape
    boxes = own.shape[0] // parts
    near_count = mats.shape[1]
    samp = lax.axis_index("samp")
    box = lax.axis_index("box")
    odd = lax.rem(samp, 2)
    first = count * (odd if late else 1 - odd)

    def piece(ref):
        return ref[ref.shape[0] - halo_rows :].astype(F32)

    if late:
        def forwarded(ref):
            return jnp.concatenate(
                [
                    ref[parent_rows:, t * LANES : (t + 1) * LANES].astype(F32)
                    for t in range(ref.shape[1] // LANES)
                ],
                axis=0,
            )

        partner = samp ^ (samp - 1 + 2 * odd)
        halo = piece(from_far[0])
        for i in range(1, len(from_far)):
            halo = jnp.where(partner == (4 << i) - 1, piece(from_far[i]), halo)
        box_odd = lax.rem(box, 2) == 1
        from_left = samp == 0
        passed = jnp.where(box_odd == from_left, forwarded(beside), forwarded(across))
        halo = jnp.where(jnp.logical_or(from_left, samp == nsamp - 1), passed, halo)
    else:
        halo = piece(from_beside)
    at = jnp.where(first > 0, boxes + count, 0)
    for i in range(count):
        window[at + i] = widen(halo[i * parts : (i + 1) * parts])
    mine = own[...].astype(F32)
    for i in range(boxes):
        window[count + i] = widen(mine[i * parts : (i + 1) * parts])
    list_copy.wait()
    base = (box * nsamp + samp) * boxes
    for i in range(count):
        acc = None
        for k in range(near_count):
            j = lax.rem(nbr[k, first + i] - base + count + total, total)
            mat = jnp.concatenate([mats[first + i, k, 0], mats[first + i, k, 1]], axis=1)
            y = nt_dot(window[j].astype(BF16), mat)
            acc = y if acc is None else acc + y
        out_ref[i] = acc


def final_kernel(*refs, pieces):
    parts_in = refs[:pieces]
    near_early, near_late, mats, out_ref, field = refs[pieces:]
    boxes, halves, rhs = out_ref.shape[:3]
    parts = halves * rhs
    half = boxes // 2
    odd = lax.rem(lax.axis_index("samp"), 2) == 1
    total = parts_in[0][...].astype(F32)
    for m in parts_in[1:]:
        total += m[...].astype(F32)
    field[...] = total.astype(BF16).astype(F32)
    for n in range(boxes):
        v = field[pl.ds(n, parts, stride=boxes), :]
        wide = jnp.concatenate([v, times_i(v)], axis=1).astype(BF16)
        y = nt_dot(wide, jnp.concatenate([mats[n, 0], mats[n, 1]], axis=1))
        i = n % half
        y = y + jnp.where(odd == (n < half), near_early[i], near_late[i])
        out_ref[n, 0] = y[:rhs]
        out_ref[n, 1] = y[rhs:]


def whole_in(kind):
    return pl.BlockSpec(memory_space=kind)


VM = pltpu.VMEM
SM = pltpu.SMEM
HBM = pltpu.HBM
DMA = pltpu.SemaphoreType.DMA
PARAMS = pltpu.CompilerParams(vmem_limit_bytes=24 * 1024 * 1024)


def stay(x):
    return pltpu.with_memory_space_constraint(x, HBM)


def on_device(
    xvec,
    near_blocks,
    neighbours,
    lift,
    place,
    interp,
    phases,
    octant,
    leaf_parent_index,
    translators,
    inter_list,
    trans_id,
):
    boxes, halves, rhs, unknowns = xvec.shape
    parts = halves * rhs
    nsamp = lax.axis_size("samp")
    nbox = lax.axis_size("box")
    total = boxes * nsamp * nbox
    reach = boxes // 2
    parents = boxes * nsamp // 8
    all_parents = parents * nbox
    samples = interp.shape[0] // nsamp
    slots = 8 * parents
    leaves = boxes * nsamp
    near_count = near_blocks.shape[1]
    halo_rows = reach * parts
    parent_rows = parents * parts
    plain_rows = parts * boxes + CODE_ROWS

    def shape(dims, dtype=BF16):
        return jax.ShapeDtypeStruct(dims, dtype)

    lift_chunks = 2
    to_far, plain, to_beside, x_rows = pl.pallas_call(
        lambda *refs: leaf_kernel(*refs, parents=parents),
        in_specs=[whole_in(HBM)] * 4,
        out_specs=[whole_in(VM)] * 4,
        out_shape=[
            shape((plain_rows + halo_rows, LANES)),
            shape((plain_rows, LANES)),
            shape((plain_rows + halo_rows, LANES)),
            shape((boxes * parts, LANES)),
        ],
        scratch_shapes=[
            VM(xvec.shape, BF16),
            VM((parts * boxes, LANES), F32),
            VM(lift.shape, BF16),
            SM((boxes,), jnp.int32),
            SM((boxes,), jnp.int32),
            DMA((lift_chunks + 3,)),
        ],
        compiler_params=PARAMS,
        name="leaf",
    )(*[stay(a) for a in (octant, leaf_parent_index, xvec, lift)])

    def exchange(x, d):
        return lax.ppermute(x, "samp", [(i, i ^ d) for i in range(nsamp)])

    order = [0, nsamp - 1, *range(1, nsamp - 1)]
    far = [(4 << i) - 1 for i in range(nsamp.bit_length() - 2)]
    messages = {0: plain}
    for d in order[1:]:
        messages[d] = exchange(to_beside if d == 1 else to_far if d in far else plain, d)
    far_messages = [messages[d] for d in far]

    dense, near_list = pl.pallas_call(
        lambda *refs: prep_kernel(*refs, parents=parents, all_parents=all_parents),
        in_specs=[whole_in(HBM)] * 5 + [whole_in(VM)],
        out_specs=[whole_in(VM)] * 2,
        out_shape=[
            shape((parents, len(zone(parents)), 2, samples), F32),
            shape((near_count, boxes), jnp.int32),
        ],
        scratch_shapes=[
            SM(inter_list.shape, jnp.int32),
            SM(trans_id.shape, jnp.int32),
            VM(translators.shape, F32),
            DMA((4,)),
        ],
        compiler_params=PARAMS,
        cost_estimate=pl.CostEstimate(
            flops=0, bytes_accessed=2 * near_blocks.size, transcendentals=0
        ),
        name="prep",
    )(
        stay(inter_list),
        stay(trans_id),
        stay(neighbours.T),
        stay(translators),
        stay(near_blocks),
        x_rows,
    )

    to_across, parent_pat, place_onehot = pl.pallas_call(
        lambda *refs: up_kernel(
            *refs, pieces=nsamp, boxes=boxes, parents=parents, parts=parts
        ),
        in_specs=[whole_in(VM)] * (nsamp + 3),
        out_specs=[whole_in(VM)] * 3,
        out_shape=[
            shape((parent_rows + halo_rows * LANES // samples, samples)),
            shape((parent_rows + halo_rows * LANES // samples, samples)),
            shape((leaves, slots)),
        ],
        scratch_shapes=[
            VM((parts * slots, samples), F32),
            VM((samples // LANES, parent_rows, LANES), F32),
        ],
        compiler_params=PARAMS,
        name="up",
    )(*[messages[d] for d in order], interp, phases, near_list)

    across = lax.ppermute(
        to_across, "box", [(i, (i + (1 if i % 2 else -1)) % nbox) for i in range(nbox)]
    )
    beside = lax.ppermute(parent_pat, "box", [(i, i ^ 1) for i in range(nbox)])

    def near_half(late, args):
        return pl.pallas_call(
            lambda *refs: near_kernel(
                *refs,
                late=late,
                nsamp=nsamp,
                total=total,
                halo_rows=halo_rows,
                parent_rows=parent_rows,
            ),
            in_specs=[whole_in(VM)] * (3 + len(args)),
            out_specs=whole_in(VM),
            out_shape=shape((reach, parts, unknowns), F32),
            scratch_shapes=[
                VM((boxes + 2 * reach, parts, 2 * unknowns), F32),
                SM((near_count, boxes), jnp.int32),
                DMA((1,)),
            ],
            compiler_params=PARAMS,
            cost_estimate=pl.CostEstimate(
                flops=parts * near_blocks.size,
                bytes_accessed=near_blocks.size,
                transcendentals=0,
            ),
            name="near",
        )(near_list, x_rows, near_blocks, *args)

    near_early = near_half(False, [place_onehot, messages[1]])

    fields = pl.pallas_call(
        lambda *refs: down_kernel(
            *refs, pieces=nsamp, boxes=boxes, parents=parents, parts=parts
        ),
        in_specs=[whole_in(VM)] * 8,
        out_specs=[whole_in(VM)] * nsamp,
        out_shape=[shape((parts * boxes, LANES))] * nsamp,
        scratch_shapes=[
            VM((3 * parents, parts, samples), F32),
            VM((samples // LANES, parent_rows, LANES), F32),
            VM((parts * slots, samples), BF16),
        ],
        compiler_params=PARAMS,
        name="down",
    )(parent_pat, across, beside, dense, interp, phases, place_onehot, near_early)

    pieces = dict(zip(order, fields))
    partial = [pieces[0]] + [exchange(pieces[d], d) for d in reversed(range(1, nsamp))]

    near_late = near_half(True, [fields[0], across, beside, *far_messages])

    return pl.pallas_call(
        lambda *refs: final_kernel(*refs, pieces=nsamp),
        in_specs=[whole_in(VM)] * (nsamp + 3),
        out_specs=whole_in(VM),
        out_shape=shape(xvec.shape, F32),
        scratch_shapes=[VM((parts * boxes, LANES), F32)],
        compiler_params=PARAMS,
        name="final",
    )(*partial, near_early, near_late, place)


def solution(mesh):
    in_specs = (
        P(("box", "samp"), None, None, None),
        P(("box", "samp"), None, None, None, None),
        P(("box", "samp"), None),
        P(("box", "samp"), None, None, None),
        P(("box", "samp"), None, None, None),
        P(),
        P(),
        P(("box", "samp")),
        P(("box", "samp")),
        P(None, None, "samp"),
        P("box", None),
        P("box", None),
    )
    out_specs = P(("box", "samp"), None, None, None)
    return jax.shard_map(
        on_device, mesh=mesh, in_specs=in_specs, out_specs=out_specs, check_vma=False
    )
```

```python
import jax
import jax.numpy as jnp
from jax import lax
from jax.experimental import pallas as pl
from jax.experimental.pallas import tpu as pltpu
from jax.sharding import PartitionSpec as P

F32 = jnp.float32
BF16 = jnp.bfloat16
LANES = 128
CODE_ROWS = 8


def nt_dot(a, b):
    return lax.dot_general(a, b, (((1,), (1,)), ((), ())), preferred_element_type=F32)


def nn_dot(a, b):
    return lax.dot_general(a, b, (((1,), (0,)), ((), ())), preferred_element_type=F32)


def times_i(v):
    half = v.shape[0] // 2
    return jnp.concatenate([-v[half:], v[:half]], axis=0)


def widen(v):
    return jnp.concatenate([v, times_i(v)], axis=1)


def leaf_kernel(
    octant, parent, x_hbm, lift_hbm, inter, trans, table_hbm,
    to_far, plain, to_beside, x_rows, dense,
    x_ref, rows, lift, oct_s, par_s, sems, inter_s, trans_s, table, more,
    *, parents, all_parents,
):
    boxes, halves, rhs, _ = x_ref.shape
    parts = halves * rhs
    reach = boxes // 2
    chunks = sems.shape[0] - 3
    per = boxes // chunks
    small = [
        pltpu.make_async_copy(x_hbm, x_ref, sems.at[chunks]),
        pltpu.make_async_copy(octant, oct_s, sems.at[chunks + 1]),
        pltpu.make_async_copy(parent, par_s, sems.at[chunks + 2]),
    ]
    big = [
        pltpu.make_async_copy(
            lift_hbm.at[pl.ds(i * per, per)], lift.at[pl.ds(i * per, per)], sems.at[i]
        )
        for i in range(chunks)
    ]
    for copy in small + big:
        copy.start()
    start, finish = fill_dense(
        dense, inter, trans, table_hbm, inter_s, trans_s, table, more, parents, all_parents
    )
    pl.when(odd_box())(start)
    for copy in small:
        copy.wait()
    own = [
        jnp.concatenate([x_ref[n, 0].astype(F32), x_ref[n, 1].astype(F32)], axis=0)
        for n in range(boxes)
    ]
    lane = lax.rem(lax.broadcasted_iota(jnp.int32, (boxes, LANES), 1), boxes)
    codes = jnp.zeros((boxes, LANES), F32)
    for n in range(boxes):
        slot = (oct_s[n] * parents + lax.rem(par_s[n], parents)).astype(F32)
        codes = jnp.where(lane == n, slot, codes)
    codes = codes[:CODE_ROWS].astype(BF16)
    x_rows[...] = jnp.concatenate(own, axis=0).astype(BF16)
    first = jnp.concatenate(own[:reach], axis=0)
    last = jnp.concatenate(own[reach:], axis=0)
    odd = lax.rem(lax.axis_index("samp"), 2) == 1
    at = parts * boxes
    to_beside[at + CODE_ROWS :] = jnp.where(odd, first, last).astype(BF16)
    to_far[at + CODE_ROWS :] = jnp.where(odd, last, first).astype(BF16)
    for ref in (plain, to_beside, to_far):
        ref[at : at + CODE_ROWS] = codes
    for n in range(boxes):
        if n % per == 0:
            big[n // per].wait()
        mat = jnp.concatenate([lift[n, 0], lift[n, 1]], axis=1)
        rows[pl.ds(n, parts, stride=boxes), :] = nt_dot(widen(own[n]).astype(BF16), mat)
    pattern = rows[...].astype(BF16)
    for ref in (plain, to_beside, to_far):
        ref[:at] = pattern
    pl.when(odd_box())(finish)


def up_kernel(*refs, pieces, boxes, parents, parts):
    msgs = refs[:pieces]
    interp_ref, phase_ref, after, out_ref, out_copy, place_ref, raised, folded = refs[pieces:]
    forward = msgs[1]
    slots = 8 * parents
    samples = raised.shape[1]
    first = lax.axis_index("samp") * samples
    mine = interp_ref[pl.ds(pl.multiple_of(first, samples), samples)]
    per_tile = LANES // boxes
    at = parts * boxes
    tiles = []
    for t in range(0, pieces, per_tile):
        lane = lax.broadcasted_iota(jnp.int32, (CODE_ROWS, LANES), 1) // boxes
        code = msgs[t][at : at + CODE_ROWS].astype(F32)
        for d in range(1, min(per_tile, pieces - t)):
            code = jnp.where(lane == d, msgs[t + d][at : at + CODE_ROWS].astype(F32), code)
        code = jnp.concatenate([code] * (slots // CODE_ROWS), axis=0)
        want = lax.broadcasted_iota(jnp.int32, (slots, LANES), 0).astype(F32)
        width = min(per_tile, pieces - t) * boxes
        tiles.append(jnp.where(code == want, 1.0, 0.0)[:, :width])
    sorter = jnp.concatenate(tiles, axis=1)
    place_ref[...] = sorter.T.astype(BF16)
    sorter = sorter.astype(BF16)
    pats = jnp.concatenate(
        [
            jnp.concatenate([m[c * boxes : (c + 1) * boxes] for m in msgs], axis=0)
            for c in range(parts)
        ],
        axis=1,
    )
    ordered = nn_dot(sorter, pats).astype(BF16)
    stacked = jnp.concatenate(
        [ordered[:, c * LANES : (c + 1) * LANES] for c in range(parts)], axis=0
    )
    raised[...] = nt_dot(stacked, mine)
    half = parts // 2
    for t in range(samples // LANES):
        lanes = slice(t * LANES, (t + 1) * LANES)
        here = pl.ds(pl.multiple_of(first + t * LANES, LANES), LANES)
        for r in range(half):
            re = im = None
            for o in range(8):
                ph_r = phase_ref[o, 0:1, here]
                ph_i = phase_ref[o, 1:2, here]
                base_r = r * slots + o * parents
                base_i = (half + r) * slots + o * parents
                xr = raised[base_r : base_r + parents, lanes]
                xi = raised[base_i : base_i + parents, lanes]
                dr = ph_r * xr - ph_i * xi
                di = ph_r * xi + ph_i * xr
                re = dr if re is None else re + dr
                im = di if im is None else im + di
            folded[t, r * parents : (r + 1) * parents] = re
            folded[t, (half + r) * parents : (half + r + 1) * parents] = im
        for p in range(0, parents, 2):
            both = jnp.concatenate(
                [folded[t, pl.ds(p + e, parts, stride=parents), :] for e in range(2)], axis=0
            )
            both = both.astype(BF16)
            for ref in (out_ref, out_copy):
                ref[p * parts : (p + 2) * parts, lanes] = both
        extra = out_ref.shape[0] - parents * parts
        start = forward.shape[0] - extra * (samples // LANES - t)
        for ref in (out_ref, out_copy):
            ref[parents * parts :, lanes] = forward[start : start + extra]


def zone(parents):
    return [d for d in range(-parents, parents + 1) if abs(d) >= 2]


def fill_dense(dense, inter_hbm, trans_hbm, table_hbm, inter, trans, table, sems, parents, all_parents):
    copies = [
        pltpu.make_async_copy(inter_hbm, inter, sems.at[0]),
        pltpu.make_async_copy(trans_hbm, trans, sems.at[1]),
        pltpu.make_async_copy(table_hbm, table, sems.at[2]),
    ]
    first = lax.axis_index("box") * parents

    def start():
        for copy in copies:
            copy.start()

    def finish():
        for copy in copies:
            copy.wait()
        if len(zone(parents)) > inter.shape[1]:
            dense[...] = jnp.zeros_like(dense)

        def fill(p, carry):
            for k in range(inter.shape[1]):
                rel = lax.rem(inter[p, k] - first - p + parents + all_parents, all_parents)
                at = jnp.where(rel < parents, rel, rel - 3)
                dense[p, at] = table[trans[p, k]]
            return carry

        lax.fori_loop(0, parents, fill, 0)

    return start, finish


def odd_box():
    return lax.rem(lax.axis_index("box"), 2) == 1


def prep_kernel(
    inter, trans, neighbours, table_hbm, mats_hbm, dense_in, after, dense, nbr,
    inter_s, trans_s, table, sems, *, parents, all_parents,
):
    copy = pltpu.make_async_copy(neighbours, nbr, sems.at[3])
    copy.start()
    start, finish = fill_dense(
        dense, inter, trans, table_hbm, inter_s, trans_s, table, sems, parents, all_parents
    )

    @pl.when(jnp.logical_not(odd_box()))
    def _():
        start()
        finish()

    copy.wait()


def down_kernel(
    own, across, beside, dense, interp_ref, phase_ref, place_ref, after, *refs, pieces, boxes, parents, parts
):
    outs = refs[:pieces]
    window, incoming, shifted = refs[pieces:]
    samples = window.shape[2]
    first = lax.axis_index("samp") * samples
    mine = interp_ref[pl.ds(pl.multiple_of(first, samples), samples)]
    slots = 8 * parents
    half = parts // 2
    odd = lax.rem(lax.axis_index("box"), 2)
    rows = parents * parts
    window[parents : 2 * parents] = own[:rows].astype(F32).reshape(parents, parts, samples)
    window[pl.ds(2 * parents * odd, parents)] = (
        across[:rows].astype(F32).reshape(parents, parts, samples)
    )
    window[pl.ds(2 * parents * (1 - odd), parents)] = (
        beside[:rows].astype(F32).reshape(parents, parts, samples)
    )
    offsets = zone(parents)

    def one(p, t, source):
        lanes = slice(t * LANES, (t + 1) * LANES)
        acc_r = acc_i = None
        for i, d in enumerate(offsets):
            x = source(p + d)
            yr = dense[p, i, 0:1, lanes] * x
            yi = dense[p, i, 1:2, lanes] * x
            acc_r = yr if acc_r is None else acc_r + yr
            acc_i = yi if acc_i is None else acc_i + yi
        got = (acc_r + times_i(acc_i)).astype(BF16).astype(F32)
        incoming[t, pl.ds(p * parts, parts), :] = got

    for t in range(samples // LANES):
        lanes = slice(t * LANES, (t + 1) * LANES)
        if parents <= 8:
            held = [window[j, :, lanes] for j in range(3 * parents)]
            for p in range(parents):
                one(p, t, lambda j: held[parents + j])
        else:
            lax.fori_loop(
                0,
                parents,
                lambda p, c: (one(p, t, lambda j: window[parents + j, :, lanes]), c)[1],
                0,
            )
    for t in range(samples // LANES):
        lanes = slice(t * LANES, (t + 1) * LANES)
        here = pl.ds(pl.multiple_of(first + t * LANES, LANES), LANES)
        for r in range(half):
            ir = incoming[t, pl.ds(r, parents, stride=parts), :]
            ii = incoming[t, pl.ds(half + r, parents, stride=parts), :]
            re, im = [], []
            for o in range(8):
                ph_r = phase_ref[o, 0:1, here]
                ph_i = phase_ref[o, 1:2, here]
                re.append(ph_r * ir - ph_i * ii)
                im.append(ph_r * ii + ph_i * ir)
            shifted[r * slots : (r + 1) * slots, lanes] = jnp.concatenate(re, axis=0).astype(BF16)
            shifted[(half + r) * slots : (half + r + 1) * slots, lanes] = jnp.concatenate(
                im, axis=0
            ).astype(BF16)
    field = nn_dot(shifted[...], mine).astype(BF16)
    spread = jnp.concatenate([field[c * slots : (c + 1) * slots] for c in range(parts)], axis=1)
    leaves = nn_dot(place_ref[...], spread).astype(BF16)
    for d in range(pieces):
        for c in range(parts):
            outs[d][c * boxes : (c + 1) * boxes] = leaves[
                d * boxes : (d + 1) * boxes, c * LANES : (c + 1) * LANES
            ]


def near_kernel(*refs, late, nsamp, total, halo_rows, parent_rows):
    neighbours, own, mats, after, *halos, out_ref, window, nbr, sems = refs
    if late:
        across, beside, *from_far = halos
    else:
        (from_beside,) = halos
    list_copy = pltpu.make_async_copy(neighbours, nbr, sems.at[0])
    list_copy.start()
    count, parts, unknowns = out_ref.shape
    boxes = own.shape[0] // parts
    near_count = mats.shape[1]
    samp = lax.axis_index("samp")
    box = lax.axis_index("box")
    odd = lax.rem(samp, 2)
    first = count * (odd if late else 1 - odd)

    def piece(ref):
        return ref[ref.shape[0] - halo_rows :].astype(F32)

    if late:
        def forwarded(ref):
            return jnp.concatenate(
                [
                    ref[parent_rows:, t * LANES : (t + 1) * LANES].astype(F32)
                    for t in range(ref.shape[1] // LANES)
                ],
                axis=0,
            )

        partner = samp ^ (samp - 1 + 2 * odd)
        halo = piece(from_far[0])
        for i in range(1, len(from_far)):
            halo = jnp.where(partner == (4 << i) - 1, piece(from_far[i]), halo)
        box_odd = lax.rem(box, 2) == 1
        from_left = samp == 0
        passed = jnp.where(box_odd == from_left, forwarded(beside), forwarded(across))
        halo = jnp.where(jnp.logical_or(from_left, samp == nsamp - 1), passed, halo)
    else:
        halo = piece(from_beside)
    at = jnp.where(first > 0, boxes + count, 0)
    for i in range(count):
        window[at + i] = widen(halo[i * parts : (i + 1) * parts])
    mine = own[...].astype(F32)
    for i in range(boxes):
        window[count + i] = widen(mine[i * parts : (i + 1) * parts])
    list_copy.wait()
    base = (box * nsamp + samp) * boxes
    for i in range(count):
        acc = None
        for k in range(near_count):
            j = lax.rem(nbr[k, first + i] - base + count + total, total)
            mat = jnp.concatenate([mats[first + i, k, 0], mats[first + i, k, 1]], axis=1)
            y = nt_dot(window[j].astype(BF16), mat)
            acc = y if acc is None else acc + y
        out_ref[i] = acc


def final_kernel(*refs, pieces):
    parts_in = refs[:pieces]
    near_early, near_late, mats, out_ref, field = refs[pieces:]
    boxes, halves, rhs = out_ref.shape[:3]
    parts = halves * rhs
    half = boxes // 2
    odd = lax.rem(lax.axis_index("samp"), 2) == 1
    total = parts_in[0][...].astype(F32)
    for m in parts_in[1:]:
        total += m[...].astype(F32)
    field[...] = total.astype(BF16).astype(F32)
    for n in range(boxes):
        v = field[pl.ds(n, parts, stride=boxes), :]
        wide = jnp.concatenate([v, times_i(v)], axis=1).astype(BF16)
        y = nt_dot(wide, jnp.concatenate([mats[n, 0], mats[n, 1]], axis=1))
        i = n % half
        y = y + jnp.where(odd == (n < half), near_early[i], near_late[i])
        out_ref[n, 0] = y[:rhs]
        out_ref[n, 1] = y[rhs:]


def whole_in(kind):
    return pl.BlockSpec(memory_space=kind)


VM = pltpu.VMEM
SM = pltpu.SMEM
HBM = pltpu.HBM
DMA = pltpu.SemaphoreType.DMA
PARAMS = pltpu.CompilerParams(vmem_limit_bytes=24 * 1024 * 1024)


def stay(x):
    return pltpu.with_memory_space_constraint(x, HBM)


def on_device(
    xvec,
    near_blocks,
    neighbours,
    lift,
    place,
    interp,
    phases,
    octant,
    leaf_parent_index,
    translators,
    inter_list,
    trans_id,
):
    boxes, halves, rhs, unknowns = xvec.shape
    parts = halves * rhs
    nsamp = lax.axis_size("samp")
    nbox = lax.axis_size("box")
    total = boxes * nsamp * nbox
    reach = boxes // 2
    parents = boxes * nsamp // 8
    all_parents = parents * nbox
    samples = interp.shape[0] // nsamp
    slots = 8 * parents
    leaves = boxes * nsamp
    near_count = near_blocks.shape[1]
    halo_rows = reach * parts
    parent_rows = parents * parts
    plain_rows = parts * boxes + CODE_ROWS

    def shape(dims, dtype=BF16):
        return jax.ShapeDtypeStruct(dims, dtype)

    lift_chunks = 2
    to_far, plain, to_beside, x_rows, dense = pl.pallas_call(
        lambda *refs: leaf_kernel(*refs, parents=parents, all_parents=all_parents),
        in_specs=[whole_in(HBM)] * 7,
        out_specs=[whole_in(VM)] * 5,
        out_shape=[
            shape((plain_rows + halo_rows, LANES)),
            shape((plain_rows, LANES)),
            shape((plain_rows + halo_rows, LANES)),
            shape((boxes * parts, LANES)),
            shape((parents, len(zone(parents)), 2, samples), F32),
        ],
        scratch_shapes=[
            VM(xvec.shape, BF16),
            VM((parts * boxes, LANES), F32),
            VM(lift.shape, BF16),
            SM((boxes,), jnp.int32),
            SM((boxes,), jnp.int32),
            DMA((lift_chunks + 3,)),
            SM(inter_list.shape, jnp.int32),
            SM(trans_id.shape, jnp.int32),
            VM(translators.shape, F32),
            DMA((3,)),
        ],
        compiler_params=PARAMS,
        name="leaf",
    )(
        *[stay(a) for a in (octant, leaf_parent_index, xvec, lift)],
        *[stay(a) for a in (inter_list, trans_id, translators)],
    )

    def exchange(x, d):
        return lax.ppermute(x, "samp", [(i, i ^ d) for i in range(nsamp)])

    order = [0, nsamp - 1, *range(1, nsamp - 1)]
    far = [(4 << i) - 1 for i in range(nsamp.bit_length() - 2)]
    messages = {0: plain}
    for d in order[1:]:
        messages[d] = exchange(to_beside if d == 1 else to_far if d in far else plain, d)
    far_messages = [messages[d] for d in far]

    dense, near_list = pl.pallas_call(
        lambda *refs: prep_kernel(*refs, parents=parents, all_parents=all_parents),
        in_specs=[whole_in(HBM)] * 5 + [whole_in(VM)] * 2,
        out_specs=[whole_in(VM)] * 2,
        input_output_aliases={5: 0},
        out_shape=[
            shape((parents, len(zone(parents)), 2, samples), F32),
            shape((near_count, boxes), jnp.int32),
        ],
        scratch_shapes=[
            SM(inter_list.shape, jnp.int32),
            SM(trans_id.shape, jnp.int32),
            VM(translators.shape, F32),
            DMA((4,)),
        ],
        compiler_params=PARAMS,
        cost_estimate=pl.CostEstimate(
            flops=0, bytes_accessed=2 * near_blocks.size, transcendentals=0
        ),
        name="prep",
    )(
        stay(inter_list),
        stay(trans_id),
        stay(neighbours.T),
        stay(translators),
        stay(near_blocks),
        dense,
        x_rows,
    )

    to_across, parent_pat, place_onehot = pl.pallas_call(
        lambda *refs: up_kernel(
            *refs, pieces=nsamp, boxes=boxes, parents=parents, parts=parts
        ),
        in_specs=[whole_in(VM)] * (nsamp + 3),
        out_specs=[whole_in(VM)] * 3,
        out_shape=[
            shape((parent_rows + halo_rows * LANES // samples, samples)),
            shape((parent_rows + halo_rows * LANES // samples, samples)),
            shape((leaves, slots)),
        ],
        scratch_shapes=[
            VM((parts * slots, samples), F32),
            VM((samples // LANES, parent_rows, LANES), F32),
        ],
        compiler_params=PARAMS,
        name="up",
    )(*[messages[d] for d in order], interp, phases, near_list)

    across = lax.ppermute(
        to_across, "box", [(i, (i + (1 if i % 2 else -1)) % nbox) for i in range(nbox)]
    )
    beside = lax.ppermute(parent_pat, "box", [(i, i ^ 1) for i in range(nbox)])

    def near_half(late, args):
        return pl.pallas_call(
            lambda *refs: near_kernel(
                *refs,
                late=late,
                nsamp=nsamp,
                total=total,
                halo_rows=halo_rows,
                parent_rows=parent_rows,
            ),
            in_specs=[whole_in(VM)] * (3 + len(args)),
            out_specs=whole_in(VM),
            out_shape=shape((reach, parts, unknowns), F32),
            scratch_shapes=[
                VM((boxes + 2 * reach, parts, 2 * unknowns), F32),
                SM((near_count, boxes), jnp.int32),
                DMA((1,)),
            ],
            compiler_params=PARAMS,
            cost_estimate=pl.CostEstimate(
                flops=parts * near_blocks.size,
                bytes_accessed=near_blocks.size,
                transcendentals=0,
            ),
            name="near",
        )(near_list, x_rows, near_blocks, *args)

    near_early = near_half(False, [place_onehot, messages[1]])

    fields = pl.pallas_call(
        lambda *refs: down_kernel(
            *refs, pieces=nsamp, boxes=boxes, parents=parents, parts=parts
        ),
        in_specs=[whole_in(VM)] * 8,
        out_specs=[whole_in(VM)] * nsamp,
        out_shape=[shape((parts * boxes, LANES))] * nsamp,
        scratch_shapes=[
            VM((3 * parents, parts, samples), F32),
            VM((samples // LANES, parent_rows, LANES), F32),
            VM((parts * slots, samples), BF16),
        ],
        compiler_params=PARAMS,
        name="down",
    )(parent_pat, across, beside, dense, interp, phases, place_onehot, near_early)

    pieces = dict(zip(order, fields))
    partial = [pieces[0]] + [exchange(pieces[d], d) for d in reversed(range(1, nsamp))]

    near_late = near_half(True, [fields[0], across, beside, *far_messages])

    return pl.pallas_call(
        lambda *refs: final_kernel(*refs, pieces=nsamp),
        in_specs=[whole_in(VM)] * (nsamp + 3),
        out_specs=whole_in(VM),
        out_shape=shape(xvec.shape, F32),
        scratch_shapes=[VM((parts * boxes, LANES), F32)],
        compiler_params=PARAMS,
        name="final",
    )(*partial, near_early, near_late, place)


def solution(mesh):
    in_specs = (
        P(("box", "samp"), None, None, None),
        P(("box", "samp"), None, None, None, None),
        P(("box", "samp"), None),
        P(("box", "samp"), None, None, None),
        P(("box", "samp"), None, None, None),
        P(),
        P(),
        P(("box", "samp")),
        P(("box", "samp")),
        P(None, None, "samp"),
        P("box", None),
        P("box", None),
    )
    out_specs = P(("box", "samp"), None, None, None)
    return jax.shard_map(
        on_device, mesh=mesh, in_specs=in_specs, out_specs=out_specs, check_vma=False
    )
```

```python
import jax
import jax.numpy as jnp
from jax import lax
from jax.experimental import pallas as pl
from jax.experimental.pallas import tpu as pltpu
from jax.sharding import PartitionSpec as P

F32 = jnp.float32
BF16 = jnp.bfloat16
LANES = 128
CODE_ROWS = 8


def nt_dot(a, b):
    return lax.dot_general(a, b, (((1,), (1,)), ((), ())), preferred_element_type=F32)


def nn_dot(a, b):
    return lax.dot_general(a, b, (((1,), (0,)), ((), ())), preferred_element_type=F32)


def times_i(v):
    half = v.shape[0] // 2
    return jnp.concatenate([-v[half:], v[:half]], axis=0)


def widen(v):
    return jnp.concatenate([v, times_i(v)], axis=1)


def leaf_kernel(
    octant, parent, x_hbm, lift_hbm, inter, trans, table_hbm,
    to_far, plain, to_beside, x_rows, dense,
    x_ref, rows, lift, oct_s, par_s, sems, inter_s, trans_s, table, more,
    *, parents, all_parents,
):
    boxes, halves, rhs, _ = x_ref.shape
    parts = halves * rhs
    reach = boxes // 2
    chunks = sems.shape[0] - 3
    per = boxes // chunks
    small = [
        pltpu.make_async_copy(x_hbm, x_ref, sems.at[chunks]),
        pltpu.make_async_copy(octant, oct_s, sems.at[chunks + 1]),
        pltpu.make_async_copy(parent, par_s, sems.at[chunks + 2]),
    ]
    big = [
        pltpu.make_async_copy(
            lift_hbm.at[pl.ds(i * per, per)], lift.at[pl.ds(i * per, per)], sems.at[i]
        )
        for i in range(chunks)
    ]
    for copy in small + big:
        copy.start()
    start, finish = fill_dense(
        dense, inter, trans, table_hbm, inter_s, trans_s, table, more, parents, all_parents
    )
    pl.when(odd_box())(start)
    for copy in small:
        copy.wait()
    own = [
        jnp.concatenate([x_ref[n, 0].astype(F32), x_ref[n, 1].astype(F32)], axis=0)
        for n in range(boxes)
    ]
    lane = lax.rem(lax.broadcasted_iota(jnp.int32, (boxes, LANES), 1), boxes)
    codes = jnp.zeros((boxes, LANES), F32)
    for n in range(boxes):
        slot = (oct_s[n] * parents + lax.rem(par_s[n], parents)).astype(F32)
        codes = jnp.where(lane == n, slot, codes)
    codes = codes[:CODE_ROWS].astype(BF16)
    x_rows[...] = jnp.concatenate(own, axis=0).astype(BF16)
    first = jnp.concatenate(own[:reach], axis=0)
    last = jnp.concatenate(own[reach:], axis=0)
    odd = lax.rem(lax.axis_index("samp"), 2) == 1
    at = parts * boxes
    to_beside[at + CODE_ROWS :] = jnp.where(odd, first, last).astype(BF16)
    to_far[at + CODE_ROWS :] = jnp.where(odd, last, first).astype(BF16)
    for ref in (plain, to_beside, to_far):
        ref[at : at + CODE_ROWS] = codes
    for n in range(boxes):
        if n % per == 0:
            big[n // per].wait()
        mat = jnp.concatenate([lift[n, 0], lift[n, 1]], axis=1)
        rows[pl.ds(n, parts, stride=boxes), :] = nt_dot(widen(own[n]).astype(BF16), mat)
    pattern = rows[...].astype(BF16)
    for ref in (plain, to_beside, to_far):
        ref[:at] = pattern
    pl.when(odd_box())(finish)


def up_kernel(*refs, pieces, boxes, parents, parts):
    msgs = refs[:pieces]
    interp_ref, phase_ref, after, out_ref, out_copy, place_ref, raised, folded = refs[pieces:]
    forward = msgs[2]
    slots = 8 * parents
    samples = raised.shape[1]
    first = lax.axis_index("samp") * samples
    mine = interp_ref[pl.ds(pl.multiple_of(first, samples), samples)]
    per_tile = LANES // boxes
    at = parts * boxes
    tiles = []
    for t in range(0, pieces, per_tile):
        lane = lax.broadcasted_iota(jnp.int32, (CODE_ROWS, LANES), 1) // boxes
        code = msgs[t][at : at + CODE_ROWS].astype(F32)
        for d in range(1, min(per_tile, pieces - t)):
            code = jnp.where(lane == d, msgs[t + d][at : at + CODE_ROWS].astype(F32), code)
        code = jnp.concatenate([code] * (slots // CODE_ROWS), axis=0)
        want = lax.broadcasted_iota(jnp.int32, (slots, LANES), 0).astype(F32)
        width = min(per_tile, pieces - t) * boxes
        tiles.append(jnp.where(code == want, 1.0, 0.0)[:, :width])
    sorter = jnp.concatenate(tiles, axis=1)
    place_ref[...] = sorter.T.astype(BF16)
    sorter = sorter.astype(BF16)
    pats = jnp.concatenate(
        [
            jnp.concatenate([m[c * boxes : (c + 1) * boxes] for m in msgs], axis=0)
            for c in range(parts)
        ],
        axis=1,
    )
    ordered = nn_dot(sorter, pats).astype(BF16)
    stacked = jnp.concatenate(
        [ordered[:, c * LANES : (c + 1) * LANES] for c in range(parts)], axis=0
    )
    raised[...] = nt_dot(stacked, mine)
    half = parts // 2
    for t in range(samples // LANES):
        lanes = slice(t * LANES, (t + 1) * LANES)
        here = pl.ds(pl.multiple_of(first + t * LANES, LANES), LANES)
        for r in range(half):
            re = im = None
            for o in range(8):
                ph_r = phase_ref[o, 0:1, here]
                ph_i = phase_ref[o, 1:2, here]
                base_r = r * slots + o * parents
                base_i = (half + r) * slots + o * parents
                xr = raised[base_r : base_r + parents, lanes]
                xi = raised[base_i : base_i + parents, lanes]
                dr = ph_r * xr - ph_i * xi
                di = ph_r * xi + ph_i * xr
                re = dr if re is None else re + dr
                im = di if im is None else im + di
            folded[t, r * parents : (r + 1) * parents] = re
            folded[t, (half + r) * parents : (half + r + 1) * parents] = im
        for p in range(0, parents, 2):
            both = jnp.concatenate(
                [folded[t, pl.ds(p + e, parts, stride=parents), :] for e in range(2)], axis=0
            )
            both = both.astype(BF16)
            for ref in (out_ref, out_copy):
                ref[p * parts : (p + 2) * parts, lanes] = both
        extra = out_ref.shape[0] - parents * parts
        start = forward.shape[0] - extra * (samples // LANES - t)
        for ref in (out_ref, out_copy):
            ref[parents * parts :, lanes] = forward[start : start + extra]


def zone(parents):
    return [d for d in range(-parents, parents + 1) if abs(d) >= 2]


def fill_dense(dense, inter_hbm, trans_hbm, table_hbm, inter, trans, table, sems, parents, all_parents):
    copies = [
        pltpu.make_async_copy(inter_hbm, inter, sems.at[0]),
        pltpu.make_async_copy(trans_hbm, trans, sems.at[1]),
        pltpu.make_async_copy(table_hbm, table, sems.at[2]),
    ]
    first = lax.axis_index("box") * parents

    def start():
        for copy in copies:
            copy.start()

    def finish():
        for copy in copies:
            copy.wait()
        if len(zone(parents)) > inter.shape[1]:
            dense[...] = jnp.zeros_like(dense)

        def fill(p, carry):
            for k in range(inter.shape[1]):
                rel = lax.rem(inter[p, k] - first - p + parents + all_parents, all_parents)
                at = jnp.where(rel < parents, rel, rel - 3)
                dense[p, at] = table[trans[p, k]]
            return carry

        lax.fori_loop(0, parents, fill, 0)

    return start, finish


def odd_box():
    return lax.rem(lax.axis_index("box"), 2) == 1


def prep_kernel(
    inter, trans, neighbours, table_hbm, mats_hbm, dense_in, after, dense, nbr,
    inter_s, trans_s, table, sems, *, parents, all_parents,
):
    copy = pltpu.make_async_copy(neighbours, nbr, sems.at[3])
    copy.start()
    start, finish = fill_dense(
        dense, inter, trans, table_hbm, inter_s, trans_s, table, sems, parents, all_parents
    )

    @pl.when(jnp.logical_not(odd_box()))
    def _():
        start()
        finish()

    copy.wait()


def down_kernel(
    own, across, beside, dense, interp_ref, phase_ref, place_ref, after, *refs, pieces, boxes, parents, parts
):
    outs = refs[:pieces]
    window, incoming, shifted = refs[pieces:]
    samples = window.shape[2]
    first = lax.axis_index("samp") * samples
    mine = interp_ref[pl.ds(pl.multiple_of(first, samples), samples)]
    slots = 8 * parents
    half = parts // 2
    odd = lax.rem(lax.axis_index("box"), 2)
    rows = parents * parts
    window[parents : 2 * parents] = own[:rows].astype(F32).reshape(parents, parts, samples)
    window[pl.ds(2 * parents * odd, parents)] = (
        across[:rows].astype(F32).reshape(parents, parts, samples)
    )
    window[pl.ds(2 * parents * (1 - odd), parents)] = (
        beside[:rows].astype(F32).reshape(parents, parts, samples)
    )
    offsets = zone(parents)

    def one(p, t, source):
        lanes = slice(t * LANES, (t + 1) * LANES)
        acc_r = acc_i = None
        for i, d in enumerate(offsets):
            x = source(p + d)
            yr = dense[p, i, 0:1, lanes] * x
            yi = dense[p, i, 1:2, lanes] * x
            acc_r = yr if acc_r is None else acc_r + yr
            acc_i = yi if acc_i is None else acc_i + yi
        got = (acc_r + times_i(acc_i)).astype(BF16).astype(F32)
        incoming[t, pl.ds(p * parts, parts), :] = got

    for t in range(samples // LANES):
        lanes = slice(t * LANES, (t + 1) * LANES)
        if parents <= 8:
            held = [window[j, :, lanes] for j in range(3 * parents)]
            for p in range(parents):
                one(p, t, lambda j: held[parents + j])
        else:
            lax.fori_loop(
                0,
                parents,
                lambda p, c: (one(p, t, lambda j: window[parents + j, :, lanes]), c)[1],
                0,
            )
    for t in range(samples // LANES):
        lanes = slice(t * LANES, (t + 1) * LANES)
        here = pl.ds(pl.multiple_of(first + t * LANES, LANES), LANES)
        for r in range(half):
            ir = incoming[t, pl.ds(r, parents, stride=parts), :]
            ii = incoming[t, pl.ds(half + r, parents, stride=parts), :]
            re, im = [], []
            for o in range(8):
                ph_r = phase_ref[o, 0:1, here]
                ph_i = phase_ref[o, 1:2, here]
                re.append(ph_r * ir - ph_i * ii)
                im.append(ph_r * ii + ph_i * ir)
            shifted[r * slots : (r + 1) * slots, lanes] = jnp.concatenate(re, axis=0).astype(BF16)
            shifted[(half + r) * slots : (half + r + 1) * slots, lanes] = jnp.concatenate(
                im, axis=0
            ).astype(BF16)
    field = nn_dot(shifted[...], mine).astype(BF16)
    spread = jnp.concatenate([field[c * slots : (c + 1) * slots] for c in range(parts)], axis=1)
    leaves = nn_dot(place_ref[...], spread).astype(BF16)
    for d in range(pieces):
        for c in range(parts):
            outs[d][c * boxes : (c + 1) * boxes] = leaves[
                d * boxes : (d + 1) * boxes, c * LANES : (c + 1) * LANES
            ]


def near_kernel(*refs, late, nsamp, total, halo_rows, parent_rows):
    neighbours, own, mats, after, *halos, out_ref, window, nbr, sems = refs
    if late:
        across, beside, *from_far = halos
    else:
        (from_beside,) = halos
    list_copy = pltpu.make_async_copy(neighbours, nbr, sems.at[0])
    list_copy.start()
    count, parts, unknowns = out_ref.shape
    boxes = own.shape[0] // parts
    near_count = mats.shape[1]
    samp = lax.axis_index("samp")
    box = lax.axis_index("box")
    odd = lax.rem(samp, 2)
    first = count * (odd if late else 1 - odd)

    def piece(ref):
        return ref[ref.shape[0] - halo_rows :].astype(F32)

    if late:
        def forwarded(ref):
            return jnp.concatenate(
                [
                    ref[parent_rows:, t * LANES : (t + 1) * LANES].astype(F32)
                    for t in range(ref.shape[1] // LANES)
                ],
                axis=0,
            )

        partner = samp ^ (samp - 1 + 2 * odd)
        halo = piece(from_far[0])
        for i in range(1, len(from_far)):
            halo = jnp.where(partner == (4 << i) - 1, piece(from_far[i]), halo)
        box_odd = lax.rem(box, 2) == 1
        from_left = samp == 0
        passed = jnp.where(box_odd == from_left, forwarded(beside), forwarded(across))
        halo = jnp.where(jnp.logical_or(from_left, samp == nsamp - 1), passed, halo)
    else:
        halo = piece(from_beside)
    at = jnp.where(first > 0, boxes + count, 0)
    for i in range(count):
        window[at + i] = widen(halo[i * parts : (i + 1) * parts])
    mine = own[...].astype(F32)
    for i in range(boxes):
        window[count + i] = widen(mine[i * parts : (i + 1) * parts])
    list_copy.wait()
    base = (box * nsamp + samp) * boxes
    for i in range(count):
        acc = None
        for k in range(near_count):
            j = lax.rem(nbr[k, first + i] - base + count + total, total)
            mat = jnp.concatenate([mats[first + i, k, 0], mats[first + i, k, 1]], axis=1)
            y = nt_dot(window[j].astype(BF16), mat)
            acc = y if acc is None else acc + y
        out_ref[i] = acc


def final_kernel(*refs, pieces):
    parts_in = refs[:pieces]
    near_early, near_late, mats, out_ref, field = refs[pieces:]
    boxes, halves, rhs = out_ref.shape[:3]
    parts = halves * rhs
    half = boxes // 2
    odd = lax.rem(lax.axis_index("samp"), 2) == 1
    total = parts_in[0][...].astype(F32)
    for m in parts_in[1:]:
        total += m[...].astype(F32)
    field[...] = total.astype(BF16).astype(F32)
    for n in range(boxes):
        v = field[pl.ds(n, parts, stride=boxes), :]
        wide = jnp.concatenate([v, times_i(v)], axis=1).astype(BF16)
        y = nt_dot(wide, jnp.concatenate([mats[n, 0], mats[n, 1]], axis=1))
        i = n % half
        y = y + jnp.where(odd == (n < half), near_early[i], near_late[i])
        out_ref[n, 0] = y[:rhs]
        out_ref[n, 1] = y[rhs:]


def whole_in(kind):
    return pl.BlockSpec(memory_space=kind)


VM = pltpu.VMEM
SM = pltpu.SMEM
HBM = pltpu.HBM
DMA = pltpu.SemaphoreType.DMA
PARAMS = pltpu.CompilerParams(vmem_limit_bytes=24 * 1024 * 1024)


def stay(x):
    return pltpu.with_memory_space_constraint(x, HBM)


def on_device(
    xvec,
    near_blocks,
    neighbours,
    lift,
    place,
    interp,
    phases,
    octant,
    leaf_parent_index,
    translators,
    inter_list,
    trans_id,
):
    boxes, halves, rhs, unknowns = xvec.shape
    parts = halves * rhs
    nsamp = lax.axis_size("samp")
    nbox = lax.axis_size("box")
    total = boxes * nsamp * nbox
    reach = boxes // 2
    parents = boxes * nsamp // 8
    all_parents = parents * nbox
    samples = interp.shape[0] // nsamp
    slots = 8 * parents
    leaves = boxes * nsamp
    near_count = near_blocks.shape[1]
    halo_rows = reach * parts
    parent_rows = parents * parts
    plain_rows = parts * boxes + CODE_ROWS

    def shape(dims, dtype=BF16):
        return jax.ShapeDtypeStruct(dims, dtype)

    lift_chunks = 2
    to_far, plain, to_beside, x_rows, dense = pl.pallas_call(
        lambda *refs: leaf_kernel(*refs, parents=parents, all_parents=all_parents),
        in_specs=[whole_in(HBM)] * 7,
        out_specs=[whole_in(VM)] * 5,
        out_shape=[
            shape((plain_rows + halo_rows, LANES)),
            shape((plain_rows, LANES)),
            shape((plain_rows + halo_rows, LANES)),
            shape((boxes * parts, LANES)),
            shape((parents, len(zone(parents)), 2, samples), F32),
        ],
        scratch_shapes=[
            VM(xvec.shape, BF16),
            VM((parts * boxes, LANES), F32),
            VM(lift.shape, BF16),
            SM((boxes,), jnp.int32),
            SM((boxes,), jnp.int32),
            DMA((lift_chunks + 3,)),
            SM(inter_list.shape, jnp.int32),
            SM(trans_id.shape, jnp.int32),
            VM(translators.shape, F32),
            DMA((3,)),
        ],
        compiler_params=PARAMS,
        name="leaf",
    )(
        *[stay(a) for a in (octant, leaf_parent_index, xvec, lift)],
        *[stay(a) for a in (inter_list, trans_id, translators)],
    )

    def exchange(x, d):
        return lax.ppermute(x, "samp", [(i, i ^ d) for i in range(nsamp)])

    order = [0, 1, nsamp - 1, *range(2, nsamp - 1)]
    far = [(4 << i) - 1 for i in range(nsamp.bit_length() - 2)]
    messages = {0: plain}
    for d in order[1:]:
        messages[d] = exchange(to_beside if d == 1 else to_far if d in far else plain, d)
    far_messages = [messages[d] for d in far]

    dense, near_list = pl.pallas_call(
        lambda *refs: prep_kernel(*refs, parents=parents, all_parents=all_parents),
        in_specs=[whole_in(HBM)] * 5 + [whole_in(VM)] * 2,
        out_specs=[whole_in(VM)] * 2,
        input_output_aliases={5: 0},
        out_shape=[
            shape((parents, len(zone(parents)), 2, samples), F32),
            shape((near_count, boxes), jnp.int32),
        ],
        scratch_shapes=[
            SM(inter_list.shape, jnp.int32),
            SM(trans_id.shape, jnp.int32),
            VM(translators.shape, F32),
            DMA((4,)),
        ],
        compiler_params=PARAMS,
        cost_estimate=pl.CostEstimate(
            flops=0, bytes_accessed=2 * near_blocks.size, transcendentals=0
        ),
        name="prep",
    )(
        stay(inter_list),
        stay(trans_id),
        stay(neighbours.T),
        stay(translators),
        stay(near_blocks),
        dense,
        x_rows,
    )

    to_across, parent_pat, place_onehot = pl.pallas_call(
        lambda *refs: up_kernel(
            *refs, pieces=nsamp, boxes=boxes, parents=parents, parts=parts
        ),
        in_specs=[whole_in(VM)] * (nsamp + 3),
        out_specs=[whole_in(VM)] * 3,
        out_shape=[
            shape((parent_rows + halo_rows * LANES // samples, samples)),
            shape((parent_rows + halo_rows * LANES // samples, samples)),
            shape((leaves, slots)),
        ],
        scratch_shapes=[
            VM((parts * slots, samples), F32),
            VM((samples // LANES, parent_rows, LANES), F32),
        ],
        compiler_params=PARAMS,
        name="up",
    )(*[messages[d] for d in order], interp, phases, near_list)

    across = lax.ppermute(
        to_across, "box", [(i, (i + (1 if i % 2 else -1)) % nbox) for i in range(nbox)]
    )
    beside = lax.ppermute(parent_pat, "box", [(i, i ^ 1) for i in range(nbox)])

    def near_half(late, args):
        return pl.pallas_call(
            lambda *refs: near_kernel(
                *refs,
                late=late,
                nsamp=nsamp,
                total=total,
                halo_rows=halo_rows,
                parent_rows=parent_rows,
            ),
            in_specs=[whole_in(VM)] * (3 + len(args)),
            out_specs=whole_in(VM),
            out_shape=shape((reach, parts, unknowns), F32),
            scratch_shapes=[
                VM((boxes + 2 * reach, parts, 2 * unknowns), F32),
                SM((near_count, boxes), jnp.int32),
                DMA((1,)),
            ],
            compiler_params=PARAMS,
            cost_estimate=pl.CostEstimate(
                flops=parts * near_blocks.size,
                bytes_accessed=near_blocks.size,
                transcendentals=0,
            ),
            name="near",
        )(near_list, x_rows, near_blocks, *args)

    near_early = near_half(False, [place_onehot, messages[1]])

    fields = pl.pallas_call(
        lambda *refs: down_kernel(
            *refs, pieces=nsamp, boxes=boxes, parents=parents, parts=parts
        ),
        in_specs=[whole_in(VM)] * 8,
        out_specs=[whole_in(VM)] * nsamp,
        out_shape=[shape((parts * boxes, LANES))] * nsamp,
        scratch_shapes=[
            VM((3 * parents, parts, samples), F32),
            VM((samples // LANES, parent_rows, LANES), F32),
            VM((parts * slots, samples), BF16),
        ],
        compiler_params=PARAMS,
        name="down",
    )(parent_pat, across, beside, dense, interp, phases, place_onehot, near_early)

    pieces = dict(zip(order, fields))
    partial = [pieces[0]] + [exchange(pieces[d], d) for d in reversed(range(1, nsamp))]

    near_late = near_half(True, [fields[0], across, beside, *far_messages])

    return pl.pallas_call(
        lambda *refs: final_kernel(*refs, pieces=nsamp),
        in_specs=[whole_in(VM)] * (nsamp + 3),
        out_specs=whole_in(VM),
        out_shape=shape(xvec.shape, F32),
        scratch_shapes=[VM((parts * boxes, LANES), F32)],
        compiler_params=PARAMS,
        name="final",
    )(*partial, near_early, near_late, place)


def solution(mesh):
    in_specs = (
        P(("box", "samp"), None, None, None),
        P(("box", "samp"), None, None, None, None),
        P(("box", "samp"), None),
        P(("box", "samp"), None, None, None),
        P(("box", "samp"), None, None, None),
        P(),
        P(),
        P(("box", "samp")),
        P(("box", "samp")),
        P(None, None, "samp"),
        P("box", None),
        P("box", None),
    )
    out_specs = P(("box", "samp"), None, None, None)
    return jax.shard_map(
        on_device, mesh=mesh, in_specs=in_specs, out_specs=out_specs, check_vma=False
    )
```

```python
import jax
import jax.numpy as jnp
from jax import lax
from jax.experimental import pallas as pl
from jax.experimental.pallas import tpu as pltpu
from jax.sharding import PartitionSpec as P

F32 = jnp.float32
BF16 = jnp.bfloat16
LANES = 128
CODE_ROWS = 8


def nt_dot(a, b):
    return lax.dot_general(a, b, (((1,), (1,)), ((), ())), preferred_element_type=F32)


def nn_dot(a, b):
    return lax.dot_general(a, b, (((1,), (0,)), ((), ())), preferred_element_type=F32)


def times_i(v):
    half = v.shape[0] // 2
    return jnp.concatenate([-v[half:], v[:half]], axis=0)


def widen(v):
    return jnp.concatenate([v, times_i(v)], axis=1)


def leaf_kernel(
    octant, parent, x_hbm, lift_hbm, inter, trans, table_hbm,
    message, plain, x_rows, dense,
    x_ref, rows, lift, oct_s, par_s, sems, inter_s, trans_s, table, more,
    *, parents, all_parents,
):
    boxes, halves, rhs, _ = x_ref.shape
    parts = halves * rhs
    reach = boxes // 2
    chunks = sems.shape[0] - 3
    per = boxes // chunks
    small = [
        pltpu.make_async_copy(x_hbm, x_ref, sems.at[chunks]),
        pltpu.make_async_copy(octant, oct_s, sems.at[chunks + 1]),
        pltpu.make_async_copy(parent, par_s, sems.at[chunks + 2]),
    ]
    big = [
        pltpu.make_async_copy(
            lift_hbm.at[pl.ds(i * per, per)], lift.at[pl.ds(i * per, per)], sems.at[i]
        )
        for i in range(chunks)
    ]
    for copy in small + big:
        copy.start()
    start, finish = fill_dense(
        dense, inter, trans, table_hbm, inter_s, trans_s, table, more, parents, all_parents
    )
    pl.when(odd_box())(start)
    for copy in small:
        copy.wait()
    own = [
        jnp.concatenate([x_ref[n, 0].astype(F32), x_ref[n, 1].astype(F32)], axis=0)
        for n in range(boxes)
    ]
    lane = lax.rem(lax.broadcasted_iota(jnp.int32, (boxes, LANES), 1), boxes)
    codes = jnp.zeros((boxes, LANES), F32)
    for n in range(boxes):
        slot = (oct_s[n] * parents + lax.rem(par_s[n], parents)).astype(F32)
        codes = jnp.where(lane == n, slot, codes)
    codes = codes[:CODE_ROWS].astype(BF16)
    x_rows[...] = jnp.concatenate(own, axis=0).astype(BF16)
    first = jnp.concatenate(own[:reach], axis=0)
    last = jnp.concatenate(own[reach:], axis=0)
    at = parts * boxes
    halo = first.shape[0]
    message[at + CODE_ROWS : at + CODE_ROWS + halo] = first.astype(BF16)
    message[at + CODE_ROWS + halo :] = last.astype(BF16)
    for ref in (plain, message):
        ref[at : at + CODE_ROWS] = codes
    for n in range(boxes):
        if n % per == 0:
            big[n // per].wait()
        mat = jnp.concatenate([lift[n, 0], lift[n, 1]], axis=1)
        rows[pl.ds(n, parts, stride=boxes), :] = nt_dot(widen(own[n]).astype(BF16), mat)
    pattern = rows[...].astype(BF16)
    for ref in (plain, message):
        ref[:at] = pattern
    pl.when(odd_box())(finish)


def up_kernel(*refs, pieces, boxes, parents, parts):
    msgs = refs[:pieces]
    interp_ref, phase_ref, after, out_ref, out_copy, place_ref, raised, folded = refs[pieces:]
    forward = msgs[1]
    slots = 8 * parents
    samples = raised.shape[1]
    first = lax.axis_index("samp") * samples
    mine = interp_ref[pl.ds(pl.multiple_of(first, samples), samples)]
    per_tile = LANES // boxes
    at = parts * boxes
    tiles = []
    for t in range(0, pieces, per_tile):
        lane = lax.broadcasted_iota(jnp.int32, (CODE_ROWS, LANES), 1) // boxes
        code = msgs[t][at : at + CODE_ROWS].astype(F32)
        for d in range(1, min(per_tile, pieces - t)):
            code = jnp.where(lane == d, msgs[t + d][at : at + CODE_ROWS].astype(F32), code)
        code = jnp.concatenate([code] * (slots // CODE_ROWS), axis=0)
        want = lax.broadcasted_iota(jnp.int32, (slots, LANES), 0).astype(F32)
        width = min(per_tile, pieces - t) * boxes
        tiles.append(jnp.where(code == want, 1.0, 0.0)[:, :width])
    sorter = jnp.concatenate(tiles, axis=1)
    place_ref[...] = sorter.T.astype(BF16)
    sorter = sorter.astype(BF16)
    pats = jnp.concatenate(
        [
            jnp.concatenate([m[c * boxes : (c + 1) * boxes] for m in msgs], axis=0)
            for c in range(parts)
        ],
        axis=1,
    )
    ordered = nn_dot(sorter, pats).astype(BF16)
    stacked = jnp.concatenate(
        [ordered[:, c * LANES : (c + 1) * LANES] for c in range(parts)], axis=0
    )
    raised[...] = nt_dot(stacked, mine)
    half = parts // 2
    for t in range(samples // LANES):
        lanes = slice(t * LANES, (t + 1) * LANES)
        here = pl.ds(pl.multiple_of(first + t * LANES, LANES), LANES)
        for r in range(half):
            re = im = None
            for o in range(8):
                ph_r = phase_ref[o, 0:1, here]
                ph_i = phase_ref[o, 1:2, here]
                base_r = r * slots + o * parents
                base_i = (half + r) * slots + o * parents
                xr = raised[base_r : base_r + parents, lanes]
                xi = raised[base_i : base_i + parents, lanes]
                dr = ph_r * xr - ph_i * xi
                di = ph_r * xi + ph_i * xr
                re = dr if re is None else re + dr
                im = di if im is None else im + di
            folded[t, r * parents : (r + 1) * parents] = re
            folded[t, (half + r) * parents : (half + r + 1) * parents] = im
        for p in range(0, parents, 2):
            both = jnp.concatenate(
                [folded[t, pl.ds(p + e, parts, stride=parents), :] for e in range(2)], axis=0
            )
            both = both.astype(BF16)
            for ref in (out_ref, out_copy):
                ref[p * parts : (p + 2) * parts, lanes] = both
        extra = out_ref.shape[0] - parents * parts
        start = forward.shape[0] - extra * (samples // LANES - t)
        for ref in (out_ref, out_copy):
            ref[parents * parts :, lanes] = forward[start : start + extra]


def zone(parents):
    return [d for d in range(-parents, parents + 1) if abs(d) >= 2]


def fill_dense(dense, inter_hbm, trans_hbm, table_hbm, inter, trans, table, sems, parents, all_parents):
    copies = [
        pltpu.make_async_copy(inter_hbm, inter, sems.at[0]),
        pltpu.make_async_copy(trans_hbm, trans, sems.at[1]),
        pltpu.make_async_copy(table_hbm, table, sems.at[2]),
    ]
    first = lax.axis_index("box") * parents

    def start():
        for copy in copies:
            copy.start()

    def finish():
        for copy in copies:
            copy.wait()
        if len(zone(parents)) > inter.shape[1]:
            dense[...] = jnp.zeros_like(dense)

        def fill(p, carry):
            for k in range(inter.shape[1]):
                rel = lax.rem(inter[p, k] - first - p + parents + all_parents, all_parents)
                at = jnp.where(rel < parents, rel, rel - 3)
                dense[p, at] = table[trans[p, k]]
            return carry

        lax.fori_loop(0, parents, fill, 0)

    return start, finish


def odd_box():
    return lax.rem(lax.axis_index("box"), 2) == 1


def prep_kernel(
    inter, trans, neighbours, table_hbm, mats_hbm, dense_in, after, dense, nbr,
    inter_s, trans_s, table, sems, *, parents, all_parents,
):
    copy = pltpu.make_async_copy(neighbours, nbr, sems.at[3])
    copy.start()
    start, finish = fill_dense(
        dense, inter, trans, table_hbm, inter_s, trans_s, table, sems, parents, all_parents
    )

    @pl.when(jnp.logical_not(odd_box()))
    def _():
        start()
        finish()

    copy.wait()


def down_kernel(
    own, across, beside, dense, interp_ref, phase_ref, place_ref, after, *refs, pieces, boxes, parents, parts
):
    outs = refs[:pieces]
    window, incoming, shifted = refs[pieces:]
    samples = window.shape[2]
    first = lax.axis_index("samp") * samples
    mine = interp_ref[pl.ds(pl.multiple_of(first, samples), samples)]
    slots = 8 * parents
    half = parts // 2
    odd = lax.rem(lax.axis_index("box"), 2)
    rows = parents * parts
    window[parents : 2 * parents] = own[:rows].astype(F32).reshape(parents, parts, samples)
    window[pl.ds(2 * parents * odd, parents)] = (
        across[:rows].astype(F32).reshape(parents, parts, samples)
    )
    window[pl.ds(2 * parents * (1 - odd), parents)] = (
        beside[:rows].astype(F32).reshape(parents, parts, samples)
    )
    offsets = zone(parents)

    def one(p, t, source):
        lanes = slice(t * LANES, (t + 1) * LANES)
        acc_r = acc_i = None
        for i, d in enumerate(offsets):
            x = source(p + d)
            yr = dense[p, i, 0:1, lanes] * x
            yi = dense[p, i, 1:2, lanes] * x
            acc_r = yr if acc_r is None else acc_r + yr
            acc_i = yi if acc_i is None else acc_i + yi
        got = (acc_r + times_i(acc_i)).astype(BF16).astype(F32)
        incoming[t, pl.ds(p * parts, parts), :] = got

    for t in range(samples // LANES):
        lanes = slice(t * LANES, (t + 1) * LANES)
        if parents <= 8:
            held = [window[j, :, lanes] for j in range(3 * parents)]
            for p in range(parents):
                one(p, t, lambda j: held[parents + j])
        else:
            lax.fori_loop(
                0,
                parents,
                lambda p, c: (one(p, t, lambda j: window[parents + j, :, lanes]), c)[1],
                0,
            )
    for t in range(samples // LANES):
        lanes = slice(t * LANES, (t + 1) * LANES)
        here = pl.ds(pl.multiple_of(first + t * LANES, LANES), LANES)
        for r in range(half):
            ir = incoming[t, pl.ds(r, parents, stride=parts), :]
            ii = incoming[t, pl.ds(half + r, parents, stride=parts), :]
            re, im = [], []
            for o in range(8):
                ph_r = phase_ref[o, 0:1, here]
                ph_i = phase_ref[o, 1:2, here]
                re.append(ph_r * ir - ph_i * ii)
                im.append(ph_r * ii + ph_i * ir)
            shifted[r * slots : (r + 1) * slots, lanes] = jnp.concatenate(re, axis=0).astype(BF16)
            shifted[(half + r) * slots : (half + r + 1) * slots, lanes] = jnp.concatenate(
                im, axis=0
            ).astype(BF16)
    field = nn_dot(shifted[...], mine).astype(BF16)
    spread = jnp.concatenate([field[c * slots : (c + 1) * slots] for c in range(parts)], axis=1)
    leaves = nn_dot(place_ref[...], spread).astype(BF16)
    for d in range(pieces):
        for c in range(parts):
            outs[d][c * boxes : (c + 1) * boxes] = leaves[
                d * boxes : (d + 1) * boxes, c * LANES : (c + 1) * LANES
            ]


def near_kernel(*refs, late, nsamp, total, halo_rows, parent_rows):
    neighbours, own, mats, after, *halos, out_ref, window, nbr, sems = refs
    if late:
        across, beside, *from_far = halos
    else:
        (from_beside,) = halos
    list_copy = pltpu.make_async_copy(neighbours, nbr, sems.at[0])
    list_copy.start()
    count, parts, unknowns = out_ref.shape
    boxes = own.shape[0] // parts
    near_count = mats.shape[1]
    samp = lax.axis_index("samp")
    box = lax.axis_index("box")
    odd = lax.rem(samp, 2)
    first = count * (odd if late else 1 - odd)

    def piece(ref):
        return ref[ref.shape[0] - halo_rows :].astype(F32)

    if late:
        def forwarded(ref):
            return jnp.concatenate(
                [
                    ref[parent_rows:, t * LANES : (t + 1) * LANES].astype(F32)
                    for t in range(ref.shape[1] // LANES)
                ],
                axis=0,
            )

        partner = samp ^ (samp - 1 + 2 * odd)
        halo = piece(from_far[0])
        for i in range(1, len(from_far)):
            halo = jnp.where(partner == (4 << i) - 1, piece(from_far[i]), halo)
        box_odd = lax.rem(box, 2) == 1
        from_left = samp == 0
        passed = jnp.where(box_odd == from_left, forwarded(beside), forwarded(across))
        halo = jnp.where(jnp.logical_or(from_left, samp == nsamp - 1), passed, halo)
    else:
        halo = piece(from_beside)
    at = jnp.where(first > 0, boxes + count, 0)
    for i in range(count):
        window[at + i] = widen(halo[i * parts : (i + 1) * parts])
    mine = own[...].astype(F32)
    for i in range(boxes):
        window[count + i] = widen(mine[i * parts : (i + 1) * parts])
    list_copy.wait()
    base = (box * nsamp + samp) * boxes
    for i in range(count):
        acc = None
        for k in range(near_count):
            j = lax.rem(nbr[k, first + i] - base + count + total, total)
            mat = jnp.concatenate([mats[first + i, k, 0], mats[first + i, k, 1]], axis=1)
            y = nt_dot(window[j].astype(BF16), mat)
            acc = y if acc is None else acc + y
        out_ref[i] = acc


def final_kernel(*refs, pieces):
    parts_in = refs[:pieces]
    near_early, near_late, mats, out_ref, field = refs[pieces:]
    boxes, halves, rhs = out_ref.shape[:3]
    parts = halves * rhs
    half = boxes // 2
    odd = lax.rem(lax.axis_index("samp"), 2) == 1
    total = parts_in[0][...].astype(F32)
    for m in parts_in[1:]:
        total += m[...].astype(F32)
    field[...] = total.astype(BF16).astype(F32)
    for n in range(boxes):
        v = field[pl.ds(n, parts, stride=boxes), :]
        wide = jnp.concatenate([v, times_i(v)], axis=1).astype(BF16)
        y = nt_dot(wide, jnp.concatenate([mats[n, 0], mats[n, 1]], axis=1))
        i = n % half
        y = y + jnp.where(odd == (n < half), near_early[i], near_late[i])
        out_ref[n, 0] = y[:rhs]
        out_ref[n, 1] = y[rhs:]


def whole_in(kind):
    return pl.BlockSpec(memory_space=kind)


VM = pltpu.VMEM
SM = pltpu.SMEM
HBM = pltpu.HBM
DMA = pltpu.SemaphoreType.DMA
PARAMS = pltpu.CompilerParams(vmem_limit_bytes=24 * 1024 * 1024)


def stay(x):
    return pltpu.with_memory_space_constraint(x, HBM)


def on_device(
    xvec,
    near_blocks,
    neighbours,
    lift,
    place,
    interp,
    phases,
    octant,
    leaf_parent_index,
    translators,
    inter_list,
    trans_id,
):
    boxes, halves, rhs, unknowns = xvec.shape
    parts = halves * rhs
    nsamp = lax.axis_size("samp")
    nbox = lax.axis_size("box")
    total = boxes * nsamp * nbox
    reach = boxes // 2
    parents = boxes * nsamp // 8
    all_parents = parents * nbox
    samples = interp.shape[0] // nsamp
    slots = 8 * parents
    leaves = boxes * nsamp
    near_count = near_blocks.shape[1]
    halo_rows = reach * parts
    parent_rows = parents * parts
    plain_rows = parts * boxes + CODE_ROWS

    def shape(dims, dtype=BF16):
        return jax.ShapeDtypeStruct(dims, dtype)

    lift_chunks = 2
    message, plain, x_rows, dense = pl.pallas_call(
        lambda *refs: leaf_kernel(*refs, parents=parents, all_parents=all_parents),
        in_specs=[whole_in(HBM)] * 7,
        out_specs=[whole_in(VM)] * 4,
        out_shape=[
            shape((plain_rows + 2 * halo_rows, LANES)),
            shape((plain_rows, LANES)),
            shape((boxes * parts, LANES)),
            shape((parents, len(zone(parents)), 2, samples), F32),
        ],
        scratch_shapes=[
            VM(xvec.shape, BF16),
            VM((parts * boxes, LANES), F32),
            VM(lift.shape, BF16),
            SM((boxes,), jnp.int32),
            SM((boxes,), jnp.int32),
            DMA((lift_chunks + 3,)),
            SM(inter_list.shape, jnp.int32),
            SM(trans_id.shape, jnp.int32),
            VM(translators.shape, F32),
            DMA((3,)),
        ],
        compiler_params=PARAMS,
        name="leaf",
    )(
        *[stay(a) for a in (octant, leaf_parent_index, xvec, lift)],
        *[stay(a) for a in (inter_list, trans_id, translators)],
    )

    def exchange(x, d):
        return lax.ppermute(x, "samp", [(i, i ^ d) for i in range(nsamp)])

    order = [0, nsamp - 1, *range(1, nsamp - 1)]
    far = [(4 << i) - 1 for i in range(nsamp.bit_length() - 2)]
    gathered = lax.all_gather(message, "samp")
    samp = lax.axis_index("samp").astype(jnp.int32)
    messages = {0: plain}
    for d in order[1:]:
        got = lax.dynamic_index_in_dim(gathered, samp ^ d, 0, keepdims=False)
        if d == 1 or d in far:
            sender_odd = (samp ^ d) % 2
            take_last = 1 - sender_odd if d == 1 else sender_odd
            halo = lax.dynamic_slice_in_dim(got, plain_rows + halo_rows * take_last, halo_rows, 0)
            got = jnp.concatenate([got[:plain_rows], halo], axis=0)
        else:
            got = got[:plain_rows]
        messages[d] = got
    far_messages = [messages[d] for d in far]

    dense, near_list = pl.pallas_call(
        lambda *refs: prep_kernel(*refs, parents=parents, all_parents=all_parents),
        in_specs=[whole_in(HBM)] * 5 + [whole_in(VM)] * 2,
        out_specs=[whole_in(VM)] * 2,
        input_output_aliases={5: 0},
        out_shape=[
            shape((parents, len(zone(parents)), 2, samples), F32),
            shape((near_count, boxes), jnp.int32),
        ],
        scratch_shapes=[
            SM(inter_list.shape, jnp.int32),
            SM(trans_id.shape, jnp.int32),
            VM(translators.shape, F32),
            DMA((4,)),
        ],
        compiler_params=PARAMS,
        cost_estimate=pl.CostEstimate(
            flops=0, bytes_accessed=2 * near_blocks.size, transcendentals=0
        ),
        name="prep",
    )(
        stay(inter_list),
        stay(trans_id),
        stay(neighbours.T),
        stay(translators),
        stay(near_blocks),
        dense,
        x_rows,
    )

    to_across, parent_pat, place_onehot = pl.pallas_call(
        lambda *refs: up_kernel(
            *refs, pieces=nsamp, boxes=boxes, parents=parents, parts=parts
        ),
        in_specs=[whole_in(VM)] * (nsamp + 3),
        out_specs=[whole_in(VM)] * 3,
        out_shape=[
            shape((parent_rows + halo_rows * LANES // samples, samples)),
            shape((parent_rows + halo_rows * LANES // samples, samples)),
            shape((leaves, slots)),
        ],
        scratch_shapes=[
            VM((parts * slots, samples), F32),
            VM((samples // LANES, parent_rows, LANES), F32),
        ],
        compiler_params=PARAMS,
        name="up",
    )(*[messages[d] for d in order], interp, phases, near_list)

    across = lax.ppermute(
        to_across, "box", [(i, (i + (1 if i % 2 else -1)) % nbox) for i in range(nbox)]
    )
    beside = lax.ppermute(parent_pat, "box", [(i, i ^ 1) for i in range(nbox)])

    def near_half(late, args):
        return pl.pallas_call(
            lambda *refs: near_kernel(
                *refs,
                late=late,
                nsamp=nsamp,
                total=total,
                halo_rows=halo_rows,
                parent_rows=parent_rows,
            ),
            in_specs=[whole_in(VM)] * (3 + len(args)),
            out_specs=whole_in(VM),
            out_shape=shape((reach, parts, unknowns), F32),
            scratch_shapes=[
                VM((boxes + 2 * reach, parts, 2 * unknowns), F32),
                SM((near_count, boxes), jnp.int32),
                DMA((1,)),
            ],
            compiler_params=PARAMS,
            cost_estimate=pl.CostEstimate(
                flops=parts * near_blocks.size,
                bytes_accessed=near_blocks.size,
                transcendentals=0,
            ),
            name="near",
        )(near_list, x_rows, near_blocks, *args)

    near_early = near_half(False, [place_onehot, messages[1]])

    fields = pl.pallas_call(
        lambda *refs: down_kernel(
            *refs, pieces=nsamp, boxes=boxes, parents=parents, parts=parts
        ),
        in_specs=[whole_in(VM)] * 8,
        out_specs=[whole_in(VM)] * nsamp,
        out_shape=[shape((parts * boxes, LANES))] * nsamp,
        scratch_shapes=[
            VM((3 * parents, parts, samples), F32),
            VM((samples // LANES, parent_rows, LANES), F32),
            VM((parts * slots, samples), BF16),
        ],
        compiler_params=PARAMS,
        name="down",
    )(parent_pat, across, beside, dense, interp, phases, place_onehot, near_early)

    pieces = dict(zip(order, fields))
    partial = [pieces[0]] + [exchange(pieces[d], d) for d in reversed(range(1, nsamp))]

    near_late = near_half(True, [fields[0], across, beside, *far_messages])

    return pl.pallas_call(
        lambda *refs: final_kernel(*refs, pieces=nsamp),
        in_specs=[whole_in(VM)] * (nsamp + 3),
        out_specs=whole_in(VM),
        out_shape=shape(xvec.shape, F32),
        scratch_shapes=[VM((parts * boxes, LANES), F32)],
        compiler_params=PARAMS,
        name="final",
    )(*partial, near_early, near_late, place)


def solution(mesh):
    in_specs = (
        P(("box", "samp"), None, None, None),
        P(("box", "samp"), None, None, None, None),
        P(("box", "samp"), None),
        P(("box", "samp"), None, None, None),
        P(("box", "samp"), None, None, None),
        P(),
        P(),
        P(("box", "samp")),
        P(("box", "samp")),
        P(None, None, "samp"),
        P("box", None),
        P("box", None),
    )
    out_specs = P(("box", "samp"), None, None, None)
    return jax.shard_map(
        on_device, mesh=mesh, in_specs=in_specs, out_specs=out_specs, check_vma=False
    )
```

```python
import jax
import jax.numpy as jnp
from jax import lax
from jax.experimental import pallas as pl
from jax.experimental.pallas import tpu as pltpu
from jax.sharding import PartitionSpec as P

F32 = jnp.float32
BF16 = jnp.bfloat16
LANES = 128
CODE_ROWS = 8


def nt_dot(a, b):
    return lax.dot_general(a, b, (((1,), (1,)), ((), ())), preferred_element_type=F32)


def nn_dot(a, b):
    return lax.dot_general(a, b, (((1,), (0,)), ((), ())), preferred_element_type=F32)


def pair_dot(x0, x1, a0, a1):
    both = nt_dot(
        jnp.concatenate([x0, x1], axis=0).astype(BF16), jnp.concatenate([a0, a1], axis=0)
    )
    rows, cols = x0.shape[0], a0.shape[0]
    return both[:rows, :cols], both[rows:, cols:]


def abreast(a):
    return jnp.concatenate([a[0], a[1]], axis=1)


def times_i(v):
    half = v.shape[0] // 2
    return jnp.concatenate([-v[half:], v[:half]], axis=0)


def widen(v):
    return jnp.concatenate([v, times_i(v)], axis=1)


def leaf_kernel(
    octant, parent, x_hbm, lift_hbm, inter, trans, table_hbm,
    to_far, plain, to_beside, x_rows, dense,
    x_ref, rows, lift, oct_s, par_s, sems, inter_s, trans_s, table, more,
    *, parents, all_parents,
):
    boxes, halves, rhs, _ = x_ref.shape
    parts = halves * rhs
    reach = boxes // 2
    chunks = sems.shape[0] - 3
    per = boxes // chunks
    small = [
        pltpu.make_async_copy(x_hbm, x_ref, sems.at[chunks]),
        pltpu.make_async_copy(octant, oct_s, sems.at[chunks + 1]),
        pltpu.make_async_copy(parent, par_s, sems.at[chunks + 2]),
    ]
    big = [
        pltpu.make_async_copy(
            lift_hbm.at[pl.ds(i * per, per)], lift.at[pl.ds(i * per, per)], sems.at[i]
        )
        for i in range(chunks)
    ]
    for copy in small + big:
        copy.start()
    start, finish = fill_dense(
        dense, inter, trans, table_hbm, inter_s, trans_s, table, more, parents, all_parents
    )
    pl.when(odd_box())(start)
    for copy in small:
        copy.wait()
    own = [
        jnp.concatenate([x_ref[n, 0].astype(F32), x_ref[n, 1].astype(F32)], axis=0)
        for n in range(boxes)
    ]
    lane = lax.rem(lax.broadcasted_iota(jnp.int32, (boxes, LANES), 1), boxes)
    codes = jnp.zeros((boxes, LANES), F32)
    for n in range(boxes):
        slot = (oct_s[n] * parents + lax.rem(par_s[n], parents)).astype(F32)
        codes = jnp.where(lane == n, slot, codes)
    codes = codes[:CODE_ROWS].astype(BF16)
    x_rows[...] = jnp.concatenate(own, axis=0).astype(BF16)
    first = jnp.concatenate(own[:reach], axis=0)
    last = jnp.concatenate(own[reach:], axis=0)
    odd = lax.rem(lax.axis_index("samp"), 2) == 1
    at = parts * boxes
    to_beside[at + CODE_ROWS :] = jnp.where(odd, first, last).astype(BF16)
    to_far[at + CODE_ROWS :] = jnp.where(odd, last, first).astype(BF16)
    for ref in (plain, to_beside, to_far):
        ref[at : at + CODE_ROWS] = codes
    for n in range(0, boxes, 2):
        if n % per == 0:
            big[n // per].wait()
        y0, y1 = pair_dot(widen(own[n]), widen(own[n + 1]), abreast(lift[n]), abreast(lift[n + 1]))
        rows[pl.ds(n, parts, stride=boxes), :] = y0
        rows[pl.ds(n + 1, parts, stride=boxes), :] = y1
    pattern = rows[...].astype(BF16)
    for ref in (plain, to_beside, to_far):
        ref[:at] = pattern
    pl.when(odd_box())(finish)


def up_kernel(*refs, pieces, boxes, parents, parts):
    msgs = refs[:pieces]
    interp_ref, phase_ref, after, out_ref, out_copy, place_ref, raised, folded = refs[pieces:]
    forward = msgs[1]
    slots = 8 * parents
    samples = raised.shape[1]
    first = lax.axis_index("samp") * samples
    mine = interp_ref[pl.ds(pl.multiple_of(first, samples), samples)]
    per_tile = LANES // boxes
    at = parts * boxes
    tiles = []
    for t in range(0, pieces, per_tile):
        lane = lax.broadcasted_iota(jnp.int32, (CODE_ROWS, LANES), 1) // boxes
        code = msgs[t][at : at + CODE_ROWS].astype(F32)
        for d in range(1, min(per_tile, pieces - t)):
            code = jnp.where(lane == d, msgs[t + d][at : at + CODE_ROWS].astype(F32), code)
        code = jnp.concatenate([code] * (slots // CODE_ROWS), axis=0)
        want = lax.broadcasted_iota(jnp.int32, (slots, LANES), 0).astype(F32)
        width = min(per_tile, pieces - t) * boxes
        tiles.append(jnp.where(code == want, 1.0, 0.0)[:, :width])
    sorter = jnp.concatenate(tiles, axis=1)
    place_ref[...] = sorter.T.astype(BF16)
    sorter = sorter.astype(BF16)
    pats = jnp.concatenate(
        [
            jnp.concatenate([m[c * boxes : (c + 1) * boxes] for m in msgs], axis=0)
            for c in range(parts)
        ],
        axis=1,
    )
    ordered = nn_dot(sorter, pats).astype(BF16)
    stacked = jnp.concatenate(
        [ordered[:, c * LANES : (c + 1) * LANES] for c in range(parts)], axis=0
    )
    raised[...] = nt_dot(stacked, mine)
    half = parts // 2
    for t in range(samples // LANES):
        lanes = slice(t * LANES, (t + 1) * LANES)
        here = pl.ds(pl.multiple_of(first + t * LANES, LANES), LANES)
        for r in range(half):
            re = im = None
            for o in range(8):
                ph_r = phase_ref[o, 0:1, here]
                ph_i = phase_ref[o, 1:2, here]
                base_r = r * slots + o * parents
                base_i = (half + r) * slots + o * parents
                xr = raised[base_r : base_r + parents, lanes]
                xi = raised[base_i : base_i + parents, lanes]
                dr = ph_r * xr - ph_i * xi
                di = ph_r * xi + ph_i * xr
                re = dr if re is None else re + dr
                im = di if im is None else im + di
            folded[t, r * parents : (r + 1) * parents] = re
            folded[t, (half + r) * parents : (half + r + 1) * parents] = im
        for p in range(0, parents, 2):
            both = jnp.concatenate(
                [folded[t, pl.ds(p + e, parts, stride=parents), :] for e in range(2)], axis=0
            )
            both = both.astype(BF16)
            for ref in (out_ref, out_copy):
                ref[p * parts : (p + 2) * parts, lanes] = both
        extra = out_ref.shape[0] - parents * parts
        start = forward.shape[0] - extra * (samples // LANES - t)
        for ref in (out_ref, out_copy):
            ref[parents * parts :, lanes] = forward[start : start + extra]


def zone(parents):
    return [d for d in range(-parents, parents + 1) if abs(d) >= 2]


def fill_dense(dense, inter_hbm, trans_hbm, table_hbm, inter, trans, table, sems, parents, all_parents):
    copies = [
        pltpu.make_async_copy(inter_hbm, inter, sems.at[0]),
        pltpu.make_async_copy(trans_hbm, trans, sems.at[1]),
        pltpu.make_async_copy(table_hbm, table, sems.at[2]),
    ]
    first = lax.axis_index("box") * parents

    def start():
        for copy in copies:
            copy.start()

    def finish():
        for copy in copies:
            copy.wait()
        if len(zone(parents)) > inter.shape[1]:
            dense[...] = jnp.zeros_like(dense)

        def fill(p, carry):
            for k in range(inter.shape[1]):
                rel = lax.rem(inter[p, k] - first - p + parents + all_parents, all_parents)
                at = jnp.where(rel < parents, rel, rel - 3)
                dense[p, at] = table[trans[p, k]]
            return carry

        lax.fori_loop(0, parents, fill, 0)

    return start, finish


def odd_box():
    return lax.rem(lax.axis_index("box"), 2) == 1


def prep_kernel(
    inter, trans, neighbours, table_hbm, mats_hbm, dense_in, after, dense, nbr,
    inter_s, trans_s, table, sems, *, parents, all_parents,
):
    copy = pltpu.make_async_copy(neighbours, nbr, sems.at[3])
    copy.start()
    start, finish = fill_dense(
        dense, inter, trans, table_hbm, inter_s, trans_s, table, sems, parents, all_parents
    )

    @pl.when(jnp.logical_not(odd_box()))
    def _():
        start()
        finish()

    copy.wait()


def down_kernel(
    own, across, beside, dense, interp_ref, phase_ref, place_ref, after, *refs, pieces, boxes, parents, parts
):
    outs = refs[:pieces]
    window, incoming, shifted = refs[pieces:]
    samples = window.shape[2]
    first = lax.axis_index("samp") * samples
    mine = interp_ref[pl.ds(pl.multiple_of(first, samples), samples)]
    slots = 8 * parents
    half = parts // 2
    odd = lax.rem(lax.axis_index("box"), 2)
    rows = parents * parts
    window[parents : 2 * parents] = own[:rows].astype(F32).reshape(parents, parts, samples)
    window[pl.ds(2 * parents * odd, parents)] = (
        across[:rows].astype(F32).reshape(parents, parts, samples)
    )
    window[pl.ds(2 * parents * (1 - odd), parents)] = (
        beside[:rows].astype(F32).reshape(parents, parts, samples)
    )
    offsets = zone(parents)

    def one(p, t, source):
        lanes = slice(t * LANES, (t + 1) * LANES)
        acc_r = acc_i = None
        for i, d in enumerate(offsets):
            x = source(p + d)
            yr = dense[p, i, 0:1, lanes] * x
            yi = dense[p, i, 1:2, lanes] * x
            acc_r = yr if acc_r is None else acc_r + yr
            acc_i = yi if acc_i is None else acc_i + yi
        got = (acc_r + times_i(acc_i)).astype(BF16).astype(F32)
        incoming[t, pl.ds(p * parts, parts), :] = got

    for t in range(samples // LANES):
        lanes = slice(t * LANES, (t + 1) * LANES)
        if parents <= 8:
            held = [window[j, :, lanes] for j in range(3 * parents)]
            for p in range(parents):
                one(p, t, lambda j: held[parents + j])
        else:
            lax.fori_loop(
                0,
                parents,
                lambda p, c: (one(p, t, lambda j: window[parents + j, :, lanes]), c)[1],
                0,
            )
    for t in range(samples // LANES):
        lanes = slice(t * LANES, (t + 1) * LANES)
        here = pl.ds(pl.multiple_of(first + t * LANES, LANES), LANES)
        for r in range(half):
            ir = incoming[t, pl.ds(r, parents, stride=parts), :]
            ii = incoming[t, pl.ds(half + r, parents, stride=parts), :]
            re, im = [], []
            for o in range(8):
                ph_r = phase_ref[o, 0:1, here]
                ph_i = phase_ref[o, 1:2, here]
                re.append(ph_r * ir - ph_i * ii)
                im.append(ph_r * ii + ph_i * ir)
            shifted[r * slots : (r + 1) * slots, lanes] = jnp.concatenate(re, axis=0).astype(BF16)
            shifted[(half + r) * slots : (half + r + 1) * slots, lanes] = jnp.concatenate(
                im, axis=0
            ).astype(BF16)
    field = nn_dot(shifted[...], mine).astype(BF16)
    spread = jnp.concatenate([field[c * slots : (c + 1) * slots] for c in range(parts)], axis=1)
    leaves = nn_dot(place_ref[...], spread).astype(BF16)
    for d in range(pieces):
        for c in range(parts):
            outs[d][c * boxes : (c + 1) * boxes] = leaves[
                d * boxes : (d + 1) * boxes, c * LANES : (c + 1) * LANES
            ]


def near_kernel(*refs, late, nsamp, total, halo_rows, parent_rows):
    neighbours, own, mats, after, *halos, out_ref, window, nbr, sems = refs
    if late:
        across, beside, *from_far = halos
    else:
        (from_beside,) = halos
    list_copy = pltpu.make_async_copy(neighbours, nbr, sems.at[0])
    list_copy.start()
    count, parts, unknowns = out_ref.shape
    boxes = own.shape[0] // parts
    near_count = mats.shape[1]
    samp = lax.axis_index("samp")
    box = lax.axis_index("box")
    odd = lax.rem(samp, 2)
    first = count * (odd if late else 1 - odd)

    def piece(ref):
        return ref[ref.shape[0] - halo_rows :].astype(F32)

    if late:
        def forwarded(ref):
            return jnp.concatenate(
                [
                    ref[parent_rows:, t * LANES : (t + 1) * LANES].astype(F32)
                    for t in range(ref.shape[1] // LANES)
                ],
                axis=0,
            )

        partner = samp ^ (samp - 1 + 2 * odd)
        halo = piece(from_far[0])
        for i in range(1, len(from_far)):
            halo = jnp.where(partner == (4 << i) - 1, piece(from_far[i]), halo)
        box_odd = lax.rem(box, 2) == 1
        from_left = samp == 0
        passed = jnp.where(box_odd == from_left, forwarded(beside), forwarded(across))
        halo = jnp.where(jnp.logical_or(from_left, samp == nsamp - 1), passed, halo)
    else:
        halo = piece(from_beside)
    at = jnp.where(first > 0, boxes + count, 0)
    for i in range(count):
        window[at + i] = widen(halo[i * parts : (i + 1) * parts])
    mine = own[...].astype(F32)
    for i in range(boxes):
        window[count + i] = widen(mine[i * parts : (i + 1) * parts])
    list_copy.wait()
    base = (box * nsamp + samp) * boxes
    for i in range(count):
        acc = None
        for k in range(0, near_count, 2):
            j0, j1 = (
                lax.rem(nbr[k + e, first + i] - base + count + total, total) for e in range(2)
            )
            y0, y1 = pair_dot(
                window[j0], window[j1], abreast(mats[first + i, k]), abreast(mats[first + i, k + 1])
            )
            y = y0 + y1
            acc = y if acc is None else acc + y
        out_ref[i] = acc


def final_kernel(*refs, pieces):
    parts_in = refs[:pieces]
    near_early, near_late, mats, out_ref, field = refs[pieces:]
    boxes, halves, rhs = out_ref.shape[:3]
    parts = halves * rhs
    half = boxes // 2
    odd = lax.rem(lax.axis_index("samp"), 2) == 1
    total = parts_in[0][...].astype(F32)
    for m in parts_in[1:]:
        total += m[...].astype(F32)
    field[...] = total.astype(BF16).astype(F32)
    for n in range(0, boxes, 2):
        wide = [field[pl.ds(n + e, parts, stride=boxes), :] for e in range(2)]
        wide = [widen(v) for v in wide]
        for e, y in enumerate(pair_dot(*wide, abreast(mats[n]), abreast(mats[n + 1]))):
            i = (n + e) % half
            y = y + jnp.where(odd == (n < half), near_early[i], near_late[i])
            out_ref[n + e, 0] = y[:rhs]
            out_ref[n + e, 1] = y[rhs:]


def whole_in(kind):
    return pl.BlockSpec(memory_space=kind)


VM = pltpu.VMEM
SM = pltpu.SMEM
HBM = pltpu.HBM
DMA = pltpu.SemaphoreType.DMA
PARAMS = pltpu.CompilerParams(vmem_limit_bytes=24 * 1024 * 1024)


def stay(x):
    return pltpu.with_memory_space_constraint(x, HBM)


def on_device(
    xvec,
    near_blocks,
    neighbours,
    lift,
    place,
    interp,
    phases,
    octant,
    leaf_parent_index,
    translators,
    inter_list,
    trans_id,
):
    boxes, halves, rhs, unknowns = xvec.shape
    parts = halves * rhs
    nsamp = lax.axis_size("samp")
    nbox = lax.axis_size("box")
    total = boxes * nsamp * nbox
    reach = boxes // 2
    parents = boxes * nsamp // 8
    all_parents = parents * nbox
    samples = interp.shape[0] // nsamp
    slots = 8 * parents
    leaves = boxes * nsamp
    near_count = near_blocks.shape[1]
    halo_rows = reach * parts
    parent_rows = parents * parts
    plain_rows = parts * boxes + CODE_ROWS

    def shape(dims, dtype=BF16):
        return jax.ShapeDtypeStruct(dims, dtype)

    lift_chunks = 2
    to_far, plain, to_beside, x_rows, dense = pl.pallas_call(
        lambda *refs: leaf_kernel(*refs, parents=parents, all_parents=all_parents),
        in_specs=[whole_in(HBM)] * 7,
        out_specs=[whole_in(VM)] * 5,
        out_shape=[
            shape((plain_rows + halo_rows, LANES)),
            shape((plain_rows, LANES)),
            shape((plain_rows + halo_rows, LANES)),
            shape((boxes * parts, LANES)),
            shape((parents, len(zone(parents)), 2, samples), F32),
        ],
        scratch_shapes=[
            VM(xvec.shape, BF16),
            VM((parts * boxes, LANES), F32),
            VM(lift.shape, BF16),
            SM((boxes,), jnp.int32),
            SM((boxes,), jnp.int32),
            DMA((lift_chunks + 3,)),
            SM(inter_list.shape, jnp.int32),
            SM(trans_id.shape, jnp.int32),
            VM(translators.shape, F32),
            DMA((3,)),
        ],
        compiler_params=PARAMS,
        name="leaf",
    )(
        *[stay(a) for a in (octant, leaf_parent_index, xvec, lift)],
        *[stay(a) for a in (inter_list, trans_id, translators)],
    )

    def exchange(x, d):
        return lax.ppermute(x, "samp", [(i, i ^ d) for i in range(nsamp)])

    order = [0, nsamp - 1, *range(1, nsamp - 1)]
    far = [(4 << i) - 1 for i in range(nsamp.bit_length() - 2)]
    messages = {0: plain}
    for d in order[1:]:
        messages[d] = exchange(to_beside if d == 1 else to_far if d in far else plain, d)
    far_messages = [messages[d] for d in far]

    dense, near_list = pl.pallas_call(
        lambda *refs: prep_kernel(*refs, parents=parents, all_parents=all_parents),
        in_specs=[whole_in(HBM)] * 5 + [whole_in(VM)] * 2,
        out_specs=[whole_in(VM)] * 2,
        input_output_aliases={5: 0},
        out_shape=[
            shape((parents, len(zone(parents)), 2, samples), F32),
            shape((near_count, boxes), jnp.int32),
        ],
        scratch_shapes=[
            SM(inter_list.shape, jnp.int32),
            SM(trans_id.shape, jnp.int32),
            VM(translators.shape, F32),
            DMA((4,)),
        ],
        compiler_params=PARAMS,
        cost_estimate=pl.CostEstimate(
            flops=0, bytes_accessed=2 * near_blocks.size, transcendentals=0
        ),
        name="prep",
    )(
        stay(inter_list),
        stay(trans_id),
        stay(neighbours.T),
        stay(translators),
        stay(near_blocks),
        dense,
        x_rows,
    )

    to_across, parent_pat, place_onehot = pl.pallas_call(
        lambda *refs: up_kernel(
            *refs, pieces=nsamp, boxes=boxes, parents=parents, parts=parts
        ),
        in_specs=[whole_in(VM)] * (nsamp + 3),
        out_specs=[whole_in(VM)] * 3,
        out_shape=[
            shape((parent_rows + halo_rows * LANES // samples, samples)),
            shape((parent_rows + halo_rows * LANES // samples, samples)),
            shape((leaves, slots)),
        ],
        scratch_shapes=[
            VM((parts * slots, samples), F32),
            VM((samples // LANES, parent_rows, LANES), F32),
        ],
        compiler_params=PARAMS,
        name="up",
    )(*[messages[d] for d in order], interp, phases, near_list)

    across = lax.ppermute(
        to_across, "box", [(i, (i + (1 if i % 2 else -1)) % nbox) for i in range(nbox)]
    )
    beside = lax.ppermute(parent_pat, "box", [(i, i ^ 1) for i in range(nbox)])

    def near_half(late, args):
        return pl.pallas_call(
            lambda *refs: near_kernel(
                *refs,
                late=late,
                nsamp=nsamp,
                total=total,
                halo_rows=halo_rows,
                parent_rows=parent_rows,
            ),
            in_specs=[whole_in(VM)] * (3 + len(args)),
            out_specs=whole_in(VM),
            out_shape=shape((reach, parts, unknowns), F32),
            scratch_shapes=[
                VM((boxes + 2 * reach, parts, 2 * unknowns), F32),
                SM((near_count, boxes), jnp.int32),
                DMA((1,)),
            ],
            compiler_params=PARAMS,
            cost_estimate=pl.CostEstimate(
                flops=parts * near_blocks.size,
                bytes_accessed=near_blocks.size,
                transcendentals=0,
            ),
            name="near",
        )(near_list, x_rows, near_blocks, *args)

    near_early = near_half(False, [place_onehot, messages[1]])

    fields = pl.pallas_call(
        lambda *refs: down_kernel(
            *refs, pieces=nsamp, boxes=boxes, parents=parents, parts=parts
        ),
        in_specs=[whole_in(VM)] * 8,
        out_specs=[whole_in(VM)] * nsamp,
        out_shape=[shape((parts * boxes, LANES))] * nsamp,
        scratch_shapes=[
            VM((3 * parents, parts, samples), F32),
            VM((samples // LANES, parent_rows, LANES), F32),
            VM((parts * slots, samples), BF16),
        ],
        compiler_params=PARAMS,
        name="down",
    )(parent_pat, across, beside, dense, interp, phases, place_onehot, near_early)

    pieces = dict(zip(order, fields))
    partial = [pieces[0]] + [exchange(pieces[d], d) for d in reversed(range(1, nsamp))]

    near_late = near_half(True, [fields[0], across, beside, *far_messages])

    return pl.pallas_call(
        lambda *refs: final_kernel(*refs, pieces=nsamp),
        in_specs=[whole_in(VM)] * (nsamp + 3),
        out_specs=whole_in(VM),
        out_shape=shape(xvec.shape, F32),
        scratch_shapes=[VM((parts * boxes, LANES), F32)],
        compiler_params=PARAMS,
        name="final",
    )(*partial, near_early, near_late, place)


def solution(mesh):
    in_specs = (
        P(("box", "samp"), None, None, None),
        P(("box", "samp"), None, None, None, None),
        P(("box", "samp"), None),
        P(("box", "samp"), None, None, None),
        P(("box", "samp"), None, None, None),
        P(),
        P(),
        P(("box", "samp")),
        P(("box", "samp")),
        P(None, None, "samp"),
        P("box", None),
        P("box", None),
    )
    out_specs = P(("box", "samp"), None, None, None)
    return jax.shard_map(
        on_device, mesh=mesh, in_specs=in_specs, out_specs=out_specs, check_vma=False
    )
```

```python
import jax
import jax.numpy as jnp
from jax import lax
from jax.experimental import pallas as pl
from jax.experimental.pallas import tpu as pltpu
from jax.sharding import PartitionSpec as P

F32 = jnp.float32
BF16 = jnp.bfloat16
LANES = 128
CODE_ROWS = 8


def nt_dot(a, b):
    return lax.dot_general(a, b, (((1,), (1,)), ((), ())), preferred_element_type=F32)


def nn_dot(a, b):
    return lax.dot_general(a, b, (((1,), (0,)), ((), ())), preferred_element_type=F32)


def pair_dot(x0, x1, a0, a1):
    both = nt_dot(
        jnp.concatenate([x0, x1], axis=0).astype(BF16), jnp.concatenate([a0, a1], axis=0)
    )
    rows, cols = x0.shape[0], a0.shape[0]
    return both[:rows, :cols], both[rows:, cols:]


def abreast(a):
    return jnp.concatenate([a[0], a[1]], axis=1)


def times_i(v):
    half = v.shape[0] // 2
    return jnp.concatenate([-v[half:], v[:half]], axis=0)


def widen(v):
    return jnp.concatenate([v, times_i(v)], axis=1)


def leaf_kernel(
    octant, parent, x_hbm, lift_hbm, inter, trans, table_hbm,
    to_far, plain, to_beside, x_rows, dense,
    x_ref, rows, lift, oct_s, par_s, sems, inter_s, trans_s, table, more,
    *, parents, all_parents,
):
    boxes, halves, rhs, _ = x_ref.shape
    parts = halves * rhs
    reach = boxes // 2
    chunks = sems.shape[0] - 3
    per = boxes // chunks
    small = [
        pltpu.make_async_copy(x_hbm, x_ref, sems.at[chunks]),
        pltpu.make_async_copy(octant, oct_s, sems.at[chunks + 1]),
        pltpu.make_async_copy(parent, par_s, sems.at[chunks + 2]),
    ]
    big = [
        pltpu.make_async_copy(
            lift_hbm.at[pl.ds(i * per, per)], lift.at[pl.ds(i * per, per)], sems.at[i]
        )
        for i in range(chunks)
    ]
    for copy in small + big:
        copy.start()
    start, finish = fill_dense(
        dense, inter, trans, table_hbm, inter_s, trans_s, table, more, parents, all_parents
    )
    pl.when(odd_box())(start)
    for copy in small:
        copy.wait()
    own = [
        jnp.concatenate([x_ref[n, 0].astype(F32), x_ref[n, 1].astype(F32)], axis=0)
        for n in range(boxes)
    ]
    lane = lax.rem(lax.broadcasted_iota(jnp.int32, (boxes, LANES), 1), boxes)
    codes = jnp.zeros((boxes, LANES), F32)
    for n in range(boxes):
        slot = (oct_s[n] * parents + lax.rem(par_s[n], parents)).astype(F32)
        codes = jnp.where(lane == n, slot, codes)
    codes = codes[:CODE_ROWS].astype(BF16)
    x_rows[...] = jnp.concatenate(own, axis=0).astype(BF16)
    first = jnp.concatenate(own[:reach], axis=0)
    last = jnp.concatenate(own[reach:], axis=0)
    odd = lax.rem(lax.axis_index("samp"), 2) == 1
    at = parts * boxes
    to_beside[at + CODE_ROWS :] = jnp.where(odd, first, last).astype(BF16)
    to_far[at + CODE_ROWS :] = jnp.where(odd, last, first).astype(BF16)
    for ref in (plain, to_beside, to_far):
        ref[at : at + CODE_ROWS] = codes
    for n in range(0, boxes, 2):
        if n % per == 0:
            big[n // per].wait()
        y0, y1 = pair_dot(widen(own[n]), widen(own[n + 1]), abreast(lift[n]), abreast(lift[n + 1]))
        rows[pl.ds(n, parts, stride=boxes), :] = y0
        rows[pl.ds(n + 1, parts, stride=boxes), :] = y1
    pattern = rows[...].astype(BF16)
    for ref in (plain, to_beside, to_far):
        ref[:at] = pattern
    pl.when(odd_box())(finish)


def up_kernel(*refs, pieces, boxes, parents, parts):
    msgs = refs[:pieces]
    interp_ref, phase_ref, after, out_ref, out_copy, place_ref, raised, folded = refs[pieces:]
    forward = msgs[1]
    slots = 8 * parents
    samples = raised.shape[1]
    first = lax.axis_index("samp") * samples
    mine = interp_ref[pl.ds(pl.multiple_of(first, samples), samples)]
    per_tile = LANES // boxes
    at = parts * boxes
    tiles = []
    for t in range(0, pieces, per_tile):
        lane = lax.broadcasted_iota(jnp.int32, (CODE_ROWS, LANES), 1) // boxes
        code = msgs[t][at : at + CODE_ROWS].astype(F32)
        for d in range(1, min(per_tile, pieces - t)):
            code = jnp.where(lane == d, msgs[t + d][at : at + CODE_ROWS].astype(F32), code)
        code = jnp.concatenate([code] * (slots // CODE_ROWS), axis=0)
        want = lax.broadcasted_iota(jnp.int32, (slots, LANES), 0).astype(F32)
        width = min(per_tile, pieces - t) * boxes
        tiles.append(jnp.where(code == want, 1.0, 0.0)[:, :width])
    sorter = jnp.concatenate(tiles, axis=1)
    place_ref[...] = sorter.T.astype(BF16)
    sorter = sorter.astype(BF16)
    pats = jnp.concatenate(
        [
            jnp.concatenate([m[c * boxes : (c + 1) * boxes] for m in msgs], axis=0)
            for c in range(parts)
        ],
        axis=1,
    )
    ordered = nn_dot(sorter, pats).astype(BF16)
    stacked = jnp.concatenate(
        [ordered[:, c * LANES : (c + 1) * LANES] for c in range(parts)], axis=0
    )
    raised[...] = nt_dot(stacked, mine)
    half = parts // 2
    for t in range(samples // LANES):
        lanes = slice(t * LANES, (t + 1) * LANES)
        here = pl.ds(pl.multiple_of(first + t * LANES, LANES), LANES)
        for r in range(half):
            re = im = None
            for o in range(8):
                ph_r = phase_ref[o, 0:1, here]
                ph_i = phase_ref[o, 1:2, here]
                base_r = r * slots + o * parents
                base_i = (half + r) * slots + o * parents
                xr = raised[base_r : base_r + parents, lanes]
                xi = raised[base_i : base_i + parents, lanes]
                dr = ph_r * xr - ph_i * xi
                di = ph_r * xi + ph_i * xr
                re = dr if re is None else re + dr
                im = di if im is None else im + di
            folded[t, r * parents : (r + 1) * parents] = re
            folded[t, (half + r) * parents : (half + r + 1) * parents] = im
        for p in range(0, parents, 2):
            both = jnp.concatenate(
                [folded[t, pl.ds(p + e, parts, stride=parents), :] for e in range(2)], axis=0
            )
            both = both.astype(BF16)
            for ref in (out_ref, out_copy):
                ref[p * parts : (p + 2) * parts, lanes] = both
        extra = out_ref.shape[0] - parents * parts
        start = forward.shape[0] - extra * (samples // LANES - t)
        for ref in (out_ref, out_copy):
            ref[parents * parts :, lanes] = forward[start : start + extra]


def zone(parents):
    return [d for d in range(-parents, parents + 1) if abs(d) >= 2]


def fill_dense(dense, inter_hbm, trans_hbm, table_hbm, inter, trans, table, sems, parents, all_parents):
    copies = [
        pltpu.make_async_copy(inter_hbm, inter, sems.at[0]),
        pltpu.make_async_copy(trans_hbm, trans, sems.at[1]),
        pltpu.make_async_copy(table_hbm, table, sems.at[2]),
    ]
    first = lax.axis_index("box") * parents

    def start():
        for copy in copies:
            copy.start()

    def finish():
        for copy in copies:
            copy.wait()
        if len(zone(parents)) > inter.shape[1]:
            dense[...] = jnp.zeros_like(dense)

        def fill(p, carry):
            for k in range(inter.shape[1]):
                rel = lax.rem(inter[p, k] - first - p + parents + all_parents, all_parents)
                at = jnp.where(rel < parents, rel, rel - 3)
                dense[p, at] = table[trans[p, k]]
            return carry

        lax.fori_loop(0, parents, fill, 0)

    return start, finish


def odd_box():
    return lax.rem(lax.axis_index("box"), 2) == 1


def prep_kernel(
    inter, trans, neighbours, table_hbm, mats_hbm, dense_in, after, dense, nbr,
    inter_s, trans_s, table, sems, *, parents, all_parents,
):
    copy = pltpu.make_async_copy(neighbours, nbr, sems.at[3])
    copy.start()
    start, finish = fill_dense(
        dense, inter, trans, table_hbm, inter_s, trans_s, table, sems, parents, all_parents
    )

    @pl.when(jnp.logical_not(odd_box()))
    def _():
        start()
        finish()

    copy.wait()


def down_kernel(
    own, across, beside, dense, interp_ref, phase_ref, place_ref, after,
    neighbours, x_rows, mats, *refs, pieces, boxes, parents, parts, sizes
):
    far = len(refs) - pieces - 7
    from_far, refs = refs[:far], refs[far:]
    outs = refs[:pieces]
    near_out, window, incoming, shifted, near_window, nbr, sems = refs[pieces:]
    samples = window.shape[2]
    first = lax.axis_index("samp") * samples
    mine = interp_ref[pl.ds(pl.multiple_of(first, samples), samples)]
    slots = 8 * parents
    half = parts // 2
    odd = lax.rem(lax.axis_index("box"), 2)
    rows = parents * parts
    window[parents : 2 * parents] = own[:rows].astype(F32).reshape(parents, parts, samples)
    window[pl.ds(2 * parents * odd, parents)] = (
        across[:rows].astype(F32).reshape(parents, parts, samples)
    )
    window[pl.ds(2 * parents * (1 - odd), parents)] = (
        beside[:rows].astype(F32).reshape(parents, parts, samples)
    )
    offsets = zone(parents)

    def one(p, t, source):
        lanes = slice(t * LANES, (t + 1) * LANES)
        acc_r = acc_i = None
        for i, d in enumerate(offsets):
            x = source(p + d)
            yr = dense[p, i, 0:1, lanes] * x
            yi = dense[p, i, 1:2, lanes] * x
            acc_r = yr if acc_r is None else acc_r + yr
            acc_i = yi if acc_i is None else acc_i + yi
        got = (acc_r + times_i(acc_i)).astype(BF16).astype(F32)
        incoming[t, pl.ds(p * parts, parts), :] = got

    for t in range(samples // LANES):
        lanes = slice(t * LANES, (t + 1) * LANES)
        if parents <= 8:
            held = [window[j, :, lanes] for j in range(3 * parents)]
            for p in range(parents):
                one(p, t, lambda j: held[parents + j])
        else:
            lax.fori_loop(
                0,
                parents,
                lambda p, c: (one(p, t, lambda j: window[parents + j, :, lanes]), c)[1],
                0,
            )
    for t in range(samples // LANES):
        lanes = slice(t * LANES, (t + 1) * LANES)
        here = pl.ds(pl.multiple_of(first + t * LANES, LANES), LANES)
        for r in range(half):
            ir = incoming[t, pl.ds(r, parents, stride=parts), :]
            ii = incoming[t, pl.ds(half + r, parents, stride=parts), :]
            re, im = [], []
            for o in range(8):
                ph_r = phase_ref[o, 0:1, here]
                ph_i = phase_ref[o, 1:2, here]
                re.append(ph_r * ir - ph_i * ii)
                im.append(ph_r * ii + ph_i * ir)
            shifted[r * slots : (r + 1) * slots, lanes] = jnp.concatenate(re, axis=0).astype(BF16)
            shifted[(half + r) * slots : (half + r + 1) * slots, lanes] = jnp.concatenate(
                im, axis=0
            ).astype(BF16)
    field = nn_dot(shifted[...], mine).astype(BF16)
    spread = jnp.concatenate([field[c * slots : (c + 1) * slots] for c in range(parts)], axis=1)
    leaves = nn_dot(place_ref[...], spread).astype(BF16)
    for d in range(pieces):
        for c in range(parts):
            outs[d][c * boxes : (c + 1) * boxes] = leaves[
                d * boxes : (d + 1) * boxes, c * LANES : (c + 1) * LANES
            ]

    @pl.when(odd_box())
    def _():
        halos = (across, beside, *from_far)
        near_half_of(True, neighbours, x_rows, mats, halos, near_out, near_window, nbr, sems, **sizes)


def near_half_of(late, neighbours, own, mats, halos, out_ref, window, nbr, sems, nsamp, total, halo_rows, parent_rows):
    if late:
        across, beside, *from_far = halos
    else:
        (from_beside,) = halos
    list_copy = pltpu.make_async_copy(neighbours, nbr, sems.at[0])
    list_copy.start()
    count, parts, unknowns = out_ref.shape
    boxes = own.shape[0] // parts
    near_count = mats.shape[1]
    samp = lax.axis_index("samp")
    box = lax.axis_index("box")
    odd = lax.rem(samp, 2)
    first = count * (odd if late else 1 - odd)

    def piece(ref):
        return ref[ref.shape[0] - halo_rows :].astype(F32)

    if late:
        def forwarded(ref):
            return jnp.concatenate(
                [
                    ref[parent_rows:, t * LANES : (t + 1) * LANES].astype(F32)
                    for t in range(ref.shape[1] // LANES)
                ],
                axis=0,
            )

        partner = samp ^ (samp - 1 + 2 * odd)
        halo = piece(from_far[0])
        for i in range(1, len(from_far)):
            halo = jnp.where(partner == (4 << i) - 1, piece(from_far[i]), halo)
        box_odd = lax.rem(box, 2) == 1
        from_left = samp == 0
        passed = jnp.where(box_odd == from_left, forwarded(beside), forwarded(across))
        halo = jnp.where(jnp.logical_or(from_left, samp == nsamp - 1), passed, halo)
    else:
        halo = piece(from_beside)
    at = jnp.where(first > 0, boxes + count, 0)
    for i in range(count):
        window[at + i] = widen(halo[i * parts : (i + 1) * parts])
    mine = own[...].astype(F32)
    for i in range(boxes):
        window[count + i] = widen(mine[i * parts : (i + 1) * parts])
    list_copy.wait()
    base = (box * nsamp + samp) * boxes
    for i in range(count):
        acc = None
        for k in range(0, near_count, 2):
            j0, j1 = (
                lax.rem(nbr[k + e, first + i] - base + count + total, total) for e in range(2)
            )
            y0, y1 = pair_dot(
                window[j0], window[j1], abreast(mats[first + i, k]), abreast(mats[first + i, k + 1])
            )
            y = y0 + y1
            acc = y if acc is None else acc + y
        out_ref[i] = acc


def near_kernel(*refs, late, **sizes):
    if not late:
        neighbours, own, mats, after, *halos, out_ref, window, nbr, sems = refs
        near_half_of(late, neighbours, own, mats, halos, out_ref, window, nbr, sems, **sizes)
        return
    neighbours, own, mats, done_in, *halos, out_ref, window, nbr, sems = refs

    @pl.when(jnp.logical_not(odd_box()))
    def _():
        near_half_of(late, neighbours, own, mats, halos, out_ref, window, nbr, sems, **sizes)


def final_kernel(*refs, pieces):
    parts_in = refs[:pieces]
    near_early, near_late, mats, out_ref, field = refs[pieces:]
    boxes, halves, rhs = out_ref.shape[:3]
    parts = halves * rhs
    half = boxes // 2
    odd = lax.rem(lax.axis_index("samp"), 2) == 1
    total = parts_in[0][...].astype(F32)
    for m in parts_in[1:]:
        total += m[...].astype(F32)
    field[...] = total.astype(BF16).astype(F32)
    for n in range(0, boxes, 2):
        wide = [field[pl.ds(n + e, parts, stride=boxes), :] for e in range(2)]
        wide = [widen(v) for v in wide]
        for e, y in enumerate(pair_dot(*wide, abreast(mats[n]), abreast(mats[n + 1]))):
            i = (n + e) % half
            y = y + jnp.where(odd == (n < half), near_early[i], near_late[i])
            out_ref[n + e, 0] = y[:rhs]
            out_ref[n + e, 1] = y[rhs:]


def whole_in(kind):
    return pl.BlockSpec(memory_space=kind)


VM = pltpu.VMEM
SM = pltpu.SMEM
HBM = pltpu.HBM
DMA = pltpu.SemaphoreType.DMA
PARAMS = pltpu.CompilerParams(vmem_limit_bytes=24 * 1024 * 1024)


def stay(x):
    return pltpu.with_memory_space_constraint(x, HBM)


def on_device(
    xvec,
    near_blocks,
    neighbours,
    lift,
    place,
    interp,
    phases,
    octant,
    leaf_parent_index,
    translators,
    inter_list,
    trans_id,
):
    boxes, halves, rhs, unknowns = xvec.shape
    parts = halves * rhs
    nsamp = lax.axis_size("samp")
    nbox = lax.axis_size("box")
    total = boxes * nsamp * nbox
    reach = boxes // 2
    parents = boxes * nsamp // 8
    all_parents = parents * nbox
    samples = interp.shape[0] // nsamp
    slots = 8 * parents
    leaves = boxes * nsamp
    near_count = near_blocks.shape[1]
    halo_rows = reach * parts
    parent_rows = parents * parts
    plain_rows = parts * boxes + CODE_ROWS

    def shape(dims, dtype=BF16):
        return jax.ShapeDtypeStruct(dims, dtype)

    lift_chunks = 2
    to_far, plain, to_beside, x_rows, dense = pl.pallas_call(
        lambda *refs: leaf_kernel(*refs, parents=parents, all_parents=all_parents),
        in_specs=[whole_in(HBM)] * 7,
        out_specs=[whole_in(VM)] * 5,
        out_shape=[
            shape((plain_rows + halo_rows, LANES)),
            shape((plain_rows, LANES)),
            shape((plain_rows + halo_rows, LANES)),
            shape((boxes * parts, LANES)),
            shape((parents, len(zone(parents)), 2, samples), F32),
        ],
        scratch_shapes=[
            VM(xvec.shape, BF16),
            VM((parts * boxes, LANES), F32),
            VM(lift.shape, BF16),
            SM((boxes,), jnp.int32),
            SM((boxes,), jnp.int32),
            DMA((lift_chunks + 3,)),
            SM(inter_list.shape, jnp.int32),
            SM(trans_id.shape, jnp.int32),
            VM(translators.shape, F32),
            DMA((3,)),
        ],
        compiler_params=PARAMS,
        name="leaf",
    )(
        *[stay(a) for a in (octant, leaf_parent_index, xvec, lift)],
        *[stay(a) for a in (inter_list, trans_id, translators)],
    )

    def exchange(x, d):
        return lax.ppermute(x, "samp", [(i, i ^ d) for i in range(nsamp)])

    order = [0, nsamp - 1, *range(1, nsamp - 1)]
    far = [(4 << i) - 1 for i in range(nsamp.bit_length() - 2)]
    messages = {0: plain}
    for d in order[1:]:
        messages[d] = exchange(to_beside if d == 1 else to_far if d in far else plain, d)
    far_messages = [messages[d] for d in far]

    dense, near_list = pl.pallas_call(
        lambda *refs: prep_kernel(*refs, parents=parents, all_parents=all_parents),
        in_specs=[whole_in(HBM)] * 5 + [whole_in(VM)] * 2,
        out_specs=[whole_in(VM)] * 2,
        input_output_aliases={5: 0},
        out_shape=[
            shape((parents, len(zone(parents)), 2, samples), F32),
            shape((near_count, boxes), jnp.int32),
        ],
        scratch_shapes=[
            SM(inter_list.shape, jnp.int32),
            SM(trans_id.shape, jnp.int32),
            VM(translators.shape, F32),
            DMA((4,)),
        ],
        compiler_params=PARAMS,
        cost_estimate=pl.CostEstimate(
            flops=0, bytes_accessed=2 * near_blocks.size, transcendentals=0
        ),
        name="prep",
    )(
        stay(inter_list),
        stay(trans_id),
        stay(neighbours.T),
        stay(translators),
        stay(near_blocks),
        dense,
        x_rows,
    )

    to_across, parent_pat, place_onehot = pl.pallas_call(
        lambda *refs: up_kernel(
            *refs, pieces=nsamp, boxes=boxes, parents=parents, parts=parts
        ),
        in_specs=[whole_in(VM)] * (nsamp + 3),
        out_specs=[whole_in(VM)] * 3,
        out_shape=[
            shape((parent_rows + halo_rows * LANES // samples, samples)),
            shape((parent_rows + halo_rows * LANES // samples, samples)),
            shape((leaves, slots)),
        ],
        scratch_shapes=[
            VM((parts * slots, samples), F32),
            VM((samples // LANES, parent_rows, LANES), F32),
        ],
        compiler_params=PARAMS,
        name="up",
    )(*[messages[d] for d in order], interp, phases, near_list)

    across = lax.ppermute(
        to_across, "box", [(i, (i + (1 if i % 2 else -1)) % nbox) for i in range(nbox)]
    )
    beside = lax.ppermute(parent_pat, "box", [(i, i ^ 1) for i in range(nbox)])

    sizes = dict(nsamp=nsamp, total=total, halo_rows=halo_rows, parent_rows=parent_rows)
    near_scratch = [
        VM((boxes + 2 * reach, parts, 2 * unknowns), F32),
        SM((near_count, boxes), jnp.int32),
        DMA((1,)),
    ]

    def near_half(late, args):
        return pl.pallas_call(
            lambda *refs: near_kernel(*refs, late=late, **sizes),
            in_specs=[whole_in(VM)] * (3 + len(args)),
            out_specs=whole_in(VM),
            out_shape=shape((reach, parts, unknowns), F32),
            input_output_aliases={3: 0} if late else {},
            scratch_shapes=near_scratch,
            compiler_params=PARAMS,
            cost_estimate=pl.CostEstimate(
                flops=parts * near_blocks.size,
                bytes_accessed=near_blocks.size,
                transcendentals=0,
            ),
            name="near",
        )(near_list, x_rows, near_blocks, *args)

    near_early = near_half(False, [place_onehot, messages[1]])

    *fields, near_done = pl.pallas_call(
        lambda *refs: down_kernel(
            *refs, pieces=nsamp, boxes=boxes, parents=parents, parts=parts, sizes=sizes
        ),
        in_specs=[whole_in(VM)] * (11 + len(far_messages)),
        out_specs=[whole_in(VM)] * (nsamp + 1),
        out_shape=[shape((parts * boxes, LANES))] * nsamp
        + [shape((reach, parts, unknowns), F32)],
        scratch_shapes=[
            VM((3 * parents, parts, samples), F32),
            VM((samples // LANES, parent_rows, LANES), F32),
            VM((parts * slots, samples), BF16),
            *near_scratch,
        ],
        compiler_params=PARAMS,
        name="down",
    )(
        parent_pat,
        across,
        beside,
        dense,
        interp,
        phases,
        place_onehot,
        near_early,
        near_list,
        x_rows,
        near_blocks,
        *far_messages,
    )

    pieces = dict(zip(order, fields))
    partial = [pieces[0]] + [exchange(pieces[d], d) for d in reversed(range(1, nsamp))]

    near_late = near_half(True, [near_done, across, beside, *far_messages])

    return pl.pallas_call(
        lambda *refs: final_kernel(*refs, pieces=nsamp),
        in_specs=[whole_in(VM)] * (nsamp + 3),
        out_specs=whole_in(VM),
        out_shape=shape(xvec.shape, F32),
        scratch_shapes=[VM((parts * boxes, LANES), F32)],
        compiler_params=PARAMS,
        name="final",
    )(*partial, near_early, near_late, place)


def solution(mesh):
    in_specs = (
        P(("box", "samp"), None, None, None),
        P(("box", "samp"), None, None, None, None),
        P(("box", "samp"), None),
        P(("box", "samp"), None, None, None),
        P(("box", "samp"), None, None, None),
        P(),
        P(),
        P(("box", "samp")),
        P(("box", "samp")),
        P(None, None, "samp"),
        P("box", None),
        P("box", None),
    )
    out_specs = P(("box", "samp"), None, None, None)
    return jax.shard_map(
        on_device, mesh=mesh, in_specs=in_specs, out_specs=out_specs, check_vma=False
    )
```

```python
import jax
import jax.numpy as jnp
from jax import lax
from jax.experimental import pallas as pl
from jax.experimental.pallas import tpu as pltpu
from jax.sharding import PartitionSpec as P

F32 = jnp.float32
BF16 = jnp.bfloat16
LANES = 128
CODE_ROWS = 16


def nt_dot(a, b):
    return lax.dot_general(a, b, (((1,), (1,)), ((), ())), preferred_element_type=F32)


def nn_dot(a, b):
    return lax.dot_general(a, b, (((1,), (0,)), ((), ())), preferred_element_type=F32)


def pair_dot(x0, x1, a0, a1):
    both = nt_dot(
        jnp.concatenate([x0, x1], axis=0).astype(BF16), jnp.concatenate([a0, a1], axis=0)
    )
    rows, cols = x0.shape[0], a0.shape[0]
    return both[:rows, :cols], both[rows:, cols:]


def abreast(a):
    return jnp.concatenate([a[0], a[1]], axis=1)


def times_i(v):
    half = v.shape[0] // 2
    return jnp.concatenate([-v[half:], v[:half]], axis=0)


def widen(v):
    return jnp.concatenate([v, times_i(v)], axis=1)


def leaf_kernel(
    octant, parent, x_hbm, lift_hbm, inter, trans, table_hbm,
    to_far, plain, to_beside, x_rows, dense,
    x_ref, rows, lift, oct_s, par_s, sems, inter_s, trans_s, table, more,
    *, parents, all_parents,
):
    boxes, halves, rhs, _ = x_ref.shape
    parts = halves * rhs
    reach = boxes // 2
    chunks = sems.shape[0] - 3
    per = boxes // chunks
    small = [
        pltpu.make_async_copy(x_hbm, x_ref, sems.at[chunks]),
        pltpu.make_async_copy(octant, oct_s, sems.at[chunks + 1]),
        pltpu.make_async_copy(parent, par_s, sems.at[chunks + 2]),
    ]
    big = [
        pltpu.make_async_copy(
            lift_hbm.at[pl.ds(i * per, per)], lift.at[pl.ds(i * per, per)], sems.at[i]
        )
        for i in range(chunks)
    ]
    for copy in small + big:
        copy.start()
    start, finish = fill_dense(
        dense, inter, trans, table_hbm, inter_s, trans_s, table, more, parents, all_parents
    )
    pl.when(odd_box())(start)
    for copy in small:
        copy.wait()
    own = [
        jnp.concatenate([x_ref[n, 0].astype(F32), x_ref[n, 1].astype(F32)], axis=0)
        for n in range(boxes)
    ]
    lane = lax.rem(lax.broadcasted_iota(jnp.int32, (boxes, LANES), 1), boxes)
    codes = jnp.zeros((boxes, LANES), F32)
    for n in range(boxes):
        slot = (oct_s[n] * parents + lax.rem(par_s[n], parents)).astype(F32)
        codes = jnp.where(lane == n, slot, codes)
    codes = codes[:CODE_ROWS].astype(BF16)
    x_rows[...] = jnp.concatenate(own, axis=0).astype(BF16)
    first = jnp.concatenate(own[:reach], axis=0)
    last = jnp.concatenate(own[reach:], axis=0)
    odd = lax.rem(lax.axis_index("samp"), 2) == 1
    at = parts * boxes
    to_beside[at + CODE_ROWS :] = jnp.where(odd, first, last).astype(BF16)
    to_far[at + CODE_ROWS :] = jnp.where(odd, last, first).astype(BF16)
    for ref in (plain, to_beside, to_far):
        ref[at : at + CODE_ROWS] = codes
    for n in range(0, boxes, 2):
        if n % per == 0:
            big[n // per].wait()
        y0, y1 = pair_dot(widen(own[n]), widen(own[n + 1]), abreast(lift[n]), abreast(lift[n + 1]))
        rows[pl.ds(n, parts, stride=boxes), :] = y0
        rows[pl.ds(n + 1, parts, stride=boxes), :] = y1
    pattern = rows[...].astype(BF16)
    for ref in (plain, to_beside, to_far):
        ref[:at] = pattern
    pl.when(odd_box())(finish)


def up_kernel(*refs, pieces, boxes, parents, parts):
    msgs = refs[:pieces]
    interp_ref, phase_ref, after, out_ref, out_copy, place_ref, raised, folded = refs[pieces:]
    forward = msgs[1]
    slots = 8 * parents
    samples = raised.shape[1]
    first = lax.axis_index("samp") * samples
    mine = interp_ref[pl.ds(pl.multiple_of(first, samples), samples)]
    per_tile = LANES // boxes
    at = parts * boxes
    tiles = []
    for t in range(0, pieces, per_tile):
        lane = lax.broadcasted_iota(jnp.int32, (CODE_ROWS, LANES), 1) // boxes
        code = msgs[t][at : at + CODE_ROWS].astype(F32)
        for d in range(1, min(per_tile, pieces - t)):
            code = jnp.where(lane == d, msgs[t + d][at : at + CODE_ROWS].astype(F32), code)
        code = jnp.concatenate([code] * (slots // CODE_ROWS), axis=0)
        want = lax.broadcasted_iota(jnp.int32, (slots, LANES), 0).astype(F32)
        width = min(per_tile, pieces - t) * boxes
        tiles.append(jnp.where(code == want, 1.0, 0.0)[:, :width])
    sorter = jnp.concatenate(tiles, axis=1)
    place_ref[...] = sorter.T.astype(BF16)
    sorter = sorter.astype(BF16)
    pats = jnp.concatenate(
        [
            jnp.concatenate([m[c * boxes : (c + 1) * boxes] for m in msgs], axis=0)
            for c in range(parts)
        ],
        axis=1,
    )
    ordered = nn_dot(sorter, pats).astype(BF16)
    stacked = jnp.concatenate(
        [ordered[:, c * LANES : (c + 1) * LANES] for c in range(parts)], axis=0
    )
    raised[...] = nt_dot(stacked, mine)
    half = parts // 2
    for t in range(samples // LANES):
        lanes = slice(t * LANES, (t + 1) * LANES)
        here = pl.ds(pl.multiple_of(first + t * LANES, LANES), LANES)
        for r in range(half):
            re = im = None
            for o in range(8):
                ph_r = phase_ref[o, 0:1, here]
                ph_i = phase_ref[o, 1:2, here]
                base_r = r * slots + o * parents
                base_i = (half + r) * slots + o * parents
                xr = raised[base_r : base_r + parents, lanes]
                xi = raised[base_i : base_i + parents, lanes]
                dr = ph_r * xr - ph_i * xi
                di = ph_r * xi + ph_i * xr
                re = dr if re is None else re + dr
                im = di if im is None else im + di
            folded[t, r * parents : (r + 1) * parents] = re
            folded[t, (half + r) * parents : (half + r + 1) * parents] = im
        for p in range(0, parents, 2):
            both = jnp.concatenate(
                [folded[t, pl.ds(p + e, parts, stride=parents), :] for e in range(2)], axis=0
            )
            both = both.astype(BF16)
            for ref in (out_ref, out_copy):
                ref[p * parts : (p + 2) * parts, lanes] = both
        extra = out_ref.shape[0] - parents * parts
        start = forward.shape[0] - extra * (samples // LANES - t)
        for ref in (out_ref, out_copy):
            ref[parents * parts :, lanes] = forward[start : start + extra]


def zone(parents):
    return [d for d in range(-parents, parents + 1) if abs(d) >= 2]


def fill_dense(dense, inter_hbm, trans_hbm, table_hbm, inter, trans, table, sems, parents, all_parents):
    copies = [
        pltpu.make_async_copy(inter_hbm, inter, sems.at[0]),
        pltpu.make_async_copy(trans_hbm, trans, sems.at[1]),
        pltpu.make_async_copy(table_hbm, table, sems.at[2]),
    ]
    first = lax.axis_index("box") * parents

    def start():
        for copy in copies:
            copy.start()

    def finish():
        for copy in copies:
            copy.wait()
        if len(zone(parents)) > inter.shape[1]:
            dense[...] = jnp.zeros_like(dense)

        def fill(p, carry):
            for k in range(inter.shape[1]):
                rel = lax.rem(inter[p, k] - first - p + parents + all_parents, all_parents)
                at = jnp.where(rel < parents, rel, rel - 3)
                dense[p, at] = table[trans[p, k]]
            return carry

        lax.fori_loop(0, parents, fill, 0)

    return start, finish


def odd_box():
    return lax.rem(lax.axis_index("box"), 2) == 1


def prep_kernel(
    inter, trans, neighbours, table_hbm, mats_hbm, dense_in, after, dense, nbr,
    inter_s, trans_s, table, sems, *, parents, all_parents,
):
    copy = pltpu.make_async_copy(neighbours, nbr, sems.at[3])
    copy.start()
    start, finish = fill_dense(
        dense, inter, trans, table_hbm, inter_s, trans_s, table, sems, parents, all_parents
    )

    @pl.when(jnp.logical_not(odd_box()))
    def _():
        start()
        finish()

    copy.wait()


def down_kernel(
    own, across, beside, dense, interp_ref, phase_ref, place_ref, after, *refs, pieces, boxes, parents, parts
):
    outs = refs[:pieces]
    window, incoming, shifted = refs[pieces:]
    samples = window.shape[2]
    first = lax.axis_index("samp") * samples
    mine = interp_ref[pl.ds(pl.multiple_of(first, samples), samples)]
    slots = 8 * parents
    half = parts // 2
    odd = lax.rem(lax.axis_index("box"), 2)
    rows = parents * parts
    window[parents : 2 * parents] = own[:rows].astype(F32).reshape(parents, parts, samples)
    window[pl.ds(2 * parents * odd, parents)] = (
        across[:rows].astype(F32).reshape(parents, parts, samples)
    )
    window[pl.ds(2 * parents * (1 - odd), parents)] = (
        beside[:rows].astype(F32).reshape(parents, parts, samples)
    )
    offsets = zone(parents)

    def one(p, t, source):
        lanes = slice(t * LANES, (t + 1) * LANES)
        acc_r = acc_i = None
        for i, d in enumerate(offsets):
            x = source(p + d)
            yr = dense[p, i, 0:1, lanes] * x
            yi = dense[p, i, 1:2, lanes] * x
            acc_r = yr if acc_r is None else acc_r + yr
            acc_i = yi if acc_i is None else acc_i + yi
        got = (acc_r + times_i(acc_i)).astype(BF16).astype(F32)
        incoming[t, pl.ds(p * parts, parts), :] = got

    for t in range(samples // LANES):
        lanes = slice(t * LANES, (t + 1) * LANES)
        if parents <= 8:
            held = [window[j, :, lanes] for j in range(3 * parents)]
            for p in range(parents):
                one(p, t, lambda j: held[parents + j])
        else:
            lax.fori_loop(
                0,
                parents,
                lambda p, c: (one(p, t, lambda j: window[parents + j, :, lanes]), c)[1],
                0,
            )
    for t in range(samples // LANES):
        lanes = slice(t * LANES, (t + 1) * LANES)
        here = pl.ds(pl.multiple_of(first + t * LANES, LANES), LANES)
        for r in range(half):
            ir = incoming[t, pl.ds(r, parents, stride=parts), :]
            ii = incoming[t, pl.ds(half + r, parents, stride=parts), :]
            re, im = [], []
            for o in range(8):
                ph_r = phase_ref[o, 0:1, here]
                ph_i = phase_ref[o, 1:2, here]
                re.append(ph_r * ir - ph_i * ii)
                im.append(ph_r * ii + ph_i * ir)
            shifted[r * slots : (r + 1) * slots, lanes] = jnp.concatenate(re, axis=0).astype(BF16)
            shifted[(half + r) * slots : (half + r + 1) * slots, lanes] = jnp.concatenate(
                im, axis=0
            ).astype(BF16)
    field = nn_dot(shifted[...], mine).astype(BF16)
    spread = jnp.concatenate([field[c * slots : (c + 1) * slots] for c in range(parts)], axis=1)
    leaves = nn_dot(place_ref[...], spread).astype(BF16)
    for d in range(pieces):
        for c in range(parts):
            outs[d][c * boxes : (c + 1) * boxes] = leaves[
                d * boxes : (d + 1) * boxes, c * LANES : (c + 1) * LANES
            ]


def near_kernel(*refs, late, nsamp, total, halo_rows, parent_rows):
    neighbours, own, mats, after, *halos, out_ref, window, nbr, sems = refs
    if late:
        across, beside, *from_far = halos
    else:
        (from_beside,) = halos
    list_copy = pltpu.make_async_copy(neighbours, nbr, sems.at[0])
    list_copy.start()
    count, parts, unknowns = out_ref.shape
    boxes = own.shape[0] // parts
    near_count = mats.shape[1]
    samp = lax.axis_index("samp")
    box = lax.axis_index("box")
    odd = lax.rem(samp, 2)
    first = count * (odd if late else 1 - odd)

    def piece(ref):
        return ref[ref.shape[0] - halo_rows :].astype(F32)

    if late:
        def forwarded(ref):
            return jnp.concatenate(
                [
                    ref[parent_rows:, t * LANES : (t + 1) * LANES].astype(F32)
                    for t in range(ref.shape[1] // LANES)
                ],
                axis=0,
            )

        partner = samp ^ (samp - 1 + 2 * odd)
        halo = piece(from_far[0])
        for i in range(1, len(from_far)):
            halo = jnp.where(partner == (4 << i) - 1, piece(from_far[i]), halo)
        box_odd = lax.rem(box, 2) == 1
        from_left = samp == 0
        passed = jnp.where(box_odd == from_left, forwarded(beside), forwarded(across))
        halo = jnp.where(jnp.logical_or(from_left, samp == nsamp - 1), passed, halo)
    else:
        halo = piece(from_beside)
    at = jnp.where(first > 0, boxes + count, 0)
    for i in range(count):
        window[at + i] = widen(halo[i * parts : (i + 1) * parts])
    mine = own[...].astype(F32)
    for i in range(boxes):
        window[count + i] = widen(mine[i * parts : (i + 1) * parts])
    list_copy.wait()
    base = (box * nsamp + samp) * boxes
    for i in range(count):
        acc = None
        for k in range(0, near_count, 2):
            j0, j1 = (
                lax.rem(nbr[k + e, first + i] - base + count + total, total) for e in range(2)
            )
            y0, y1 = pair_dot(
                window[j0], window[j1], abreast(mats[first + i, k]), abreast(mats[first + i, k + 1])
            )
            y = y0 + y1
            acc = y if acc is None else acc + y
        out_ref[i] = acc


def final_kernel(*refs, pieces):
    parts_in = refs[:pieces]
    near_early, near_late, mats, out_ref, field = refs[pieces:]
    boxes, halves, rhs = out_ref.shape[:3]
    parts = halves * rhs
    half = boxes // 2
    odd = lax.rem(lax.axis_index("samp"), 2) == 1
    total = parts_in[0][...].astype(F32)
    for m in parts_in[1:]:
        total += m[...].astype(F32)
    field[...] = total.astype(BF16).astype(F32)
    for n in range(0, boxes, 2):
        wide = [field[pl.ds(n + e, parts, stride=boxes), :] for e in range(2)]
        wide = [widen(v) for v in wide]
        for e, y in enumerate(pair_dot(*wide, abreast(mats[n]), abreast(mats[n + 1]))):
            i = (n + e) % half
            y = y + jnp.where(odd == (n < half), near_early[i], near_late[i])
            out_ref[n + e, 0] = y[:rhs]
            out_ref[n + e, 1] = y[rhs:]


def whole_in(kind):
    return pl.BlockSpec(memory_space=kind)


VM = pltpu.VMEM
SM = pltpu.SMEM
HBM = pltpu.HBM
DMA = pltpu.SemaphoreType.DMA
PARAMS = pltpu.CompilerParams(vmem_limit_bytes=24 * 1024 * 1024)


def stay(x):
    return pltpu.with_memory_space_constraint(x, HBM)


def on_device(
    xvec,
    near_blocks,
    neighbours,
    lift,
    place,
    interp,
    phases,
    octant,
    leaf_parent_index,
    translators,
    inter_list,
    trans_id,
):
    boxes, halves, rhs, unknowns = xvec.shape
    parts = halves * rhs
    nsamp = lax.axis_size("samp")
    nbox = lax.axis_size("box")
    total = boxes * nsamp * nbox
    reach = boxes // 2
    parents = boxes * nsamp // 8
    all_parents = parents * nbox
    samples = interp.shape[0] // nsamp
    slots = 8 * parents
    leaves = boxes * nsamp
    near_count = near_blocks.shape[1]
    halo_rows = reach * parts
    parent_rows = parents * parts
    plain_rows = parts * boxes + CODE_ROWS

    def shape(dims, dtype=BF16):
        return jax.ShapeDtypeStruct(dims, dtype)

    lift_chunks = 2
    to_far, plain, to_beside, x_rows, dense = pl.pallas_call(
        lambda *refs: leaf_kernel(*refs, parents=parents, all_parents=all_parents),
        in_specs=[whole_in(HBM)] * 7,
        out_specs=[whole_in(VM)] * 5,
        out_shape=[
            shape((plain_rows + halo_rows, LANES)),
            shape((plain_rows, LANES)),
            shape((plain_rows + halo_rows, LANES)),
            shape((boxes * parts, LANES)),
            shape((parents, len(zone(parents)), 2, samples), F32),
        ],
        scratch_shapes=[
            VM(xvec.shape, BF16),
            VM((parts * boxes, LANES), F32),
            VM(lift.shape, BF16),
            SM((boxes,), jnp.int32),
            SM((boxes,), jnp.int32),
            DMA((lift_chunks + 3,)),
            SM(inter_list.shape, jnp.int32),
            SM(trans_id.shape, jnp.int32),
            VM(translators.shape, F32),
            DMA((3,)),
        ],
        compiler_params=PARAMS,
        name="leaf",
    )(
        *[stay(a) for a in (octant, leaf_parent_index, xvec, lift)],
        *[stay(a) for a in (inter_list, trans_id, translators)],
    )

    def exchange(x, d):
        return lax.ppermute(x, "samp", [(i, i ^ d) for i in range(nsamp)])

    order = [0, nsamp - 1, *range(1, nsamp - 1)]
    far = [(4 << i) - 1 for i in range(nsamp.bit_length() - 2)]
    messages = {0: plain}
    for d in order[1:]:
        messages[d] = exchange(to_beside if d == 1 else to_far if d in far else plain, d)
    far_messages = [messages[d] for d in far]

    dense, near_list = pl.pallas_call(
        lambda *refs: prep_kernel(*refs, parents=parents, all_parents=all_parents),
        in_specs=[whole_in(HBM)] * 5 + [whole_in(VM)] * 2,
        out_specs=[whole_in(VM)] * 2,
        input_output_aliases={5: 0},
        out_shape=[
            shape((parents, len(zone(parents)), 2, samples), F32),
            shape((near_count, boxes), jnp.int32),
        ],
        scratch_shapes=[
            SM(inter_list.shape, jnp.int32),
            SM(trans_id.shape, jnp.int32),
            VM(translators.shape, F32),
            DMA((4,)),
        ],
        compiler_params=PARAMS,
        cost_estimate=pl.CostEstimate(
            flops=0, bytes_accessed=2 * near_blocks.size, transcendentals=0
        ),
        name="prep",
    )(
        stay(inter_list),
        stay(trans_id),
        stay(neighbours.T),
        stay(translators),
        stay(near_blocks),
        dense,
        x_rows,
    )

    to_across, parent_pat, place_onehot = pl.pallas_call(
        lambda *refs: up_kernel(
            *refs, pieces=nsamp, boxes=boxes, parents=parents, parts=parts
        ),
        in_specs=[whole_in(VM)] * (nsamp + 3),
        out_specs=[whole_in(VM)] * 3,
        out_shape=[
            shape((parent_rows + halo_rows * LANES // samples, samples)),
            shape((parent_rows + halo_rows * LANES // samples, samples)),
            shape((leaves, slots)),
        ],
        scratch_shapes=[
            VM((parts * slots, samples), F32),
            VM((samples // LANES, parent_rows, LANES), F32),
        ],
        compiler_params=PARAMS,
        name="up",
    )(*[messages[d] for d in order], interp, phases, near_list)

    across = lax.ppermute(
        to_across, "box", [(i, (i + (1 if i % 2 else -1)) % nbox) for i in range(nbox)]
    )
    beside = lax.ppermute(parent_pat, "box", [(i, i ^ 1) for i in range(nbox)])

    def near_half(late, args):
        return pl.pallas_call(
            lambda *refs: near_kernel(
                *refs,
                late=late,
                nsamp=nsamp,
                total=total,
                halo_rows=halo_rows,
                parent_rows=parent_rows,
            ),
            in_specs=[whole_in(VM)] * (3 + len(args)),
            out_specs=whole_in(VM),
            out_shape=shape((reach, parts, unknowns), F32),
            scratch_shapes=[
                VM((boxes + 2 * reach, parts, 2 * unknowns), F32),
                SM((near_count, boxes), jnp.int32),
                DMA((1,)),
            ],
            compiler_params=PARAMS,
            cost_estimate=pl.CostEstimate(
                flops=parts * near_blocks.size,
                bytes_accessed=near_blocks.size,
                transcendentals=0,
            ),
            name="near",
        )(near_list, x_rows, near_blocks, *args)

    near_early = near_half(False, [place_onehot, messages[1]])

    fields = pl.pallas_call(
        lambda *refs: down_kernel(
            *refs, pieces=nsamp, boxes=boxes, parents=parents, parts=parts
        ),
        in_specs=[whole_in(VM)] * 8,
        out_specs=[whole_in(VM)] * nsamp,
        out_shape=[shape((parts * boxes, LANES))] * nsamp,
        scratch_shapes=[
            VM((3 * parents, parts, samples), F32),
            VM((samples // LANES, parent_rows, LANES), F32),
            VM((parts * slots, samples), BF16),
        ],
        compiler_params=PARAMS,
        name="down",
    )(parent_pat, across, beside, dense, interp, phases, place_onehot, near_early)

    pieces = dict(zip(order, fields))
    partial = [pieces[0]] + [exchange(pieces[d], d) for d in reversed(range(1, nsamp))]

    near_late = near_half(True, [fields[0], across, beside, *far_messages])

    return pl.pallas_call(
        lambda *refs: final_kernel(*refs, pieces=nsamp),
        in_specs=[whole_in(VM)] * (nsamp + 3),
        out_specs=whole_in(VM),
        out_shape=shape(xvec.shape, F32),
        scratch_shapes=[VM((parts * boxes, LANES), F32)],
        compiler_params=PARAMS,
        name="final",
    )(*partial, near_early, near_late, place)


def solution(mesh):
    in_specs = (
        P(("box", "samp"), None, None, None),
        P(("box", "samp"), None, None, None, None),
        P(("box", "samp"), None),
        P(("box", "samp"), None, None, None),
        P(("box", "samp"), None, None, None),
        P(),
        P(),
        P(("box", "samp")),
        P(("box", "samp")),
        P(None, None, "samp"),
        P("box", None),
        P("box", None),
    )
    out_specs = P(("box", "samp"), None, None, None)
    return jax.shard_map(
        on_device, mesh=mesh, in_specs=in_specs, out_specs=out_specs, check_vma=False
    )
```

```python
import jax
import jax.numpy as jnp
from jax import lax
from jax.experimental import pallas as pl
from jax.experimental.pallas import tpu as pltpu
from jax.sharding import PartitionSpec as P

F32 = jnp.float32
BF16 = jnp.bfloat16
LANES = 128
CODE_ROWS = 16


def nt_dot(a, b):
    return lax.dot_general(a, b, (((1,), (1,)), ((), ())), preferred_element_type=F32)


def nn_dot(a, b):
    return lax.dot_general(a, b, (((1,), (0,)), ((), ())), preferred_element_type=F32)


def pair_dot(x0, x1, a0, a1):
    both = nt_dot(
        jnp.concatenate([x0, x1], axis=0).astype(BF16), jnp.concatenate([a0, a1], axis=0)
    )
    rows, cols = x0.shape[0], a0.shape[0]
    return both[:rows, :cols], both[rows:, cols:]


def abreast(a):
    return jnp.concatenate([a[0], a[1]], axis=1)


def times_i(v):
    half = v.shape[0] // 2
    return jnp.concatenate([-v[half:], v[:half]], axis=0)


def widen(v):
    return jnp.concatenate([v, times_i(v)], axis=1)


def leaf_kernel(
    octant, parent, x_hbm, lift_hbm, inter, trans, table_hbm,
    to_far, plain, to_beside, x_rows, dense,
    x_ref, rows, lift, oct_s, par_s, sems, inter_s, trans_s, table, more,
    *, parents, all_parents,
):
    boxes, halves, rhs, _ = x_ref.shape
    parts = halves * rhs
    reach = boxes // 2
    chunks = sems.shape[0] - 3
    per = boxes // chunks
    small = [
        pltpu.make_async_copy(x_hbm, x_ref, sems.at[chunks]),
        pltpu.make_async_copy(octant, oct_s, sems.at[chunks + 1]),
        pltpu.make_async_copy(parent, par_s, sems.at[chunks + 2]),
    ]
    big = [
        pltpu.make_async_copy(
            lift_hbm.at[pl.ds(i * per, per)], lift.at[pl.ds(i * per, per)], sems.at[i]
        )
        for i in range(chunks)
    ]
    for copy in big + small:
        copy.start()
    start, finish = fill_dense(
        dense, inter, trans, table_hbm, inter_s, trans_s, table, more, parents, all_parents
    )
    pl.when(odd_box())(start)
    for copy in small:
        copy.wait()
    own = [
        jnp.concatenate([x_ref[n, 0].astype(F32), x_ref[n, 1].astype(F32)], axis=0)
        for n in range(boxes)
    ]
    lane = lax.rem(lax.broadcasted_iota(jnp.int32, (boxes, LANES), 1), boxes)
    codes = jnp.zeros((boxes, LANES), F32)
    for n in range(boxes):
        slot = (oct_s[n] * parents + lax.rem(par_s[n], parents)).astype(F32)
        codes = jnp.where(lane == n, slot, codes)
    codes = codes[:CODE_ROWS].astype(BF16)
    x_rows[...] = jnp.concatenate(own, axis=0).astype(BF16)
    first = jnp.concatenate(own[:reach], axis=0)
    last = jnp.concatenate(own[reach:], axis=0)
    odd = lax.rem(lax.axis_index("samp"), 2) == 1
    at = parts * boxes
    to_beside[at + CODE_ROWS :] = jnp.where(odd, first, last).astype(BF16)
    to_far[at + CODE_ROWS :] = jnp.where(odd, last, first).astype(BF16)
    for ref in (plain, to_beside, to_far):
        ref[at : at + CODE_ROWS] = codes
    for n in range(0, boxes, 2):
        if n % per == 0:
            big[n // per].wait()
        y0, y1 = pair_dot(widen(own[n]), widen(own[n + 1]), abreast(lift[n]), abreast(lift[n + 1]))
        rows[pl.ds(n, parts, stride=boxes), :] = y0
        rows[pl.ds(n + 1, parts, stride=boxes), :] = y1
    pattern = rows[...].astype(BF16)
    for ref in (plain, to_beside, to_far):
        ref[:at] = pattern
    pl.when(odd_box())(finish)


def up_kernel(*refs, pieces, boxes, parents, parts):
    msgs = refs[:pieces]
    interp_ref, phase_ref, after, out_ref, out_copy, place_ref, raised, folded = refs[pieces:]
    forward = msgs[1]
    slots = 8 * parents
    samples = raised.shape[1]
    first = lax.axis_index("samp") * samples
    mine = interp_ref[pl.ds(pl.multiple_of(first, samples), samples)]
    per_tile = LANES // boxes
    at = parts * boxes
    tiles = []
    for t in range(0, pieces, per_tile):
        lane = lax.broadcasted_iota(jnp.int32, (CODE_ROWS, LANES), 1) // boxes
        code = msgs[t][at : at + CODE_ROWS].astype(F32)
        for d in range(1, min(per_tile, pieces - t)):
            code = jnp.where(lane == d, msgs[t + d][at : at + CODE_ROWS].astype(F32), code)
        code = jnp.concatenate([code] * (slots // CODE_ROWS), axis=0)
        want = lax.broadcasted_iota(jnp.int32, (slots, LANES), 0).astype(F32)
        width = min(per_tile, pieces - t) * boxes
        tiles.append(jnp.where(code == want, 1.0, 0.0)[:, :width])
    sorter = jnp.concatenate(tiles, axis=1)
    place_ref[...] = sorter.T.astype(BF16)
    sorter = sorter.astype(BF16)
    pats = jnp.concatenate(
        [
            jnp.concatenate([m[c * boxes : (c + 1) * boxes] for m in msgs], axis=0)
            for c in range(parts)
        ],
        axis=1,
    )
    ordered = nn_dot(sorter, pats).astype(BF16)
    stacked = jnp.concatenate(
        [ordered[:, c * LANES : (c + 1) * LANES] for c in range(parts)], axis=0
    )
    raised[...] = nt_dot(stacked, mine)
    half = parts // 2
    for t in range(samples // LANES):
        lanes = slice(t * LANES, (t + 1) * LANES)
        here = pl.ds(pl.multiple_of(first + t * LANES, LANES), LANES)
        for r in range(half):
            re = im = None
            for o in range(8):
                ph_r = phase_ref[o, 0:1, here]
                ph_i = phase_ref[o, 1:2, here]
                base_r = r * slots + o * parents
                base_i = (half + r) * slots + o * parents
                xr = raised[base_r : base_r + parents, lanes]
                xi = raised[base_i : base_i + parents, lanes]
                dr = ph_r * xr - ph_i * xi
                di = ph_r * xi + ph_i * xr
                re = dr if re is None else re + dr
                im = di if im is None else im + di
            folded[t, r * parents : (r + 1) * parents] = re
            folded[t, (half + r) * parents : (half + r + 1) * parents] = im
        for p in range(0, parents, 2):
            both = jnp.concatenate(
                [folded[t, pl.ds(p + e, parts, stride=parents), :] for e in range(2)], axis=0
            )
            both = both.astype(BF16)
            for ref in (out_ref, out_copy):
                ref[p * parts : (p + 2) * parts, lanes] = both
        extra = out_ref.shape[0] - parents * parts
        start = forward.shape[0] - extra * (samples // LANES - t)
        for ref in (out_ref, out_copy):
            ref[parents * parts :, lanes] = forward[start : start + extra]


def zone(parents):
    return [d for d in range(-parents, parents + 1) if abs(d) >= 2]


def fill_dense(dense, inter_hbm, trans_hbm, table_hbm, inter, trans, table, sems, parents, all_parents):
    copies = [
        pltpu.make_async_copy(inter_hbm, inter, sems.at[0]),
        pltpu.make_async_copy(trans_hbm, trans, sems.at[1]),
        pltpu.make_async_copy(table_hbm, table, sems.at[2]),
    ]
    first = lax.axis_index("box") * parents

    def start():
        for copy in copies:
            copy.start()

    def finish():
        for copy in copies:
            copy.wait()
        if len(zone(parents)) > inter.shape[1]:
            dense[...] = jnp.zeros_like(dense)

        def fill(p, carry):
            for k in range(inter.shape[1]):
                rel = lax.rem(inter[p, k] - first - p + parents + all_parents, all_parents)
                at = jnp.where(rel < parents, rel, rel - 3)
                dense[p, at] = table[trans[p, k]]
            return carry

        lax.fori_loop(0, parents, fill, 0)

    return start, finish


def odd_box():
    return lax.rem(lax.axis_index("box"), 2) == 1


def prep_kernel(
    inter, trans, neighbours, table_hbm, mats_hbm, dense_in, after, dense, nbr,
    inter_s, trans_s, table, sems, *, parents, all_parents,
):
    copy = pltpu.make_async_copy(neighbours, nbr, sems.at[3])
    copy.start()
    start, finish = fill_dense(
        dense, inter, trans, table_hbm, inter_s, trans_s, table, sems, parents, all_parents
    )

    @pl.when(jnp.logical_not(odd_box()))
    def _():
        start()
        finish()

    copy.wait()


def down_kernel(
    own, across, beside, dense, interp_ref, phase_ref, place_ref, after, *refs, pieces, boxes, parents, parts
):
    outs = refs[:pieces]
    window, incoming, shifted = refs[pieces:]
    samples = window.shape[2]
    first = lax.axis_index("samp") * samples
    mine = interp_ref[pl.ds(pl.multiple_of(first, samples), samples)]
    slots = 8 * parents
    half = parts // 2
    odd = lax.rem(lax.axis_index("box"), 2)
    rows = parents * parts
    window[parents : 2 * parents] = own[:rows].astype(F32).reshape(parents, parts, samples)
    window[pl.ds(2 * parents * odd, parents)] = (
        across[:rows].astype(F32).reshape(parents, parts, samples)
    )
    window[pl.ds(2 * parents * (1 - odd), parents)] = (
        beside[:rows].astype(F32).reshape(parents, parts, samples)
    )
    offsets = zone(parents)

    def one(p, t, source):
        lanes = slice(t * LANES, (t + 1) * LANES)
        acc_r = acc_i = None
        for i, d in enumerate(offsets):
            x = source(p + d)
            yr = dense[p, i, 0:1, lanes] * x
            yi = dense[p, i, 1:2, lanes] * x
            acc_r = yr if acc_r is None else acc_r + yr
            acc_i = yi if acc_i is None else acc_i + yi
        got = (acc_r + times_i(acc_i)).astype(BF16).astype(F32)
        incoming[t, pl.ds(p * parts, parts), :] = got

    for t in range(samples // LANES):
        lanes = slice(t * LANES, (t + 1) * LANES)
        if parents <= 8:
            held = [window[j, :, lanes] for j in range(3 * parents)]
            for p in range(parents):
                one(p, t, lambda j: held[parents + j])
        else:
            lax.fori_loop(
                0,
                parents,
                lambda p, c: (one(p, t, lambda j: window[parents + j, :, lanes]), c)[1],
                0,
            )
    for t in range(samples // LANES):
        lanes = slice(t * LANES, (t + 1) * LANES)
        here = pl.ds(pl.multiple_of(first + t * LANES, LANES), LANES)
        for r in range(half):
            ir = incoming[t, pl.ds(r, parents, stride=parts), :]
            ii = incoming[t, pl.ds(half + r, parents, stride=parts), :]
            re, im = [], []
            for o in range(8):
                ph_r = phase_ref[o, 0:1, here]
                ph_i = phase_ref[o, 1:2, here]
                re.append(ph_r * ir - ph_i * ii)
                im.append(ph_r * ii + ph_i * ir)
            shifted[r * slots : (r + 1) * slots, lanes] = jnp.concatenate(re, axis=0).astype(BF16)
            shifted[(half + r) * slots : (half + r + 1) * slots, lanes] = jnp.concatenate(
                im, axis=0
            ).astype(BF16)
    field = nn_dot(shifted[...], mine).astype(BF16)
    spread = jnp.concatenate([field[c * slots : (c + 1) * slots] for c in range(parts)], axis=1)
    leaves = nn_dot(place_ref[...], spread).astype(BF16)
    for d in range(pieces):
        for c in range(parts):
            outs[d][c * boxes : (c + 1) * boxes] = leaves[
                d * boxes : (d + 1) * boxes, c * LANES : (c + 1) * LANES
            ]


def near_kernel(*refs, late, nsamp, total, halo_rows, parent_rows):
    neighbours, own, mats, after, *halos, out_ref, window, nbr, sems = refs
    if late:
        across, beside, *from_far = halos
    else:
        (from_beside,) = halos
    list_copy = pltpu.make_async_copy(neighbours, nbr, sems.at[0])
    list_copy.start()
    count, parts, unknowns = out_ref.shape
    boxes = own.shape[0] // parts
    near_count = mats.shape[1]
    samp = lax.axis_index("samp")
    box = lax.axis_index("box")
    odd = lax.rem(samp, 2)
    first = count * (odd if late else 1 - odd)

    def piece(ref):
        return ref[ref.shape[0] - halo_rows :].astype(F32)

    if late:
        def forwarded(ref):
            return jnp.concatenate(
                [
                    ref[parent_rows:, t * LANES : (t + 1) * LANES].astype(F32)
                    for t in range(ref.shape[1] // LANES)
                ],
                axis=0,
            )

        partner = samp ^ (samp - 1 + 2 * odd)
        halo = piece(from_far[0])
        for i in range(1, len(from_far)):
            halo = jnp.where(partner == (4 << i) - 1, piece(from_far[i]), halo)
        box_odd = lax.rem(box, 2) == 1
        from_left = samp == 0
        passed = jnp.where(box_odd == from_left, forwarded(beside), forwarded(across))
        halo = jnp.where(jnp.logical_or(from_left, samp == nsamp - 1), passed, halo)
    else:
        halo = piece(from_beside)
    at = jnp.where(first > 0, boxes + count, 0)
    for i in range(count):
        window[at + i] = widen(halo[i * parts : (i + 1) * parts])
    mine = own[...].astype(F32)
    for i in range(boxes):
        window[count + i] = widen(mine[i * parts : (i + 1) * parts])
    list_copy.wait()
    base = (box * nsamp + samp) * boxes
    for i in range(count):
        acc = None
        for k in range(0, near_count, 2):
            j0, j1 = (
                lax.rem(nbr[k + e, first + i] - base + count + total, total) for e in range(2)
            )
            y0, y1 = pair_dot(
                window[j0], window[j1], abreast(mats[first + i, k]), abreast(mats[first + i, k + 1])
            )
            y = y0 + y1
            acc = y if acc is None else acc + y
        out_ref[i] = acc


def final_kernel(*refs, pieces):
    parts_in = refs[:pieces]
    near_early, near_late, mats, out_ref, field = refs[pieces:]
    boxes, halves, rhs = out_ref.shape[:3]
    parts = halves * rhs
    half = boxes // 2
    odd = lax.rem(lax.axis_index("samp"), 2) == 1
    total = parts_in[0][...].astype(F32)
    for m in parts_in[1:]:
        total += m[...].astype(F32)
    field[...] = total.astype(BF16).astype(F32)
    for n in range(0, boxes, 2):
        wide = [field[pl.ds(n + e, parts, stride=boxes), :] for e in range(2)]
        wide = [widen(v) for v in wide]
        for e, y in enumerate(pair_dot(*wide, abreast(mats[n]), abreast(mats[n + 1]))):
            i = (n + e) % half
            y = y + jnp.where(odd == (n < half), near_early[i], near_late[i])
            out_ref[n + e, 0] = y[:rhs]
            out_ref[n + e, 1] = y[rhs:]


def whole_in(kind):
    return pl.BlockSpec(memory_space=kind)


VM = pltpu.VMEM
SM = pltpu.SMEM
HBM = pltpu.HBM
DMA = pltpu.SemaphoreType.DMA
PARAMS = pltpu.CompilerParams(vmem_limit_bytes=24 * 1024 * 1024)


def stay(x):
    return pltpu.with_memory_space_constraint(x, HBM)


def on_device(
    xvec,
    near_blocks,
    neighbours,
    lift,
    place,
    interp,
    phases,
    octant,
    leaf_parent_index,
    translators,
    inter_list,
    trans_id,
):
    boxes, halves, rhs, unknowns = xvec.shape
    parts = halves * rhs
    nsamp = lax.axis_size("samp")
    nbox = lax.axis_size("box")
    total = boxes * nsamp * nbox
    reach = boxes // 2
    parents = boxes * nsamp // 8
    all_parents = parents * nbox
    samples = interp.shape[0] // nsamp
    slots = 8 * parents
    leaves = boxes * nsamp
    near_count = near_blocks.shape[1]
    halo_rows = reach * parts
    parent_rows = parents * parts
    plain_rows = parts * boxes + CODE_ROWS

    def shape(dims, dtype=BF16):
        return jax.ShapeDtypeStruct(dims, dtype)

    lift_chunks = 2
    to_far, plain, to_beside, x_rows, dense = pl.pallas_call(
        lambda *refs: leaf_kernel(*refs, parents=parents, all_parents=all_parents),
        in_specs=[whole_in(HBM)] * 7,
        out_specs=[whole_in(VM)] * 5,
        out_shape=[
            shape((plain_rows + halo_rows, LANES)),
            shape((plain_rows, LANES)),
            shape((plain_rows + halo_rows, LANES)),
            shape((boxes * parts, LANES)),
            shape((parents, len(zone(parents)), 2, samples), F32),
        ],
        scratch_shapes=[
            VM(xvec.shape, BF16),
            VM((parts * boxes, LANES), F32),
            VM(lift.shape, BF16),
            SM((boxes,), jnp.int32),
            SM((boxes,), jnp.int32),
            DMA((lift_chunks + 3,)),
            SM(inter_list.shape, jnp.int32),
            SM(trans_id.shape, jnp.int32),
            VM(translators.shape, F32),
            DMA((3,)),
        ],
        compiler_params=PARAMS,
        name="leaf",
    )(
        *[stay(a) for a in (octant, leaf_parent_index, xvec, lift)],
        *[stay(a) for a in (inter_list, trans_id, translators)],
    )

    def exchange(x, d):
        return lax.ppermute(x, "samp", [(i, i ^ d) for i in range(nsamp)])

    order = [0, nsamp - 1, *range(1, nsamp - 1)]
    far = [(4 << i) - 1 for i in range(nsamp.bit_length() - 2)]
    messages = {0: plain}
    for d in order[1:]:
        messages[d] = exchange(to_beside if d == 1 else to_far if d in far else plain, d)
    far_messages = [messages[d] for d in far]

    dense, near_list = pl.pallas_call(
        lambda *refs: prep_kernel(*refs, parents=parents, all_parents=all_parents),
        in_specs=[whole_in(HBM)] * 5 + [whole_in(VM)] * 2,
        out_specs=[whole_in(VM)] * 2,
        input_output_aliases={5: 0},
        out_shape=[
            shape((parents, len(zone(parents)), 2, samples), F32),
            shape((near_count, boxes), jnp.int32),
        ],
        scratch_shapes=[
            SM(inter_list.shape, jnp.int32),
            SM(trans_id.shape, jnp.int32),
            VM(translators.shape, F32),
            DMA((4,)),
        ],
        compiler_params=PARAMS,
        cost_estimate=pl.CostEstimate(
            flops=0, bytes_accessed=2 * near_blocks.size, transcendentals=0
        ),
        name="prep",
    )(
        stay(inter_list),
        stay(trans_id),
        stay(neighbours.T),
        stay(translators),
        stay(near_blocks),
        dense,
        x_rows,
    )

    to_across, parent_pat, place_onehot = pl.pallas_call(
        lambda *refs: up_kernel(
            *refs, pieces=nsamp, boxes=boxes, parents=parents, parts=parts
        ),
        in_specs=[whole_in(VM)] * (nsamp + 3),
        out_specs=[whole_in(VM)] * 3,
        out_shape=[
            shape((parent_rows + halo_rows * LANES // samples, samples)),
            shape((parent_rows + halo_rows * LANES // samples, samples)),
            shape((leaves, slots)),
        ],
        scratch_shapes=[
            VM((parts * slots, samples), F32),
            VM((samples // LANES, parent_rows, LANES), F32),
        ],
        compiler_params=PARAMS,
        name="up",
    )(*[messages[d] for d in order], interp, phases, near_list)

    across = lax.ppermute(
        to_across, "box", [(i, (i + (1 if i % 2 else -1)) % nbox) for i in range(nbox)]
    )
    beside = lax.ppermute(parent_pat, "box", [(i, i ^ 1) for i in range(nbox)])

    def near_half(late, args):
        return pl.pallas_call(
            lambda *refs: near_kernel(
                *refs,
                late=late,
                nsamp=nsamp,
                total=total,
                halo_rows=halo_rows,
                parent_rows=parent_rows,
            ),
            in_specs=[whole_in(VM)] * (3 + len(args)),
            out_specs=whole_in(VM),
            out_shape=shape((reach, parts, unknowns), F32),
            scratch_shapes=[
                VM((boxes + 2 * reach, parts, 2 * unknowns), F32),
                SM((near_count, boxes), jnp.int32),
                DMA((1,)),
            ],
            compiler_params=PARAMS,
            cost_estimate=pl.CostEstimate(
                flops=parts * near_blocks.size,
                bytes_accessed=near_blocks.size,
                transcendentals=0,
            ),
            name="near",
        )(near_list, x_rows, near_blocks, *args)

    near_early = near_half(False, [place_onehot, messages[1]])

    fields = pl.pallas_call(
        lambda *refs: down_kernel(
            *refs, pieces=nsamp, boxes=boxes, parents=parents, parts=parts
        ),
        in_specs=[whole_in(VM)] * 8,
        out_specs=[whole_in(VM)] * nsamp,
        out_shape=[shape((parts * boxes, LANES))] * nsamp,
        scratch_shapes=[
            VM((3 * parents, parts, samples), F32),
            VM((samples // LANES, parent_rows, LANES), F32),
            VM((parts * slots, samples), BF16),
        ],
        compiler_params=PARAMS,
        name="down",
    )(parent_pat, across, beside, dense, interp, phases, place_onehot, near_early)

    pieces = dict(zip(order, fields))
    partial = [pieces[0]] + [exchange(pieces[d], d) for d in reversed(range(1, nsamp))]

    near_late = near_half(True, [fields[0], across, beside, *far_messages])

    return pl.pallas_call(
        lambda *refs: final_kernel(*refs, pieces=nsamp),
        in_specs=[whole_in(VM)] * (nsamp + 3),
        out_specs=whole_in(VM),
        out_shape=shape(xvec.shape, F32),
        scratch_shapes=[VM((parts * boxes, LANES), F32)],
        compiler_params=PARAMS,
        name="final",
    )(*partial, near_early, near_late, place)


def solution(mesh):
    in_specs = (
        P(("box", "samp"), None, None, None),
        P(("box", "samp"), None, None, None, None),
        P(("box", "samp"), None),
        P(("box", "samp"), None, None, None),
        P(("box", "samp"), None, None, None),
        P(),
        P(),
        P(("box", "samp")),
        P(("box", "samp")),
        P(None, None, "samp"),
        P("box", None),
        P("box", None),
    )
    out_specs = P(("box", "samp"), None, None, None)
    return jax.shard_map(
        on_device, mesh=mesh, in_specs=in_specs, out_specs=out_specs, check_vma=False
    )
```
